128 devices in a mesh: dp: 64 (over x, y, z), tensor: 2 (over core).
Axes of the slice: x: 4, y: 4, z: 4, core: 2. Of those that a mesh axis runs over, the one named last changes fastest.
Arguments:
- tokens: bfloat16 [16384, 768], P(('dp', 'tensor')), may hold values from -6 to 6
- gain_attn: float32 [768], replicated, may hold values from 0.5 to 1.5
- rel_table: float32 [32, 12], replicated, may hold values from -5 to 5
- w_qkv: bfloat16 [768, 3, 768], P('dp', None, 'tensor'), may hold values from -0.078125 to 0.078125
- w_o: bfloat16 [768, 768], P(('tensor', 'dp')), may hold values from -5 to 5
- gain_moe: float32 [768], replicated, may hold values from 0.5 to 1.5
- router: float32 [768, 64], replicated, may hold values from -0.15625 to 0.15625
- w_in: bfloat16 [64, 768, 3072], P('dp', None, 'tensor'), may hold values from -0.21875 to 0.21875
- w_out: bfloat16 [64, 3072, 768], P('dp', 'tensor'), may hold values from -5 to 5
- segments: int32 [64, 256], P('dp'), may hold values from 0 to 2, never falling along the last dimension, each value on 1 to 192 neighbouring positions
- offset_buckets: int32 [511], replicated, may hold values from 0 to 31
- expert_ids: int32 [16384, 1], P(('dp', 'tensor')), may hold values from 0 to 63; in each aligned block of 128 rows (0 to 127, 128 to 255, ...) at most 2 rows name the same one
- out_grad: bfloat16 [16384, 768], P(('dp', 'tensor')), may hold values from -6 to 6
Outputs:
- activations: bfloat16 [16384, 768], P(('dp', 'tensor'))
- input_grad: bfloat16 [16384, 768], P(('dp', 'tensor'))
- grad_gain_attn: float32 [768], replicated
- grad_rel_table: float32 [32, 12], replicated
- grad_w_qkv: float32 [768, 3, 768], P('dp', None, 'tensor')
- grad_w_o: float32 [768, 768], P(('tensor', 'dp'))
- grad_gain_moe: float32 [768], replicated
- grad_router: float32 [768, 64], replicated
- grad_w_in: float32 [64, 768, 3072], P('dp', None, 'tensor')
- grad_w_out: float32 [64, 3072, 768], P('dp', 'tensor')
The draws below stay inside these ranges and needn't reach their ends.
Inputs may be any that keep to these rules, and one draw needn't show every extreme that they name: `segments`: along each row segment numbers never fall, and one segment of each row holds exactly 192 positions. `expert_ids`: among the 128 rows of one device no expert is named more than 2 times, and in every draw some device names some expert exactly 2 times.
All inputs are finite; a program needn't handle non-finite values.
Results may differ from the reference program's by a relative error of at most 0.022.
Values may be sent and summed in bfloat16 or wider, within the bound.
No kernel may reach another device: no remote copies, remote signals or barrier semaphores. Data moves between devices by JAX's collectives and lax.ppermute only.
A program may use at most 128 MiB of HBM per device.

```python
import math
import jax
import jax.numpy as jnp
import numpy as np
from jax import lax

D = 768
HEADS = 12
HEAD = 64
FF = 3072
BUCKETS = 32
TOK_DEV = 128
EXPERTS = 64
SEQ = 256
SEQS = 64
TOKENS = 16384
CAP = 2
N_DP = 64
N_TENSOR = 2


def touch_ends(array, rng, smallest, high):
    longest = array.shape.index(max(array.shape))
    spots = []
    for shift in (0, 1):
        where = [jax.random.randint(jax.random.fold_in(rng, axis), (), 0, length) for axis, length in enumerate(array.shape)]
        where[longest] = (where[longest] + shift) % array.shape[longest]
        spots.append(tuple(where))
    return array.at[spots[0]].set(smallest).at[spots[1]].set(high)


def levels(rng, dims, shards, smallest, top_value):
    level = 1.0
    for axis_at, parts in shards:
        heights = jax.random.uniform(jax.random.fold_in(jax.random.fold_in(rng, 6), axis_at), (parts,), jnp.float32, smallest / len(shards), top_value / len(shards))
        level = level * jnp.repeat(jnp.exp(heights), dims[axis_at] // parts).reshape((-1,) + (1,) * (len(dims) - 1 - axis_at))
    return level


def profile(number_of, total, reach, lean):
    portions = [(1 << 20) // math.isqrt(grade ** lean) + 1 for grade in range(2, number_of + 1)]
    spare, counts = total - reach - (number_of - 1), [1] * (number_of - 1)
    while spare > 0:
        free = [i for i in range(number_of - 1) if counts[i] < reach]
        mass, budget = sum([portions[i] for i in free]), spare
        for i in free:
            more = min(reach - counts[i], max(1, budget * portions[i] // mass), spare)
            counts[i] = counts[i] + more
            spare = spare - more
    return np.array([reach] + counts)


def ragged(key, amount, total, limit, slope):
    if amount == 2:
        one = jax.random.randint(key, (), max(1, total - limit), min(limit, total - 1) + 1)
        return jnp.stack([one, total - one])
    tallies = jnp.asarray(profile(amount, total, limit, slope), jnp.int32)
    twos = (amount - 1) // 2
    source_of, taker = tallies[1:1 + 2 * twos:2], tallies[2:2 + 2 * twos:2]
    room = jnp.minimum(source_of - 1, limit - taker)
    passed = jax.random.randint(jax.random.fold_in(key, 1), (twos,), 0, 1 << 20) % (room + 1)
    tallies = tallies.at[1:1 + 2 * twos:2].set(source_of - passed).at[2:2 + 2 * twos:2].set(taker + passed)
    return tallies[jax.random.permutation(jax.random.fold_in(key, 2), amount)]


def shared_out(own_key, own, number, rows, number_of, top, most, slope):
    sequence = jax.random.permutation(own_key, number_of)
    crowded, common = portions_of(number_of, rows * top, most, slope, True), portions_of(number_of, rows * top, most, slope, False)
    places = jnp.arange(number_of)

    def named(tallies, turn):
        used = int((tallies > 0).sum())
        fixed = max(1, used // 4)
        moved = fixed + (places - fixed + turn * (used - fixed)) % max(1, number_of - fixed)
        return jnp.zeros((number_of,), jnp.int32).at[sequence[jnp.where(places < fixed, places, moved)]].set(jnp.asarray(tallies, jnp.int32))

    tallies = jnp.where(number % 4 == 0, named(crowded, number // 4), named(common, number - number // 4 - 1))
    mixed = jax.random.permutation(jax.random.fold_in(own, 3), number_of)
    donor, receiver = mixed[0:number_of // 2 * 2:2], mixed[1:number_of // 2 * 2:2]
    margin = jnp.minimum(tallies[donor] - 1, most - tallies[receiver]) // 2
    margin = jnp.where((donor == sequence[0]) | (receiver == sequence[0]) | (tallies[receiver] == 0), 0, jnp.maximum(margin, 0))
    moved = jax.random.randint(jax.random.fold_in(own, 4), (number_of // 2,), 0, 1 << 20) % (margin + 1)
    tallies = tallies.at[donor].add(-moved).at[receiver].add(moved)
    members = jnp.searchsorted(jnp.cumsum(tallies), jnp.arange(rows * top), side="right").astype(jnp.int32)
    grid = members.reshape(top, rows).T
    grid = grid[jax.random.permutation(jax.random.fold_in(own, 1), rows)]
    turn = jax.random.randint(jax.random.fold_in(own, 2), (rows, 1), 0, top)
    return jnp.take_along_axis(grid, (jnp.arange(top)[None, :] + turn) % top, axis=1)


def portions_of(amount, total, reach, slope, full):
    weights = [(1 << 20) // math.isqrt(rank ** slope) + 1 for rank in range(1, amount + 1)]
    largest = reach if full else min(reach, max(-(-total // amount), total * weights[0] // sum(weights)))
    least = 1 if total - largest >= amount - 1 else 0
    given, spare = [largest] + [least] * (amount - 1), total - largest - least * (amount - 1)
    while spare > 0:
        movable = [i for i in range(1, amount) if given[i] < largest] or [i for i in range(1, amount) if given[i] < reach]
        mass, budget = sum([weights[i] for i in movable]), spare
        for i in movable:
            addition = min(reach - given[i], max(1, budget * weights[i] // mass), spare)
            given[i] = given[i] + addition
            spare = spare - addition
    return np.array(given)


def scatter_about(rng, dims, spread, reach, pieces=(), kind=jnp.bfloat16):
    values = spread * jax.random.normal(rng, dims, jnp.float32)
    if pieces:
        values = values * levels(rng, dims, pieces, -0.22, 0.18)
    return jnp.clip(values, -reach, reach).astype(kind)


def setup_inputs(seed: int = 0) -> dict:
    streams_of = jax.random.split(jax.random.key(seed), 14)
    tokens = scatter_about(streams_of[0], (TOKENS, D), 1.0, 6.0, ((0, 128),))
    gain_attn = jnp.clip(1.0 + 0.1 * jax.random.normal(streams_of[1], (D,), jnp.float32), 0.5, 1.5)
    rel_table = scatter_about(streams_of[2], (BUCKETS, HEADS), 1.0, 5.0, (), jnp.float32)
    w_qkv = scatter_about(streams_of[3], (D, 3, D), (8 * D) ** -0.5, 0.078125, ((0, 64), (2, 2)))
    w_o = scatter_about(streams_of[4], (D, D), 1.0, 5.0, ((0, 128),))
    gain_moe = jnp.clip(1.0 + 0.1 * jax.random.normal(streams_of[5], (D,), jnp.float32), 0.5, 1.5)
    router = scatter_about(streams_of[6], (D, EXPERTS), (2 * D) ** -0.5, 0.15625, (), jnp.float32)
    w_in = scatter_about(streams_of[7], (EXPERTS, D, FF), D ** -0.5, 0.21875, ((0, 64), (2, 2)))
    w_out = scatter_about(streams_of[8], (EXPERTS, FF, D), 1.8, 5.0, ((0, 64), (1, 2)))
    segments = jax.vmap(lambda own: jnp.searchsorted(jnp.cumsum(ragged(own, 3, SEQ, 3 * SEQ // 4, 0)), jnp.arange(SEQ), side="right"))(jax.random.split(streams_of[9], SEQS)).reshape((SEQS, SEQ)).astype(jnp.int32)
    offset_buckets = touch_ends(jax.random.randint(streams_of[10], (2 * SEQ - 1,), 0, BUCKETS), jax.random.fold_in(streams_of[10], 1), 0, BUCKETS - 1).astype(jnp.int32)
    expert_ids_keys = jax.random.split(jax.random.fold_in(streams_of[11], 1), TOKENS // TOK_DEV)
    expert_ids_turns = jax.random.permutation(jax.random.fold_in(streams_of[11], 3), TOKENS // TOK_DEV)
    expert_ids = jax.vmap(lambda own, number: shared_out(jax.random.fold_in(streams_of[11], 2), own, number, TOK_DEV, EXPERTS, 1, CAP, 2))(expert_ids_keys, expert_ids_turns).reshape((TOKENS, 1))
    out_grad = scatter_about(streams_of[12], (TOKENS, D), 1.0, 6.0, ((0, 128),))
    return dict(tokens=tokens, gain_attn=gain_attn, rel_table=rel_table, w_qkv=w_qkv, w_o=w_o, gain_moe=gain_moe, router=router, w_in=w_in, w_out=w_out, segments=segments, offset_buckets=offset_buckets, expert_ids=expert_ids, out_grad=out_grad)


@jax.custom_vjp
def low(v):
    return lax.optimization_barrier(v.astype(jnp.bfloat16)).astype(jnp.float32)

@jax.custom_vjp
def low_back(v):
    return v

def low_keep(v):
    return (low(v), None)

def low_pass(kept, grad):
    return (grad,)

def back_keep(v):
    return (v, None)

def back_low(kept, grad):
    return (low(grad),)
low.defvjp(low_keep, low_pass)
low_back.defvjp(back_keep, back_low)
PRECISE = lax.Precision.HIGHEST
EPSILON = 1e-06
MASKED = -1000000000.0

def matmul_high(left, right):
    return jnp.dot(left, right, precision=PRECISE)

def rms_norm(inputs, gain_vec):
    row_scale = lax.rsqrt(lax.optimization_barrier(jnp.mean(inputs * inputs, axis=-1, keepdims=True)) + EPSILON)
    return inputs * row_scale * gain_vec

def attend_one(qkv_seq, seg_row, pair_bias):
    query_rows = qkv_seq[:, 0]
    key_rows = qkv_seq[:, 1]
    values = qkv_seq[:, 2]
    scores = jnp.einsum('ihd,jhd->hij', query_rows, key_rows, precision=PRECISE) + pair_bias
    scores = low_back(scores)
    same_doc = seg_row[:, None] == seg_row[None, :]
    scores = jnp.where(same_doc[None], scores, MASKED)
    attn_probs = low(jax.nn.softmax(scores, axis=-1))
    context = jnp.einsum('hij,jhd->ihd', attn_probs, values, precision=PRECISE)
    return context.reshape(SEQ, D)

def expert_one(packed):
    slot_rows, w_first, w_second = packed
    pre_act = low_back(matmul_high(slot_rows, w_first))
    hidden = low(jax.nn.gelu(pre_act, approximate=False))
    return matmul_high(hidden, w_second)

def forward(tokens, gain_attn, rel_table, w_qkv, w_o, gain_moe, router, w_in, w_out, segments, offset_buckets, expert_ids):
    first_rows = low(rms_norm(tokens, gain_attn))
    qkv_rows = matmul_high(first_rows, w_qkv.reshape(D, 3 * D))
    qkv_rows = low(low_back(qkv_rows)).reshape(SEQS, SEQ, 3, HEADS, HEAD)
    table_rows = (offset_buckets[:, None] == jnp.arange(BUCKETS, dtype=jnp.int32)[None, :]).astype(jnp.float32)
    offset_bias = matmul_high(table_rows, rel_table)
    places = jnp.arange(SEQ, dtype=jnp.int32)
    pair_index = places[None, :] - places[:, None] + SEQ - 1
    pair_bias = jnp.transpose(offset_bias[pair_index], (2, 0, 1))
    context = lax.map(jax.checkpoint(lambda packed: attend_one(packed[0], packed[1], pair_bias)), (qkv_rows, segments))
    context = low(low_back(context.reshape(TOKENS, D)))
    attn_out = low_back(matmul_high(context, w_o))
    mid_rows = tokens + attn_out
    second_rows = rms_norm(mid_rows, gain_moe)
    logits = matmul_high(second_rows, router)
    router_probs = jax.nn.softmax(logits, axis=-1)
    expert_index = expert_ids[:, 0]
    expert_hits = expert_index[:, None] == jnp.arange(EXPERTS, dtype=jnp.int32)[None, :]
    gate_value = lax.optimization_barrier(jnp.sum(router_probs * expert_hits.astype(jnp.float32), axis=-1))
    second_low = low(second_rows)
    device_hits = expert_hits.astype(jnp.int32).reshape(N_DP * N_TENSOR, TOK_DEV, EXPERTS)
    slot_ranks = jnp.cumsum(device_hits, axis=1) - 1
    slot_index = lax.optimization_barrier(jnp.sum(slot_ranks * device_hits, axis=-1)).reshape(TOKENS)
    device = jnp.arange(TOKENS, dtype=jnp.int32) // TOK_DEV
    slot_place = device * CAP + slot_index
    buffers = jnp.zeros((EXPERTS, N_DP * N_TENSOR * CAP, D), jnp.float32).at[expert_index, slot_place].set(second_low)
    outputs = lax.map(jax.checkpoint(expert_one), (buffers, w_in, w_out))
    expert_out = low_back(outputs[expert_index, slot_place])
    return mid_rows + gate_value[:, None] * expert_out

def reference(tokens, gain_attn, rel_table, w_qkv, w_o, gain_moe, router, w_in, w_out, segments, offset_buckets, expert_ids, out_grad):
    floats = (tokens.astype(jnp.float32), gain_attn, rel_table, w_qkv.astype(jnp.float32), w_o.astype(jnp.float32), gain_moe, router, w_in.astype(jnp.float32), w_out.astype(jnp.float32))

    def closed(*values):
        return forward(*values, segments, offset_buckets, expert_ids)
    result, pullback = jax.vjp(closed, *floats)
    gradients = pullback(out_grad.astype(jnp.float32))
    return (result.astype(jnp.bfloat16), gradients[0].astype(jnp.bfloat16), gradients[1], gradients[2], gradients[3], gradients[4], gradients[5], gradients[6], gradients[7], gradients[8])
```

```python
import jax
import jax.numpy as jnp
from jax import lax
from jax.sharding import PartitionSpec as P

PRECISE = lax.Precision.HIGHEST
EPSILON = 1e-06
MASKED = -1000000000.0
BF = jnp.bfloat16
F32 = jnp.float32
ALL = ("dp", "tensor")


def swap(rows):
    return lax.ppermute(rows, "tensor", [(0, 1), (1, 0)])


def dot(left, right, dims=((1,), (0,)), precision=None):
    return lax.dot_general(left, right, (dims, ((), ())), precision=precision, preferred_element_type=F32)


def per_device(
    tokens, gain_attn, rel_table, w_qkv, w_o, gain_moe, router, w_in, w_out, segments, offset_buckets, expert_ids, out_grad
):
    rows, width = tokens.shape
    shard, _, cols = w_qkv.shape
    wo_rows = w_o.shape[0]
    buckets, heads_all = rel_table.shape
    head = width // heads_all
    heads = cols // head
    seq = segments.shape[1]
    n_dp = lax.axis_size("dp")
    n_t = lax.axis_size("tensor")
    experts = n_dp
    cap = rows // experts
    t = lax.axis_index("tensor")
    me = lax.axis_index("dp")

    expert_index = expert_ids[:, 0]
    hits = expert_index[:, None] == jnp.arange(experts, dtype=jnp.int32)[None, :]
    counts = jnp.cumsum(hits.astype(jnp.int32), axis=0)
    rank = jnp.sum((counts - 1) * hits.astype(jnp.int32), axis=-1)
    target = expert_index * cap + rank
    slot_hit = jnp.arange(rows, dtype=jnp.int32)[:, None] == target[None, :]
    slot_low = slot_hit.astype(BF)

    g_slots = dot(slot_low, out_grad).astype(BF)
    w_send = jnp.concatenate(
        [jnp.transpose(w_qkv, (1, 0, 2)).reshape(3 * shard, cols), w_o.reshape(wo_rows * 2, cols)], 0
    )
    w_rows = w_send.shape[0]
    send_one = jnp.concatenate(
        [jnp.broadcast_to(w_send[None], (n_dp, w_rows, cols)), g_slots.reshape(n_dp, cap * 2, cols)], 1
    )
    got_one = lax.all_to_all(send_one, "dp", 0, 0)

    xf = tokens.astype(F32)
    scale_one = lax.rsqrt(jnp.mean(xf * xf, axis=-1, keepdims=True) + EPSILON)
    hat_one = xf * scale_one
    first_rows = (hat_one * gain_attn).astype(BF)
    first_all = lax.all_gather(first_rows, "tensor", axis=0, tiled=True)

    w_q3 = [got_one[:, c * shard : (c + 1) * shard].reshape(width, cols) for c in range(3)]
    wo_full = got_one[:, 3 * shard : w_rows].reshape(cols, width)
    g_mine = got_one[:, w_rows:].reshape(rows, width)
    g_all = lax.all_gather(g_mine, "tensor", axis=0)

    q, k, v = [dot(first_all, w).astype(BF).reshape(seq, heads, head) for w in w_q3]

    table_local = lax.dynamic_slice_in_dim(rel_table, t * heads, heads, 1)
    bucket_hits = (offset_buckets[:, None] == jnp.arange(buckets, dtype=jnp.int32)[None, :]).astype(F32)
    offset_bias = jnp.einsum("bh,rb->hr", table_local, bucket_hits, precision=PRECISE)
    span = 2 * seq
    tiled = jnp.tile(jnp.pad(offset_bias, ((0, 0), (0, 1))), (1, seq))
    skewed = tiled[:, seq - 1 : seq - 1 + seq * (span - 1)]
    bias = skewed.reshape(heads, seq, span - 1)[:, :, :seq]
    seg = segments[0]
    same = seg[:, None] == seg[None, :]
    scores = jnp.einsum("ihd,jhd->hij", q, k, preferred_element_type=F32) + bias
    scores = jnp.where(same[None], scores, MASKED)
    top = jnp.max(scores, axis=-1, keepdims=True)
    shifted = jnp.exp(scores - top)
    probs = shifted / jnp.sum(shifted, axis=-1, keepdims=True)
    probs_low = probs.astype(BF)
    context = jnp.einsum("hij,jhd->ihd", probs_low, v, preferred_element_type=F32).reshape(seq, cols).astype(BF)
    part = dot(context, wo_full)
    keep = lax.dynamic_slice_in_dim(part, t * rows, rows, 0)
    give = lax.dynamic_slice_in_dim(part, (1 - t) * rows, rows, 0).astype(BF)
    mid = xf + (keep + swap(give).astype(F32))
    scale_two = lax.rsqrt(jnp.mean(mid * mid, axis=-1, keepdims=True) + EPSILON)
    second = mid * scale_two * gain_moe

    out_slots = dot(slot_low, second.astype(BF)).astype(BF)
    send_two = jnp.broadcast_to(out_slots.reshape(n_dp, 1, cap, width), (n_dp, n_t, cap, width))
    arrived = lax.all_to_all(send_two.reshape(n_dp * n_t, cap, width), ALL, 0, 0)
    arrived = arrived.reshape(n_dp * n_t * cap, width)
    g_rows = jnp.transpose(g_all.reshape(n_t, n_dp, cap, width), (1, 0, 2, 3)).reshape(n_dp * n_t * cap, width)

    logits_home = jnp.dot(second, router, precision=PRECISE)
    gate_home = jnp.sum(jax.nn.softmax(logits_home, axis=-1) * hits.astype(F32), axis=-1, keepdims=True)

    w1, w2 = w_in[0], w_out[0]
    pre = dot(arrived, w1)
    activated, gelu_back = jax.vjp(lambda u: jax.nn.gelu(u, approximate=False), pre)
    hidden = activated.astype(BF)
    out_part = dot(hidden, w2)
    logits = jnp.dot(arrived.astype(F32), router, precision=PRECISE)
    r_probs = jax.nn.softmax(logits, axis=-1)
    mine = (jnp.arange(experts, dtype=jnp.int32) == me).astype(F32)[None, :]
    gate = jnp.sum(r_probs * mine, axis=-1, keepdims=True)
    g_f = g_rows.astype(F32)
    grad_expert = (gate * g_f).astype(BF)
    grad_gate = jnp.sum(g_f * out_part, axis=-1, keepdims=True)
    grad_logits = grad_gate * gate * (mine - r_probs)
    grad_hidden = dot(grad_expert, w2, ((1,), (1,)))
    grad_pre = gelu_back(grad_hidden)[0].astype(BF)
    grad_disp = dot(grad_pre, w1, ((1,), (1,))) + dot(grad_logits, router, ((1,), (1,)), PRECISE)
    router_part = dot(grad_logits, arrived.astype(F32), ((0,), (0,)), PRECISE)

    both = jnp.concatenate(
        [out_part.astype(BF).reshape(n_dp * n_t, cap, width), grad_disp.astype(BF).reshape(n_dp * n_t, cap, width)], 1
    )
    r_send = jnp.pad(router_part.astype(BF).reshape(n_dp * n_t, 1, cols), ((0, 0), (0, 0), (0, width - cols)))
    got_three = lax.all_to_all(jnp.concatenate([both, r_send], 1), ALL, 0, 0)

    grad_w_out = dot(hidden, grad_expert, ((0,), (0,)))
    grad_w_in = dot(arrived, grad_pre, ((0,), (0,)))

    got_f = got_three.astype(F32)
    summed = jnp.sum(got_f.reshape(n_dp, n_t, 2 * cap + 1, width), axis=1)
    slot_out = summed[:, :cap].reshape(rows, width)
    slot_grad = summed[:, cap : 2 * cap].reshape(rows, width)
    router_piece = jnp.sum(summed[:, 2 * cap, :cols], axis=0)
    slot_f = slot_hit.astype(F32)
    expert_out = dot(slot_f, slot_out, ((0,), (0,)), PRECISE)
    grad_second = dot(slot_f, slot_grad, ((0,), (0,)), PRECISE)
    activations = (mid + gate_home * expert_out).astype(BF)
    u2 = grad_second * gain_moe
    gain_two = jnp.sum(grad_second * mid * scale_two, axis=0)
    spread = jnp.mean(u2 * mid, axis=-1, keepdims=True)
    grad_mid = out_grad.astype(F32) + (scale_two * u2 - scale_two * scale_two * scale_two * mid * spread)
    grad_attn = lax.all_gather(grad_mid.astype(BF), "tensor", axis=0, tiled=True)

    grad_w_o = dot(context, grad_attn, ((0,), (0,)))
    grad_context = dot(grad_attn, wo_full, ((1,), (1,))).astype(BF).reshape(seq, heads, head)
    grad_probs = jnp.einsum("ihd,jhd->hij", grad_context, v, preferred_element_type=F32)
    inner = jnp.sum(probs * grad_probs, axis=-1, keepdims=True)
    grad_scores = (probs * (grad_probs - inner)).astype(BF)
    grad_q = jnp.einsum("hij,jhd->ihd", grad_scores, k, preferred_element_type=F32)
    grad_k = jnp.einsum("hij,ihd->jhd", grad_scores, q, preferred_element_type=F32)
    grad_v = jnp.einsum("hij,ihd->jhd", probs_low, grad_context, preferred_element_type=F32)
    widened = jnp.pad(grad_scores.astype(F32), ((0, 0), (0, 0), (0, seq - 1)))
    flat = jnp.pad(widened.reshape(heads, seq * (span - 1)), ((0, 0), (seq - 1, 1)))
    diagonals = jnp.sum(flat.reshape(heads, seq, span), axis=1)
    grad_table = jnp.einsum("hr,rb->hb", diagonals[:, : span - 1], bucket_hits, precision=PRECISE)
    grad3 = [x.reshape(seq, cols).astype(BF) for x in (grad_q, grad_k, grad_v)]
    grad_w3 = [dot(first_all, x, ((0,), (0,))).astype(BF).reshape(n_dp, shard, cols) for x in grad3]

    grad_first = sum(dot(x, w, ((1,), (1,))) for x, w in zip(grad3, w_q3))
    keep_first = lax.dynamic_slice_in_dim(grad_first, t * rows, rows, 0)
    give_first = lax.dynamic_slice_in_dim(grad_first, (1 - t) * rows, rows, 0).astype(BF)

    hat_all = first_all.astype(F32) / gain_attn
    gain_one = jnp.sum(grad_first * hat_all, axis=0)

    tiny = jnp.concatenate(
        [router_piece, gain_one, gain_two, jnp.pad(grad_table.reshape(-1), (0, cols - heads * buckets))]
    ).astype(BF)
    send_four = jnp.concatenate(
        grad_w3
        + [
            grad_w_o.astype(BF).reshape(n_dp, wo_rows * 2, cols),
            jnp.broadcast_to(tiny.reshape(1, -1, cols), (n_dp, tiny.size // cols, cols)),
        ],
        1,
    )
    got_four = lax.all_to_all(send_four, "dp", 0, 0)

    grad_first_own = keep_first + swap(give_first).astype(F32)
    u1 = grad_first_own * gain_attn
    spread_one = jnp.mean(u1 * xf, axis=-1, keepdims=True)
    input_grad = (grad_mid + (scale_one * u1 - scale_one * scale_one * scale_one * xf * spread_one)).astype(BF)

    tiny_got = got_four[:, w_rows:].astype(F32)
    router_half = tiny_got[:, 0]
    sums = jnp.sum(tiny_got[:, 1:], axis=0).reshape(-1)
    packed = jnp.concatenate([router_half, sums.reshape(-1, cols)], 0)
    other = swap(packed)
    low, high = jnp.where(t == 0, packed, other), jnp.where(t == 0, other, packed)
    grad_router = jnp.concatenate([low[:n_dp], high[:n_dp]], 1).T
    total = (packed[n_dp:] + other[n_dp:]).reshape(-1)
    gain_one_sum, gain_two_sum = total[:width], total[width : 2 * width]
    tables = [x[-1, : heads * buckets].reshape(heads, buckets) for x in (low, high)]
    table_sum = jnp.concatenate(tables, 0).T
    weights = jnp.sum(got_four[:, :w_rows].astype(F32), axis=0)
    grad_qkv_shard = jnp.transpose(weights[: 3 * shard].reshape(3, shard, cols), (1, 0, 2))
    grad_o_shard = weights[3 * shard :].reshape(wo_rows, width)
    return (
        activations,
        input_grad,
        gain_one_sum,
        table_sum,
        grad_qkv_shard,
        grad_o_shard,
        gain_two_sum,
        grad_router,
        grad_w_in[None],
        grad_w_out[None],
    )


def solution(mesh):
    in_specs = (
        P(("dp", "tensor"), None),
        P(),
        P(),
        P("dp", None, "tensor"),
        P(("tensor", "dp"), None),
        P(),
        P(),
        P("dp", None, "tensor"),
        P("dp", "tensor", None),
        P("dp", None),
        P(),
        P(("dp", "tensor"), None),
        P(("dp", "tensor"), None),
    )
    out_specs = (
        P(("dp", "tensor"), None),
        P(("dp", "tensor"), None),
        P(),
        P(),
        P("dp", None, "tensor"),
        P(("tensor", "dp"), None),
        P(),
        P(),
        P("dp", None, "tensor"),
        P("dp", "tensor", None),
    )
    return jax.shard_map(per_device, mesh=mesh, in_specs=in_specs, out_specs=out_specs, check_vma=False)
```

```python
import jax
import jax.numpy as jnp
from jax import lax
from jax.experimental import pallas as pl
from jax.experimental.pallas import tpu as pltpu
from jax.sharding import PartitionSpec as P

PRECISE = lax.Precision.HIGHEST
EPSILON = 1e-06
MASKED = -1000000000.0
BF = jnp.bfloat16
F32 = jnp.float32
ALL = ("dp", "tensor")


def swap(rows):
    return lax.ppermute(rows, "tensor", [(0, 1), (1, 0)])


def dot(left, right, dims=((1,), (0,)), precision=None):
    return lax.dot_general(left, right, (dims, ((), ())), precision=precision, preferred_element_type=F32)


def dot_t(left, right):
    return dot(left, right, ((1,), (1,)))


def vmem(limit_mb, flops, moved):
    return dict(
        compiler_params=pltpu.CompilerParams(vmem_limit_bytes=limit_mb * 1024 * 1024),
        cost_estimate=pl.CostEstimate(flops=flops, bytes_accessed=moved, transcendentals=0),
    )


WHOLE = pl.BlockSpec(memory_space=pltpu.VMEM)
SCALAR = pl.BlockSpec(memory_space=pltpu.SMEM)
ANYWHERE = pl.BlockSpec(memory_space=pl.ANY)


def groups(ref):
    return [ref[:, 16 * g : 16 * g + 16, :].reshape(ref.shape[0] * 16, ref.shape[2]) for g in range(3)]


def attend_kernel(t_ref, got_ref, x_ref, so_ref, bias_ref, keep_ref, give_ref, ctx_ref, qkv_ref, probs_ref, wo_ref):
    one, two, three = groups(got_ref)
    q = (dot(x_ref[0], one) + dot(x_ref[2], three)).astype(BF)
    k = (dot(x_ref[1], one) + dot(x_ref[3], three)).astype(BF)
    v = (dot(x_ref[0], two) + dot(x_ref[4], three)).astype(BF)
    qkv_ref[0], qkv_ref[1], qkv_ref[2] = q, k, v
    cols = q.shape[1]
    for half in range(2):
        wo_ref[:, half * cols : half * cols + cols] = (
            dot(so_ref[half], two) + dot(so_ref[2 + half], three)
        ).astype(BF)
    lane = lax.broadcasted_iota(jnp.int32, (q.shape[0], 128), 1)
    zero = jnp.zeros((q.shape[0], 128), BF)
    for pair in range(cols // 128):
        at = slice(128 * pair, 128 * pair + 128)
        q2, k2, v2 = q[:, at], k[:, at], v[:, at]
        outs = []
        for which in range(2):
            mine = (lane < 64) if which == 0 else (lane >= 64)
            scores = dot_t(jnp.where(mine, q2, zero), k2) + bias_ref[2 * pair + which]
            top = jnp.max(scores, axis=-1, keepdims=True)
            shifted = jnp.exp(scores - top)
            probs = (shifted * (1.0 / jnp.sum(shifted, axis=-1, keepdims=True))).astype(BF)
            probs_ref[2 * pair + which] = probs
            outs.append(dot(probs, v2))
        ctx_ref[:, at] = jnp.where(lane < 64, outs[0], outs[1]).astype(BF)
    part = dot(ctx_ref[...], wo_ref[...])
    rows = part.shape[0] // 2
    low, high = part[:rows], part[rows:]
    first = t_ref[0] == 0
    keep_ref[...] = jnp.where(first, low, high)
    give_ref[...] = jnp.where(first, high, low).astype(BF)


def attend(t, got, x, so, bias):
    cols, seq = got.shape[2], x.shape[1]
    heads = bias.shape[0]
    shape = jax.ShapeDtypeStruct
    return pl.pallas_call(
        attend_kernel,
        in_specs=[SCALAR] + [WHOLE] * 4,
        out_specs=[WHOLE] * 6,
        out_shape=[
            shape((seq // 2, 2 * cols), F32),
            shape((seq // 2, 2 * cols), BF),
            shape((seq, cols), BF),
            shape((3, seq, cols), BF),
            shape((heads, seq, seq), BF),
            shape((cols, 2 * cols), BF),
        ],
        **vmem(50, 4_000_000_000, 14_000_000),
    )(t, got, x, so, bias)


def attend_back_kernel(
    ga_ref, wo_ref, qkv_ref, probs_ref, hits_ref, gain_ref, router_ref, two_ref, got_any, xt_any, xot_any, s_any,
    send_ref, g3_ref, got_ref, xt_ref, xot_ref, s_ref, sems,
):
    moves = [
        pltpu.make_async_copy(source, target, sems.at[i])
        for i, (source, target) in enumerate([(xt_any, xt_ref), (xot_any, xot_ref), (got_any, got_ref), (s_any, s_ref)])
    ]
    for move in moves:
        move.start()
    ga = ga_ref[...]
    q, k, v = qkv_ref[0], qkv_ref[1], qkv_ref[2]
    seq, cols = q.shape
    gctx = dot_t(ga, wo_ref[...]).astype(BF)
    lane = lax.broadcasted_iota(jnp.int32, (seq, 128), 1)
    low = lane < 64
    zero = jnp.zeros((seq, 128), BF)
    row8 = lax.broadcasted_iota(jnp.int32, (8, 2 * seq), 0)
    along = [lax.broadcasted_iota(jnp.int32, (seq, seq), axis) for axis in range(2)]
    flip = (along[0] + along[1] == seq - 1).astype(F32).astype(BF)
    diagonals = jnp.zeros((8, 2 * seq), F32)
    for pair in range(cols // 128):
        at = slice(128 * pair, 128 * pair + 128)
        q2, k2, v2, c2 = q[:, at], k[:, at], v[:, at], gctx[:, at]
        parts = []
        for which in range(2):
            mine = low if which == 0 else jnp.logical_not(low)
            probs = probs_ref[2 * pair + which]
            probs_f = probs.astype(F32)
            grad_probs = dot_t(jnp.where(mine, c2, zero), v2)
            inner = jnp.sum(probs_f * grad_probs, axis=-1, keepdims=True)
            ds = (probs_f * (grad_probs - inner)).astype(BF)
            parts.append((dot(ds, k2), dot(ds.T, q2), dot(probs.T, c2)))
            wide = jnp.concatenate([dot(flip, ds), jnp.zeros((seq, seq), F32)], 1)
            rolled = pltpu.roll(wide, 0, 1, stride=1, stride_axis=0)
            sums = jnp.sum(rolled, axis=0, keepdims=True)
            diagonals = jnp.where(row8 == 2 * pair + which, sums, diagonals)
        for c in range(3):
            g3_ref[c, :, at] = jnp.where(low, parts[0][c], parts[1][c]).astype(BF)
    gq, gk, gv = g3_ref[0], g3_ref[1], g3_ref[2]
    ga0, ga1 = ga[:, :cols], ga[:, cols:]
    moves[0].wait()
    moves[1].wait()
    one = dot(xt_ref[0], gq) + dot(xt_ref[1], gk)
    two = dot(xt_ref[0], gv) + dot(xot_ref[0], ga0) + dot(xot_ref[1], ga1)
    three = (
        dot(xt_ref[2], gq) + dot(xt_ref[3], gk) + dot(xt_ref[4], gv) + dot(xot_ref[2], ga0) + dot(xot_ref[3], ga1)
    )
    moves[2].wait()
    moves[3].wait()
    gain = jnp.zeros((128, gain_ref.shape[1]), F32)
    for g, (grad, weight) in enumerate(zip((one, two, three), groups(got_ref))):
        send_ref[:, 16 * g : 16 * g + 16, :] = grad.astype(BF).reshape(send_ref.shape[0], 16, cols)
        product = grad * weight.astype(F32)
        product = (product[:, :128] + product[:, 128:256] + product[:, 256:]).astype(BF)
        gain = gain + dot(product.T, s_ref[g])
    gain = jnp.sum(gain, axis=0, keepdims=True) / gain_ref[...]
    table = jnp.dot(diagonals, hits_ref[...], precision=PRECISE, preferred_element_type=F32)
    head_of = lax.broadcasted_iota(jnp.int32, table.shape, 1) // 64
    table = jnp.sum(
        jnp.where(head_of == lax.broadcasted_iota(jnp.int32, table.shape, 0), table, 0.0), axis=0, keepdims=True
    )
    gain_two = two_ref[...]
    row = lax.broadcasted_iota(jnp.int32, (8, cols), 0)
    tiny = jnp.zeros((8, cols), F32)
    for i, value in enumerate(
        (router_ref[...], gain[:, :cols], gain[:, cols:], gain_two[:, :cols], gain_two[:, cols:], table)
    ):
        tiny = jnp.where(row == i, value, tiny)
    send_ref[:, 48:56, :] = jnp.broadcast_to(tiny.astype(BF)[None], (send_ref.shape[0], 8, cols))


def attend_back(ga, wo, qkv, probs, hits, gain, router, two, got, xt, xot, s):
    _, seq, cols = qkv.shape
    shape = jax.ShapeDtypeStruct
    return pl.pallas_call(
        attend_back_kernel,
        in_specs=[WHOLE] * 8 + [ANYWHERE] * 4,
        out_specs=[WHOLE] * 2,
        out_shape=[shape(got.shape, BF), shape((3, seq, cols), BF)],
        scratch_shapes=[pltpu.VMEM(a.shape, BF) for a in (got, xt, xot, s)] + [pltpu.SemaphoreType.DMA((4,))],
        **vmem(50, 4_000_000_000, 16_000_000),
    )(ga, wo, qkv, probs, hits, gain, router, two, got, xt, xot, s)


def selections(n_dp, shard, cols, wo_rows):
    width = n_dp * shard
    d = jnp.arange(width, dtype=jnp.int32)[None, :, None]
    row = jnp.arange(n_dp * 16, dtype=jnp.int32)[None, None, :]
    start = jnp.array([0, 8, -8, -4, 0], jnp.int32)[:, None, None]
    big = jnp.array([False, False, True, True, True])[:, None, None]
    i = d % shard
    sel = (row == (d // shard) * 16 + i + start) & ((i >= 8) == big)
    d = jnp.arange(cols, dtype=jnp.int32)[None, :, None]
    half = jnp.array([0, 1, 0, 1], jnp.int32)[:, None, None]
    late = jnp.array([False, False, True, True])[:, None, None]
    i = d % wo_rows
    place = jnp.where(late, 12 + 2 * (i - 4), 8 + 2 * i) + half
    so = (row == (d // wo_rows) * 16 + place) & ((i >= 4) == late)
    return sel.astype(BF), so.astype(BF)


def per_device(
    tokens, gain_attn, rel_table, w_qkv, w_o, gain_moe, router, w_in, w_out, segments, offset_buckets, expert_ids, out_grad
):
    rows, width = tokens.shape
    shard, _, cols = w_qkv.shape
    wo_rows = w_o.shape[0]
    buckets, heads_all = rel_table.shape
    head = width // heads_all
    heads = cols // head
    seq = segments.shape[1]
    n_dp = lax.axis_size("dp")
    n_t = lax.axis_size("tensor")
    experts = n_dp
    cap = rows // experts
    t = lax.axis_index("tensor")
    me = lax.axis_index("dp")

    expert_index = expert_ids[:, 0]
    hits = expert_index[:, None] == jnp.arange(experts, dtype=jnp.int32)[None, :]
    counts = jnp.cumsum(hits.astype(jnp.int32), axis=0)
    rank = jnp.sum((counts - 1) * hits.astype(jnp.int32), axis=-1)
    target = expert_index * cap + rank
    slot_hit = jnp.arange(rows, dtype=jnp.int32)[:, None] == target[None, :]
    slot_low = slot_hit.astype(BF)

    g_slots = dot(slot_low, out_grad).astype(BF)
    pieces = [w_qkv[:, 0], w_qkv[:, 1], w_qkv[:, 2], w_o.reshape(wo_rows * 2, cols)]
    w_send = jnp.concatenate([x[:8] for x in pieces] + [x[8:] for x in pieces], 0)
    w_rows = w_send.shape[0]
    send_one = jnp.concatenate(
        [
            jnp.broadcast_to(w_send[None], (n_dp, w_rows, cols)),
            jnp.pad(g_slots.reshape(n_dp, cap * 2, cols), ((0, 0), (0, 8 - cap * 2), (0, 0))),
        ],
        1,
    )
    got_one = lax.all_to_all(send_one, "dp", 0, 0)

    xf = tokens.astype(F32)
    scale_one = lax.rsqrt(jnp.mean(xf * xf, axis=-1, keepdims=True) + EPSILON)
    hat_one = xf * scale_one
    first_rows = (hat_one * gain_attn).astype(BF)
    first_all = lax.all_gather(first_rows, "tensor", axis=0, tiled=True)

    sel, so = selections(n_dp, shard, cols, wo_rows)
    x = jnp.stack([dot(first_all, sel[c]).astype(BF) for c in range(5)])
    g_mine = got_one[:, w_rows : w_rows + 2 * cap].reshape(rows, width)
    g_all = lax.all_gather(g_mine, "tensor", axis=0)

    table_local = lax.dynamic_slice_in_dim(rel_table, t * heads, heads, 1)
    bucket_hits = (offset_buckets[:, None] == jnp.arange(buckets, dtype=jnp.int32)[None, :]).astype(F32)
    offset_bias = jnp.einsum("bh,rb->hr", table_local, bucket_hits, precision=PRECISE)
    span = 2 * seq
    tiled = jnp.tile(jnp.pad(offset_bias, ((0, 0), (0, 1))), (1, seq))
    skewed = tiled[:, seq - 1 : seq - 1 + seq * (span - 1)]
    bias = skewed.reshape(heads, seq, span - 1)[:, :, :seq]
    seg = segments[0]
    same = seg[:, None] == seg[None, :]
    bias = jnp.where(same[None], bias, MASKED)
    keep, give, context, qkv, probs, wo_full = attend(t.reshape(1), got_one, x, so, bias)
    mid = xf + (keep + swap(give).astype(F32))
    scale_two = lax.rsqrt(jnp.mean(mid * mid, axis=-1, keepdims=True) + EPSILON)
    second = mid * scale_two * gain_moe

    out_slots = dot(slot_low, second.astype(BF)).astype(BF)
    send_two = jnp.broadcast_to(out_slots.reshape(n_dp, 1, cap, width), (n_dp, n_t, cap, width))
    arrived = lax.all_to_all(send_two.reshape(n_dp * n_t, cap, width), ALL, 0, 0)
    arrived = arrived.reshape(n_dp * n_t * cap, width)
    g_rows = jnp.transpose(g_all.reshape(n_t, n_dp, cap, width), (1, 0, 2, 3)).reshape(n_dp * n_t * cap, width)

    logits_home = jnp.dot(second, router, precision=PRECISE)
    gate_home = jnp.sum(jax.nn.softmax(logits_home, axis=-1) * hits.astype(F32), axis=-1, keepdims=True)

    w1, w2 = w_in[0], w_out[0]
    pre = dot(arrived, w1)
    activated, gelu_back = jax.vjp(lambda u: jax.nn.gelu(u, approximate=False), pre)
    hidden = activated.astype(BF)
    out_part = dot(hidden, w2)
    logits = jnp.dot(arrived.astype(F32), router, precision=PRECISE)
    r_probs = jax.nn.softmax(logits, axis=-1)
    mine = (jnp.arange(experts, dtype=jnp.int32) == me).astype(F32)[None, :]
    gate = jnp.sum(r_probs * mine, axis=-1, keepdims=True)
    g_f = g_rows.astype(F32)
    grad_expert = (gate * g_f).astype(BF)
    grad_gate = jnp.sum(g_f * out_part, axis=-1, keepdims=True)
    grad_logits = grad_gate * gate * (mine - r_probs)
    grad_hidden = dot(grad_expert, w2, ((1,), (1,)))
    grad_pre = gelu_back(grad_hidden)[0].astype(BF)
    grad_disp = dot(grad_pre, w1, ((1,), (1,))) + dot(grad_logits, router, ((1,), (1,)), PRECISE)
    router_part = dot(grad_logits, arrived.astype(F32), ((0,), (0,)), PRECISE)

    both = jnp.concatenate(
        [out_part.astype(BF).reshape(n_dp * n_t, cap, width), grad_disp.astype(BF).reshape(n_dp * n_t, cap, width)], 1
    )
    r_send = jnp.pad(router_part.astype(BF).reshape(n_dp * n_t, 1, cols), ((0, 0), (0, 0), (0, width - cols)))
    got_three = lax.all_to_all(jnp.concatenate([both, r_send], 1), ALL, 0, 0)

    grad_w_out = dot(hidden, grad_expert, ((0,), (0,)))
    grad_w_in = dot(arrived, grad_pre, ((0,), (0,)))

    got_f = got_three.astype(F32)
    summed = jnp.sum(got_f.reshape(n_dp, n_t, 2 * cap + 1, width), axis=1)
    slot_out = summed[:, :cap].reshape(rows, width)
    slot_grad = summed[:, cap : 2 * cap].reshape(rows, width)
    router_piece = jnp.sum(summed[:, 2 * cap, :cols], axis=0)
    slot_f = slot_hit.astype(F32)
    expert_out = dot(slot_f, slot_out, ((0,), (0,)), PRECISE)
    grad_second = dot(slot_f, slot_grad, ((0,), (0,)), PRECISE)
    activations = (mid + gate_home * expert_out).astype(BF)
    u2 = grad_second * gain_moe
    gain_two = jnp.sum(grad_second * mid * scale_two, axis=0)
    spread = jnp.mean(u2 * mid, axis=-1, keepdims=True)
    grad_mid = out_grad.astype(F32) + (scale_two * u2 - scale_two * scale_two * scale_two * mid * spread)
    grad_attn = lax.all_gather(grad_mid.astype(BF), "tensor", axis=0, tiled=True)

    xt = jnp.stack([dot(sel[c], first_all, ((0,), (1,))).astype(BF) for c in range(5)])
    xot = jnp.stack([dot(so[c], context, ((0,), (1,))).astype(BF) for c in range(4)])
    back = jnp.stack([(sel[0] + sel[1]).T, sel[0].T, (sel[2] + sel[3] + sel[4]).T])
    hits_wide = jnp.tile(jnp.pad(bucket_hits, ((0, 1), (0, 64 - buckets))), (1, heads))
    send_four, grad3 = attend_back(
        grad_attn, wo_full, qkv, probs, hits_wide, gain_attn[None], router_piece[None], gain_two[None], got_one, xt, xot, back
    )

    got_four = lax.all_to_all(send_four, "dp", 0, 0)

    one, two, three = [got_one[:, 16 * g : 16 * g + 16].reshape(n_dp * 16, cols) for g in range(3)]
    spread_q, spread_k, spread_v = dot_t(grad3[0], one), dot_t(grad3[1], one), dot_t(grad3[2], two)
    last = [dot_t(grad3[c], three).astype(BF) for c in range(3)]
    grad_first = dot_t(spread_q.astype(BF), sel[0]) + dot_t(spread_k.astype(BF), sel[1]) + dot_t(spread_v.astype(BF), sel[0])
    grad_first = grad_first + sum(dot_t(last[c], sel[2 + c]) for c in range(3))
    keep_first = lax.dynamic_slice_in_dim(grad_first, t * rows, rows, 0)
    give_first = lax.dynamic_slice_in_dim(grad_first, (1 - t) * rows, rows, 0).astype(BF)
    grad_first_own = keep_first + swap(give_first).astype(F32)
    u1 = grad_first_own * gain_attn
    spread_one = jnp.mean(u1 * xf, axis=-1, keepdims=True)
    input_grad = (grad_mid + (scale_one * u1 - scale_one * scale_one * scale_one * xf * spread_one)).astype(BF)

    tiny_got = got_four[:, w_rows : w_rows + 6].astype(F32)
    router_half = tiny_got[:, 0]
    sums = jnp.sum(tiny_got[:, 1:], axis=0).reshape(-1)
    packed = jnp.concatenate([router_half, sums.reshape(-1, cols)], 0)
    other = swap(packed)
    low, high = jnp.where(t == 0, packed, other), jnp.where(t == 0, other, packed)
    grad_router = jnp.concatenate([low[:n_dp], high[:n_dp]], 1).T
    total = (packed[n_dp:] + other[n_dp:]).reshape(-1)
    gain_one_sum, gain_two_sum = total[:width], total[width : 2 * width]
    tables = [x[-1].reshape(heads, 64)[:, :buckets] for x in (low, high)]
    table_sum = jnp.concatenate(tables, 0).T
    weights = jnp.sum(got_four[:, :w_rows].astype(F32), axis=0)
    full = [jnp.concatenate([weights[8 * c : 8 * c + 8], weights[32 + 4 * c : 36 + 4 * c]], 0) for c in range(4)]
    grad_qkv_shard = jnp.stack(full[:3], 1)
    grad_o_shard = full[3].reshape(wo_rows, width)
    return (
        activations,
        input_grad,
        gain_one_sum,
        table_sum,
        grad_qkv_shard,
        grad_o_shard,
        gain_two_sum,
        grad_router,
        grad_w_in[None],
        grad_w_out[None],
    )


def solution(mesh):
    in_specs = (
        P(("dp", "tensor"), None),
        P(),
        P(),
        P("dp", None, "tensor"),
        P(("tensor", "dp"), None),
        P(),
        P(),
        P("dp", None, "tensor"),
        P("dp", "tensor", None),
        P("dp", None),
        P(),
        P(("dp", "tensor"), None),
        P(("dp", "tensor"), None),
    )
    out_specs = (
        P(("dp", "tensor"), None),
        P(("dp", "tensor"), None),
        P(),
        P(),
        P("dp", None, "tensor"),
        P(("tensor", "dp"), None),
        P(),
        P(),
        P("dp", None, "tensor"),
        P("dp", "tensor", None),
    )
    return jax.shard_map(per_device, mesh=mesh, in_specs=in_specs, out_specs=out_specs, check_vma=False)
```

```python
import jax
import jax.numpy as jnp
import numpy as np
from jax import lax
from jax.experimental import pallas as pl
from jax.experimental.pallas import tpu as pltpu
from jax.sharding import PartitionSpec as P

PRECISE = lax.Precision.HIGHEST
EPSILON = 1e-06
MASKED = -1000000000.0
BF = jnp.bfloat16
F32 = jnp.float32
ALL = ("dp", "tensor")


def swap(rows):
    return lax.ppermute(rows, "tensor", [(0, 1), (1, 0)])


def dot(left, right, dims=((1,), (0,)), precision=None):
    return lax.dot_general(left, right, (dims, ((), ())), precision=precision, preferred_element_type=F32)


def dot_t(left, right):
    return dot(left, right, ((1,), (1,)))


def vmem(limit_mb, flops, moved):
    return dict(
        compiler_params=pltpu.CompilerParams(vmem_limit_bytes=limit_mb * 1024 * 1024),
        cost_estimate=pl.CostEstimate(flops=flops, bytes_accessed=moved, transcendentals=0),
    )


WHOLE = pl.BlockSpec(memory_space=pltpu.VMEM)
SCALAR = pl.BlockSpec(memory_space=pltpu.SMEM)
ANYWHERE = pl.BlockSpec(memory_space=pl.ANY)


def groups(ref):
    return [ref[:, 16 * g : 16 * g + 16, :].reshape(ref.shape[0] * 16, ref.shape[2]) for g in range(3)]


def attend_kernel(t_ref, got_ref, x_ref, so_ref, bias_ref, keep_ref, give_ref, ctx_ref, qkv_ref, probs_ref, wo_ref):
    one, two, three = groups(got_ref)
    q = (dot(x_ref[0], one) + dot(x_ref[2], three)).astype(BF)
    k = (dot(x_ref[1], one) + dot(x_ref[3], three)).astype(BF)
    v = (dot(x_ref[0], two) + dot(x_ref[4], three)).astype(BF)
    qkv_ref[0], qkv_ref[1], qkv_ref[2] = q, k, v
    cols = q.shape[1]
    for half in range(2):
        wo_ref[:, half * cols : half * cols + cols] = (
            dot(so_ref[half], two) + dot(so_ref[2 + half], three)
        ).astype(BF)
    lane = lax.broadcasted_iota(jnp.int32, (q.shape[0], 128), 1)
    zero = jnp.zeros((q.shape[0], 128), BF)
    for pair in range(cols // 128):
        at = slice(128 * pair, 128 * pair + 128)
        q2, k2, v2 = q[:, at], k[:, at], v[:, at]
        outs = []
        for which in range(2):
            mine = (lane < 64) if which == 0 else (lane >= 64)
            scores = dot_t(jnp.where(mine, q2, zero), k2) + bias_ref[2 * pair + which]
            top = jnp.max(scores, axis=-1, keepdims=True)
            shifted = jnp.exp(scores - top)
            probs = (shifted * (1.0 / jnp.sum(shifted, axis=-1, keepdims=True))).astype(BF)
            probs_ref[2 * pair + which] = probs
            outs.append(dot(probs, v2))
        ctx_ref[:, at] = jnp.where(lane < 64, outs[0], outs[1]).astype(BF)
    part = dot(ctx_ref[...], wo_ref[...])
    rows = part.shape[0] // 2
    low, high = part[:rows], part[rows:]
    first = t_ref[0] == 0
    keep_ref[...] = jnp.where(first, low, high)
    give_ref[...] = jnp.where(first, high, low).astype(BF)


def attend(t, got, x, so, bias):
    cols, seq = got.shape[2], x.shape[1]
    heads = bias.shape[0]
    shape = jax.ShapeDtypeStruct
    return pl.pallas_call(
        attend_kernel,
        in_specs=[SCALAR] + [WHOLE] * 4,
        out_specs=[WHOLE] * 6,
        out_shape=[
            shape((seq // 2, 2 * cols), F32),
            shape((seq // 2, 2 * cols), BF),
            shape((seq, cols), BF),
            shape((3, seq, cols), BF),
            shape((heads, seq, seq), BF),
            shape((cols, 2 * cols), BF),
        ],
        **vmem(30, 4_000_000_000, 14_000_000),
    )(t, got, x, so, bias)


def attend_back_kernel(
    ga_ref, wo_ref, qkv_ref, probs_ref, hits_ref, gain_ref, router_ref, two_ref, got_any, xt_any, xot_any, s_any,
    send_ref, g3_ref, got_ref, xt_ref, xot_ref, s_ref, sems,
):
    moves = [
        pltpu.make_async_copy(source, target, sems.at[i])
        for i, (source, target) in enumerate([(xt_any, xt_ref), (xot_any, xot_ref), (got_any, got_ref), (s_any, s_ref)])
    ]
    for move in moves:
        move.start()
    ga = ga_ref[...]
    q, k, v = qkv_ref[0], qkv_ref[1], qkv_ref[2]
    seq, cols = q.shape
    gctx = dot_t(ga, wo_ref[...]).astype(BF)
    lane = lax.broadcasted_iota(jnp.int32, (seq, 128), 1)
    low = lane < 64
    zero = jnp.zeros((seq, 128), BF)
    row8 = lax.broadcasted_iota(jnp.int32, (8, 2 * seq), 0)
    along = [lax.broadcasted_iota(jnp.int32, (seq, seq), axis) for axis in range(2)]
    flip = (along[0] + along[1] == seq - 1).astype(F32).astype(BF)
    diagonals = jnp.zeros((8, 2 * seq), F32)
    for pair in range(cols // 128):
        at = slice(128 * pair, 128 * pair + 128)
        q2, k2, v2, c2 = q[:, at], k[:, at], v[:, at], gctx[:, at]
        parts = []
        for which in range(2):
            mine = low if which == 0 else jnp.logical_not(low)
            probs = probs_ref[2 * pair + which]
            probs_f = probs.astype(F32)
            grad_probs = dot_t(jnp.where(mine, c2, zero), v2)
            inner = jnp.sum(probs_f * grad_probs, axis=-1, keepdims=True)
            ds = (probs_f * (grad_probs - inner)).astype(BF)
            parts.append((dot(ds, k2), dot(ds.T, q2), dot(probs.T, c2)))
            wide = jnp.concatenate([dot(flip, ds), jnp.zeros((seq, seq), F32)], 1)
            rolled = pltpu.roll(wide, 0, 1, stride=1, stride_axis=0)
            sums = jnp.sum(rolled, axis=0, keepdims=True)
            diagonals = jnp.where(row8 == 2 * pair + which, sums, diagonals)
        for c in range(3):
            g3_ref[c, :, at] = jnp.where(low, parts[0][c], parts[1][c]).astype(BF)
    gq, gk, gv = g3_ref[0], g3_ref[1], g3_ref[2]
    ga0, ga1 = ga[:, :cols], ga[:, cols:]
    moves[0].wait()
    moves[1].wait()
    one = dot(xt_ref[0], gq) + dot(xt_ref[1], gk)
    two = dot(xt_ref[0], gv) + dot(xot_ref[0], ga0) + dot(xot_ref[1], ga1)
    three = (
        dot(xt_ref[2], gq) + dot(xt_ref[3], gk) + dot(xt_ref[4], gv) + dot(xot_ref[2], ga0) + dot(xot_ref[3], ga1)
    )
    moves[2].wait()
    moves[3].wait()
    gain = jnp.zeros((128, gain_ref.shape[1]), F32)
    for g, (grad, weight) in enumerate(zip((one, two, three), groups(got_ref))):
        send_ref[:, 16 * g : 16 * g + 16, :] = grad.astype(BF).reshape(send_ref.shape[0], 16, cols)
        product = grad * weight.astype(F32)
        product = (product[:, :128] + product[:, 128:256] + product[:, 256:]).astype(BF)
        gain = gain + dot(product.T, s_ref[g])
    gain = jnp.sum(gain, axis=0, keepdims=True) / gain_ref[...]
    table = jnp.dot(diagonals, hits_ref[...], precision=PRECISE, preferred_element_type=F32)
    head_of = lax.broadcasted_iota(jnp.int32, table.shape, 1) // 64
    table = jnp.sum(
        jnp.where(head_of == lax.broadcasted_iota(jnp.int32, table.shape, 0), table, 0.0), axis=0, keepdims=True
    )
    gain_two = two_ref[...]
    row = lax.broadcasted_iota(jnp.int32, (8, cols), 0)
    tiny = jnp.zeros((8, cols), F32)
    for i, value in enumerate(
        (router_ref[...], gain[:, :cols], gain[:, cols:], gain_two[:, :cols], gain_two[:, cols:], table)
    ):
        tiny = jnp.where(row == i, value, tiny)
    send_ref[:, 48:56, :] = jnp.broadcast_to(tiny.astype(BF)[None], (send_ref.shape[0], 8, cols))


def attend_back(ga, wo, qkv, probs, hits, gain, router, two, got, xt, xot, s):
    _, seq, cols = qkv.shape
    shape = jax.ShapeDtypeStruct
    return pl.pallas_call(
        attend_back_kernel,
        in_specs=[WHOLE] * 8 + [ANYWHERE] * 4,
        out_specs=[WHOLE] * 2,
        out_shape=[shape(got.shape, BF), shape((3, seq, cols), BF)],
        scratch_shapes=[pltpu.VMEM(a.shape, BF) for a in (got, xt, xot, s)] + [pltpu.SemaphoreType.DMA((4,))],
        **vmem(40, 4_000_000_000, 16_000_000),
    )(ga, wo, qkv, probs, hits, gain, router, two, got, xt, xot, s)


def iota(rows, columns, axis):
    return lax.broadcasted_iota(jnp.int32, (rows, columns), axis)


def split(value):
    high = value.astype(BF)
    return high, (value - high.astype(F32)).astype(BF)


def onehot(found):
    return jnp.where(found, 1.0, 0.0).astype(BF)


def ranks_along(ids, experts):
    rows = ids.shape[1]
    hits = iota(experts, rows, 0) == ids
    before = onehot(iota(rows, rows, 0) < iota(rows, rows, 1))
    return jnp.sum(dot(onehot(hits), before) * hits.astype(F32), axis=0, keepdims=True).astype(jnp.int32)


def ranks_down(ids, experts):
    rows = ids.shape[0]
    hits = iota(rows, experts, 1) == ids
    before = onehot(iota(rows, rows, 1) < iota(rows, rows, 0))
    return jnp.sum(dot(before, onehot(hits)) * hits.astype(F32), axis=1, keepdims=True).astype(jnp.int32)


def start_kernel(ids_ref, w_ref, wo_ref, og_ref, qsel_ref, osel_ref, send_ref):
    peers, _, cols = send_ref.shape
    og = og_ref[...]
    weights = dot(qsel_ref[...], w_ref[...])
    ids = ids_ref[...]
    base = ids * 8 + ranks_along(ids, peers) * 2
    row = iota(peers * 8, ids.shape[1], 0)
    rows_out = jnp.zeros((peers * 8, cols), F32)
    for half in range(2):
        at = slice(half * cols, half * cols + cols)
        weights = weights + dot(osel_ref[half], wo_ref[:, at])
        rows_out = rows_out + dot(onehot(row == base + half), og[:, at])
    send_ref[:, :48, :] = jnp.broadcast_to(weights.astype(BF)[None], (peers, 48, cols))
    send_ref[:, 48:56, :] = rows_out.astype(BF).reshape(peers, 8, cols)


def start_send(ids_row, w_rows, w_o, out_grad, peers, shard, wo_rows):
    cols = w_rows.shape[1]
    qsel, osel = np.zeros((48, 3 * shard), np.float32), np.zeros((2, 48, wo_rows), np.float32)
    for c in range(4):
        for i in range(shard):
            place = 8 * c + i if i < 8 else 32 + 4 * c + i - 8
            if c < 3:
                qsel[place, 3 * i + c] = 1
            else:
                osel[i % 2, place, i // 2] = 1
    return pl.pallas_call(
        start_kernel,
        in_specs=[WHOLE] * 6,
        out_specs=WHOLE,
        out_shape=jax.ShapeDtypeStruct((peers, 56, cols), BF),
        **vmem(24, 200_000_000, 3_500_000),
    )(ids_row, w_rows, w_o, out_grad, jnp.asarray(qsel, BF), jnp.asarray(osel, BF))


def prepare_kernel(
    first_ref, down_ref, along_ref, so_down_ref, offset_ref, seg_down_ref, seg_along_ref, x_ref, xt_ref, so_ref, s_ref, bias_ref
):
    first = first_ref[...]
    width, lanes = first.shape[1], x_ref.shape[2]
    for c in range(5):
        x_ref[c] = dot(first, onehot(iota(width, lanes, 1) == down_ref[:, c : c + 1])).astype(BF)
        sel = onehot(iota(lanes, width, 0) == along_ref[c : c + 1, :])
        xt_ref[c] = dot_t(sel, first).astype(BF)
        if c == 0:
            s_ref[0] = sel
            s_ref[1] = sel
        elif c == 1:
            s_ref[0] = s_ref[0] + sel
        elif c == 2:
            s_ref[2] = sel
        else:
            s_ref[2] = s_ref[2] + sel
    for c in range(4):
        so_ref[c] = onehot(iota(so_ref.shape[1], lanes, 1) == so_down_ref[:, c : c + 1])
    heads, seq, _ = bias_ref.shape
    same = seg_down_ref[...] == seg_along_ref[...]
    for h in range(heads):
        wide = jnp.broadcast_to(offset_ref[h : h + 1, :], (seq, 2 * seq))
        wide = pltpu.roll(wide, seq + 1, 1, stride=1, stride_axis=0)
        bias_ref[h] = jnp.where(same, wide[:, :seq], MASKED)


def places(n_dp, shard, cols, wo_rows):
    d = np.arange(n_dp * shard)
    i, p = d % shard, d // shard
    down = np.full((n_dp * shard, 8), -1, np.int32)
    for c, (start, big) in enumerate([(0, False), (8, False), (-8, True), (-4, True), (0, True)]):
        down[:, c] = np.where((i >= 8) == big, p * 16 + i + start, -1)
    d = np.arange(cols)
    i, p = d % wo_rows, d // wo_rows
    so_down = np.full((cols, 8), -1, np.int32)
    for c in range(4):
        half, late = c % 2, c // 2 == 1
        place = 12 + 2 * (i - 4) + half if late else 8 + 2 * i + half
        so_down[:, c] = np.where((i >= 4) == late, p * 16 + place, -1)
    return down, so_down


def prepare(first_all, offset_bias, segments, down, so_down, n_dp):
    seq, width = first_all.shape
    cols, lanes, heads = so_down.shape[0], n_dp * 16, 6
    shape = jax.ShapeDtypeStruct
    return pl.pallas_call(
        prepare_kernel,
        in_specs=[WHOLE] * 7,
        out_specs=[WHOLE] * 5,
        out_shape=[
            shape((5, seq, lanes), BF),
            shape((5, lanes, seq), BF),
            shape((4, cols, lanes), BF),
            shape((3, lanes, width), BF),
            shape((heads, seq, seq), F32),
        ],
        **vmem(36, 4_000_000_000, 16_000_000),
    )(
        first_all,
        jnp.asarray(down),
        jnp.asarray(np.ascontiguousarray(down.T)),
        jnp.asarray(so_down),
        offset_bias,
        segments.reshape(seq, 1),
        segments,
    )


def dispatch_kernel(ids_ref, tokens_ref, keep_ref, got_ref, gain_ref, send_ref, mid_ref, second_ref):
    mid = tokens_ref[...].astype(F32) + (keep_ref[...] + got_ref[...].astype(F32))
    scale = lax.rsqrt(jnp.mean(mid * mid, axis=-1, keepdims=True) + EPSILON)
    second = mid * scale * gain_ref[...]
    mid_ref[...] = mid
    second_ref[...] = second
    low = second.astype(BF)
    ids = ids_ref[...]
    rows = ids.shape[1]
    base = ids * 16 + ranks_along(ids, rows // 2) * 3
    row = iota(send_ref.shape[0], rows, 0)
    total = jnp.zeros(send_ref.shape, F32)
    for j in range(3):
        sel = onehot((row == base + j) | (row == base + (8 + j)))
        total = total + dot(sel, low[:, 256 * j : 256 * j + 256])
    send_ref[...] = total.astype(BF)


def dispatch(ids_row, tokens, keep, got, gain):
    rows, width = tokens.shape
    shape = jax.ShapeDtypeStruct
    return pl.pallas_call(
        dispatch_kernel,
        in_specs=[WHOLE] * 5,
        out_specs=[WHOLE] * 3,
        out_shape=[shape((rows * 8, 256), BF), shape((rows, width), F32), shape((rows, width), F32)],
        **vmem(16, 200_000_000, 2_000_000),
    )(ids_row, tokens, keep, got, gain)


def between_kernel(
    ids_ref, ctx_ref, so_along_ref, g_ref, second_ref, router_ref, xot_ref, rows_ref, selt_ref, gate_ref
):
    ctx = ctx_ref[...]
    lanes = xot_ref.shape[1]
    for c in range(4):
        sel = onehot(iota(lanes, ctx.shape[1], 0) == so_along_ref[c : c + 1, :])
        xot_ref[c] = dot_t(sel, ctx).astype(BF)
    g = g_ref[...]
    cols = g.shape[1]
    count, half_rows = rows_ref.shape[0], g.shape[0] // 2
    r = iota(count, 1, 0)
    pair = r & (count // 2 - 1)
    base = (pair & 1) * half_rows + (pair >> 1) * 8 + (r >= count // 2).astype(jnp.int32) * 2
    for half in range(2):
        sel = onehot(iota(count, g.shape[0], 1) == base + half)
        rows_ref[:, half * cols : half * cols + cols] = dot(sel, g).astype(BF)
    ids = ids_ref[...]
    rows = ids.shape[0]
    experts = router_ref.shape[1]
    base = ids * 32 + ranks_down(ids, experts) * 3
    lane = iota(rows, selt_ref.shape[1], 1)
    for part in range(6):
        shift = part if part < 3 else part + 3
        selt_ref[rows * part : rows * part + rows, :] = onehot((lane == base + shift) | (lane == base + (16 + shift)))
    s_high, s_low = split(second_ref[...])
    r_high, r_low = split(router_ref[...])
    logits = dot(s_high, r_high) + (dot(s_low, r_high) + dot(s_high, r_low))
    shifted = jnp.exp(logits - jnp.max(logits, axis=-1, keepdims=True))
    hit = iota(rows, experts, 1) == ids
    gate_ref[...] = jnp.sum(jnp.where(hit, shifted, 0.0), axis=-1, keepdims=True) / jnp.sum(
        shifted, axis=-1, keepdims=True
    )


def between(ids, ctx, so_along, g_all, second, router, n_dp):
    rows = ids.shape[0]
    seq, cols = ctx.shape
    shape = jax.ShapeDtypeStruct
    return pl.pallas_call(
        between_kernel,
        in_specs=[WHOLE] * 6,
        out_specs=[WHOLE] * 4,
        out_shape=[
            shape((4, n_dp * 16, seq), BF),
            shape((2 * rows, 2 * cols), BF),
            shape((6 * rows, rows * 16), BF),
            shape((rows, 1), F32),
        ],
        **vmem(24, 2_000_000_000, 8_000_000),
    )(ids, ctx, so_along, g_all, second, router)


def expert_kernel(
    me_ref, got_ref, g_ref, router_ref, w1_ref, w2_ref, send_ref, arrived_ref, hidden_ref, pre_ref, ge_ref, *stages
):
    got = got_ref[...]
    count = g_ref.shape[0]
    half = count // 2
    r = iota(count, 1, 0)
    base = (r & (half - 1)) * 8 + (r >= half).astype(jnp.int32) * 3
    lane = iota(count, got.shape[0], 1)
    for j in range(3):
        arrived_ref[:, 256 * j : 256 * j + 256] = dot(onehot(lane == base + j), got).astype(BF)
    arrived = arrived_ref[...]
    r_high, r_low = split(router_ref[...])
    logits = dot(arrived, r_high) + dot(arrived, r_low)
    shifted = jnp.exp(logits - jnp.max(logits, axis=-1, keepdims=True))
    probs = shifted / jnp.sum(shifted, axis=-1, keepdims=True)
    mine = (iota(count, probs.shape[1], 1) == me_ref[0]).astype(F32)
    gate = jnp.sum(probs * mine, axis=-1, keepdims=True)
    g = g_ref[...].astype(F32)
    ge = (gate * g).astype(BF)
    ge_ref[...] = ge
    width, hidden_cols = w1_ref.shape
    step = 256
    out = jnp.zeros((count, width), F32)
    back = jnp.zeros((count, width), F32)
    for f in range(0, hidden_cols, step):
        at = slice(f, f + step)
        w1, w2 = w1_ref[:, at], w2_ref[at, :]
        u = dot(arrived, w1)
        cdf = 0.5 + 0.5 * lax.erf(u * 0.7071067811865476)
        hidden = (u * cdf).astype(BF)
        slope = cdf + u * (jnp.exp(-0.5 * u * u) * 0.3989422804014327)
        grad = (dot_t(ge, w2) * slope).astype(BF)
        hidden_ref[:, at] = hidden
        pre_ref[:, at] = grad
        out = out + dot(hidden, w2)
        back = back + dot_t(grad, w1)
    grad_gate = jnp.sum(g * out, axis=-1, keepdims=True)
    grad_logits = grad_gate * gate * (mine - probs)
    l_high, l_low = split(grad_logits)
    back = back + (dot_t(l_high, r_high) + (dot_t(l_low, r_high) + dot_t(l_high, r_low)))
    t_high, t_low = split(grad_logits.T)
    router_part = dot(t_high, arrived) + dot(t_low, arrived)
    cols = width // 2
    for side, stage in enumerate(stages):
        stage[...] = jnp.zeros(stage.shape, F32)
        for j in range(3):
            at = slice(256 * j + 128 * side, 256 * j + 128 * side + 128)
            for s in range(2):
                rows = slice(s * half, s * half + half)
                stage[pl.ds(s * 3 + j, half, stride=16), :] = out[rows, at]
                stage[pl.ds(6 + s * 3 + j, half, stride=16), :] = back[rows, at]
        for t in range(2):
            for r in range(2 - side):
                at = cols * t + 256 * r + 128 * side
                stage[pl.ds(12 + r + 16 * t, half // 2, stride=32), :] = router_part[:, at : at + 128]
        send_ref[:, 128 * side : 128 * side + 128] = stage[...].astype(BF)


def expert(me, got, g_rows, router, w1, w2):
    count, width = g_rows.shape
    hidden = w1.shape[1]
    shape = jax.ShapeDtypeStruct
    return pl.pallas_call(
        expert_kernel,
        in_specs=[SCALAR] + [WHOLE] * 5,
        out_specs=[WHOLE] * 5,
        out_shape=[
            shape((count * 8, 256), BF),
            shape((count, width), BF),
            shape((count, hidden), BF),
            shape((count, hidden), BF),
            shape((count, width), BF),
        ],
        scratch_shapes=[pltpu.VMEM((count * 8, 128), F32)] * 2,
        **vmem(32, 3_000_000_000, 9_000_000),
    )(me, got, g_rows, router, w1, w2)


def home_kernel(
    got_ref, selt_ref, mid_ref, gate_ref, gain_ref, og_ref, act_ref, gmid_ref, gattn_ref, router_ref, two_ref
):
    got = got_ref[...]
    rows = mid_ref.shape[0]
    sums = dot(selt_ref[...], got)
    out = jnp.concatenate([sums[rows * j : rows * j + rows] for j in range(3)], 1)
    grad_second = jnp.concatenate([sums[rows * j : rows * j + rows] for j in range(3, 6)], 1)
    lane = iota(16, got.shape[0], 1) & 15
    piece = dot(onehot(lane == iota(16, got.shape[0], 0) + 12), got)
    router_ref[...] = jnp.concatenate([piece[0:1], piece[1:2, :128]], 1)
    mid, gain = mid_ref[...], gain_ref[...]
    act_ref[...] = (mid + gate_ref[...] * out).astype(BF)
    scale = lax.rsqrt(jnp.mean(mid * mid, axis=-1, keepdims=True) + EPSILON)
    u = grad_second * gain
    two_ref[...] = jnp.sum(grad_second * mid * scale, axis=0, keepdims=True)
    spread = jnp.mean(u * mid, axis=-1, keepdims=True)
    gmid = og_ref[...].astype(F32) + (scale * u - scale * scale * scale * mid * spread)
    gmid_ref[...] = gmid
    gattn_ref[...] = gmid.astype(BF)


def home(got, selt, mid, gate, gain, out_grad):
    rows, width = mid.shape
    shape = jax.ShapeDtypeStruct
    return pl.pallas_call(
        home_kernel,
        in_specs=[WHOLE] * 6,
        out_specs=[WHOLE] * 5,
        out_shape=[
            shape((rows, width), BF),
            shape((rows, width), F32),
            shape((rows, width), BF),
            shape((1, width // 2), F32),
            shape((1, width), F32),
        ],
        **vmem(16, 500_000_000, 6_000_000),
    )(got, selt, mid, gate, gain, out_grad)


def per_device(
    tokens, gain_attn, rel_table, w_qkv, w_o, gain_moe, router, w_in, w_out, segments, offset_buckets, expert_ids, out_grad
):
    rows, width = tokens.shape
    shard, _, cols = w_qkv.shape
    wo_rows = w_o.shape[0]
    buckets, heads_all = rel_table.shape
    heads = cols // (width // heads_all)
    seq = segments.shape[1]
    n_dp = lax.axis_size("dp")
    n_t = lax.axis_size("tensor")
    t = lax.axis_index("tensor")
    me = lax.axis_index("dp")
    ids_row = expert_ids.reshape(1, rows)

    send_one = start_send(ids_row, w_qkv.reshape(3 * shard, cols), w_o, out_grad, n_dp, shard, wo_rows)
    got_one = lax.all_to_all(send_one, "dp", 0, 0)

    xf = tokens.astype(F32)
    scale_one = lax.rsqrt(jnp.mean(xf * xf, axis=-1, keepdims=True) + EPSILON)
    first_rows = (xf * scale_one * gain_attn).astype(BF)
    first_all = lax.all_gather(first_rows, "tensor", axis=0, tiled=True)
    table_local = lax.dynamic_slice_in_dim(rel_table, t * heads, heads, 1)
    bucket_hits = (offset_buckets[:, None] == jnp.arange(buckets, dtype=jnp.int32)[None, :]).astype(F32)
    bucket_hits = jnp.pad(bucket_hits, ((0, 1), (0, 0)))
    offset_bias = jnp.einsum("bh,rb->hr", jnp.pad(table_local, ((0, 0), (0, 8 - heads))), bucket_hits, precision=PRECISE)
    hits_wide = jnp.tile(jnp.pad(bucket_hits, ((0, 0), (0, 64 - buckets))), (1, heads))
    down, so_down = places(n_dp, shard, cols, wo_rows)
    x, xt, so, back, bias = prepare(first_all, offset_bias, segments, down, so_down, n_dp)

    keep, give, context, qkv, probs, wo_full = attend(t.reshape(1), got_one, x, so, bias)
    gain_row = gain_moe[None]
    send_two, mid, second = dispatch(ids_row, tokens, keep, swap(give), gain_row)

    arrived_two = lax.all_to_all(send_two.reshape(n_dp * n_t, 8, 256), ALL, 0, 0).reshape(n_dp * n_t * 8, 256)
    g_all = lax.all_gather(got_one[:, 48:56], "tensor", axis=0).reshape(n_t * n_dp * 8, cols)
    so_along = jnp.asarray(np.ascontiguousarray(so_down.T))
    xot, g_rows, selt, gate_home = between(expert_ids, context, so_along, g_all, second, router, n_dp)

    send_three, arrived, hidden, grad_pre, grad_expert = expert(me.reshape(1), arrived_two, g_rows, router, w_in[0], w_out[0])

    got_three = lax.all_to_all(send_three.reshape(n_dp * n_t, 16, 256), ALL, 0, 0).reshape(n_dp * n_t * 16, 256)
    grad_w_out = dot(hidden, grad_expert, ((0,), (0,)))
    grad_w_in = dot(arrived, grad_pre, ((0,), (0,)))
    activations, grad_mid, grad_own, router_piece, gain_two = home(got_three, selt, mid, gate_home, gain_row, out_grad)
    grad_attn = lax.all_gather(grad_own, "tensor", axis=0, tiled=True)

    send_four, grad3 = attend_back(
        grad_attn, wo_full, qkv, probs, hits_wide, gain_attn[None], router_piece, gain_two, got_one, xt, xot, back
    )

    got_four = lax.all_to_all(send_four, "dp", 0, 0)
    one, two, three = [got_one[:, 16 * g : 16 * g + 16].reshape(n_dp * 16, cols) for g in range(3)]
    sel_t = [(jnp.arange(n_dp * 16, dtype=jnp.int32)[:, None] == jnp.asarray(down[:, c])[None, :]).astype(BF) for c in range(5)]
    spread_q, spread_k, spread_v = dot_t(grad3[0], one), dot_t(grad3[1], one), dot_t(grad3[2], two)
    last = [dot_t(grad3[c], three).astype(BF) for c in range(3)]
    grad_first = dot(spread_q.astype(BF), sel_t[0]) + dot(spread_k.astype(BF), sel_t[1]) + dot(spread_v.astype(BF), sel_t[0])
    grad_first = grad_first + sum(dot(last[c], sel_t[2 + c]) for c in range(3))
    keep_first = lax.dynamic_slice_in_dim(grad_first, t * rows, rows, 0)
    give_first = lax.dynamic_slice_in_dim(grad_first, (1 - t) * rows, rows, 0).astype(BF)
    grad_first_own = keep_first + swap(give_first).astype(F32)
    u1 = grad_first_own * gain_attn
    spread_one = jnp.mean(u1 * xf, axis=-1, keepdims=True)
    input_grad = (grad_mid + (scale_one * u1 - scale_one * scale_one * scale_one * xf * spread_one)).astype(BF)

    tiny_got = got_four[:, 48:54].astype(F32)
    router_half = tiny_got[:, 0]
    sums = jnp.sum(tiny_got[:, 1:], axis=0)
    packed = jnp.concatenate([router_half, sums], 0)
    other = swap(packed)
    low, high = jnp.where(t == 0, packed, other), jnp.where(t == 0, other, packed)
    grad_router = jnp.concatenate([low[:n_dp], high[:n_dp]], 1).T
    total = (packed[n_dp:] + other[n_dp:]).reshape(-1)
    gain_one_sum, gain_two_sum = total[:width], total[width : 2 * width]
    tables = [y[-1].reshape(heads, 64)[:, :buckets] for y in (low, high)]
    table_sum = jnp.concatenate(tables, 0).T
    weights = jnp.sum(got_four[:, :48].astype(F32), axis=0)
    full = [jnp.concatenate([weights[8 * c : 8 * c + 8], weights[32 + 4 * c : 36 + 4 * c]], 0) for c in range(4)]
    grad_qkv_shard = jnp.stack(full[:3], 1)
    grad_o_shard = full[3].reshape(wo_rows, width)
    return (
        activations,
        input_grad,
        gain_one_sum,
        table_sum,
        grad_qkv_shard,
        grad_o_shard,
        gain_two_sum,
        grad_router,
        grad_w_in[None],
        grad_w_out[None],
    )


def solution(mesh):
    in_specs = (
        P(("dp", "tensor"), None),
        P(),
        P(),
        P("dp", None, "tensor"),
        P(("tensor", "dp"), None),
        P(),
        P(),
        P("dp", None, "tensor"),
        P("dp", "tensor", None),
        P("dp", None),
        P(),
        P(("dp", "tensor"), None),
        P(("dp", "tensor"), None),
    )
    out_specs = (
        P(("dp", "tensor"), None),
        P(("dp", "tensor"), None),
        P(),
        P(),
        P("dp", None, "tensor"),
        P(("tensor", "dp"), None),
        P(),
        P(),
        P("dp", None, "tensor"),
        P("dp", "tensor", None),
    )
    return jax.shard_map(per_device, mesh=mesh, in_specs=in_specs, out_specs=out_specs, check_vma=False)
```

```python
import jax
import jax.numpy as jnp
import numpy as np
from jax import lax
from jax.experimental import pallas as pl
from jax.experimental.pallas import tpu as pltpu
from jax.sharding import PartitionSpec as P

PRECISE = lax.Precision.HIGHEST
EPSILON = 1e-06
MASKED = -1000000000.0
BF = jnp.bfloat16
F32 = jnp.float32
ALL = ("dp", "tensor")


def swap(rows):
    return lax.ppermute(rows, "tensor", [(0, 1), (1, 0)])


def dot(left, right, dims=((1,), (0,)), precision=None):
    return lax.dot_general(left, right, (dims, ((), ())), precision=precision, preferred_element_type=F32)


def dot_t(left, right):
    return dot(left, right, ((1,), (1,)))


def vmem(limit_mb, flops, moved):
    return dict(
        compiler_params=pltpu.CompilerParams(vmem_limit_bytes=limit_mb * 1024 * 1024),
        cost_estimate=pl.CostEstimate(flops=flops, bytes_accessed=moved, transcendentals=0),
    )


WHOLE = "whole"
SCALAR = pl.BlockSpec(memory_space=pltpu.SMEM)


class Arriving:
    def __init__(self, buffer, move):
        self.buffer, self.move, self.shape = buffer, move, buffer.shape

    def __getitem__(self, index):
        if self.move is not None:
            self.move.wait()
            self.move = None
        return self.buffer[index]


class Leaving:
    def __init__(self, buffer, move):
        self.buffer, self.move, self.shape, self.sent = buffer, move, buffer.shape, False

    def __getitem__(self, index):
        return self.buffer[index]

    def __setitem__(self, index, value):
        self.buffer[index] = value

    def send(self):
        if not self.sent:
            self.move.start()
            self.sent = True


def staged_call(body, in_specs, out_specs, out_shape, scratch_shapes=(), **params):
    several = isinstance(out_shape, list)
    results = out_shape if several else [out_shape]
    moved = [i for i, kind in enumerate(in_specs) if kind is WHOLE]

    def kernel(*refs):
        refs = list(refs)
        ins, outs = refs[: len(in_specs)], refs[len(in_specs) : len(in_specs) + len(results)]
        rest = refs[len(in_specs) + len(results) :]
        in_buffers, rest = rest[: len(moved)], rest[len(moved) :]
        out_buffers, rest = rest[: len(results)], rest[len(results) :]
        in_sems, out_sems, extra = rest[0], rest[1], rest[2:]
        for n, (i, buffer) in enumerate(zip(moved, in_buffers)):
            move = pltpu.make_async_copy(ins[i], buffer, in_sems.at[n])
            move.start()
            ins[i] = Arriving(buffer, move)
        leaving = [
            Leaving(buffer, pltpu.make_async_copy(buffer, out, out_sems.at[n]))
            for n, (buffer, out) in enumerate(zip(out_buffers, outs))
        ]
        body(*ins, *leaving, *extra)
        for item in ins:
            if isinstance(item, Arriving) and item.move is not None:
                item.move.wait()
        for item in leaving:
            item.send()
        for item in leaving:
            item.move.wait()

    def call(*args):
        anywhere = pl.BlockSpec(memory_space=pl.ANY)
        return pl.pallas_call(
            kernel,
            in_specs=[anywhere if kind is WHOLE else kind for kind in in_specs],
            out_specs=[anywhere] * len(results) if several else anywhere,
            out_shape=out_shape,
            scratch_shapes=[pltpu.VMEM(args[i].shape, args[i].dtype) for i in moved]
            + [pltpu.VMEM(r.shape, r.dtype) for r in results]
            + [pltpu.SemaphoreType.DMA((len(moved),)), pltpu.SemaphoreType.DMA((len(results),))]
            + list(scratch_shapes),
            **params,
        )(*args)

    return call


def groups(ref):
    return [ref[:, 16 * g : 16 * g + 16, :].reshape(ref.shape[0] * 16, ref.shape[2]) for g in range(3)]


def attend_kernel(t_ref, got_ref, x_ref, so_ref, bias_ref, keep_ref, give_ref, ctx_ref, qkv_ref, probs_ref, wo_ref):
    one, two, three = groups(got_ref)
    q = (dot(x_ref[0], one) + dot(x_ref[2], three)).astype(BF)
    k = (dot(x_ref[1], one) + dot(x_ref[3], three)).astype(BF)
    v = (dot(x_ref[0], two) + dot(x_ref[4], three)).astype(BF)
    qkv_ref[0], qkv_ref[1], qkv_ref[2] = q, k, v
    qkv_ref.send()
    cols = q.shape[1]
    for half in range(2):
        wo_ref[:, half * cols : half * cols + cols] = (
            dot(so_ref[half], two) + dot(so_ref[2 + half], three)
        ).astype(BF)
    wo_ref.send()
    lane = lax.broadcasted_iota(jnp.int32, (q.shape[0], 128), 1)
    zero = jnp.zeros((q.shape[0], 128), BF)
    for pair in range(cols // 128):
        at = slice(128 * pair, 128 * pair + 128)
        q2, k2, v2 = q[:, at], k[:, at], v[:, at]
        outs = []
        for which in range(2):
            mine = (lane < 64) if which == 0 else (lane >= 64)
            scores = dot_t(jnp.where(mine, q2, zero), k2) + bias_ref[2 * pair + which]
            top = jnp.max(scores, axis=-1, keepdims=True)
            shifted = jnp.exp(scores - top)
            probs = (shifted * (1.0 / jnp.sum(shifted, axis=-1, keepdims=True))).astype(BF)
            probs_ref[2 * pair + which] = probs
            outs.append(dot(probs, v2))
        ctx_ref[:, at] = jnp.where(lane < 64, outs[0], outs[1]).astype(BF)
    probs_ref.send()
    ctx_ref.send()
    part = dot(ctx_ref[...], wo_ref[...])
    rows = part.shape[0] // 2
    low, high = part[:rows], part[rows:]
    first = t_ref[0] == 0
    keep_ref[...] = jnp.where(first, low, high)
    give_ref[...] = jnp.where(first, high, low).astype(BF)


def attend(t, got, x, so, bias):
    cols, seq = got.shape[2], x.shape[1]
    heads = bias.shape[0]
    shape = jax.ShapeDtypeStruct
    return staged_call(
        attend_kernel,
        in_specs=[SCALAR] + [WHOLE] * 4,
        out_specs=[WHOLE] * 6,
        out_shape=[
            shape((seq // 2, 2 * cols), F32),
            shape((seq // 2, 2 * cols), BF),
            shape((seq, cols), BF),
            shape((3, seq, cols), BF),
            shape((heads, seq, seq), BF),
            shape((cols, 2 * cols), BF),
        ],
        **vmem(58, 4_000_000_000, 14_000_000),
    )(t, got, x, so, bias)


def attend_back_kernel(
    t_ref, own_ref, other_ref, wo_ref, qkv_ref, probs_ref, hits_ref, gain_ref, router_ref, two_ref, xt_ref, xot_ref, got_ref, s_ref,
    send_ref, g3_ref,
):
    own, other = own_ref[...], other_ref[...]
    first = t_ref[0] == 0
    ga = jnp.concatenate([jnp.where(first, own, other), jnp.where(first, other, own)], 0)
    q, k, v = qkv_ref[0], qkv_ref[1], qkv_ref[2]
    seq, cols = q.shape
    gctx = dot_t(ga, wo_ref[...]).astype(BF)
    lane = lax.broadcasted_iota(jnp.int32, (seq, 128), 1)
    low = lane < 64
    zero = jnp.zeros((seq, 128), BF)
    row8 = lax.broadcasted_iota(jnp.int32, (8, 2 * seq), 0)
    along = [lax.broadcasted_iota(jnp.int32, (seq, seq), axis) for axis in range(2)]
    flip = (along[0] + along[1] == seq - 1).astype(F32).astype(BF)
    diagonals = jnp.zeros((8, 2 * seq), F32)
    for pair in range(cols // 128):
        at = slice(128 * pair, 128 * pair + 128)
        q2, k2, v2, c2 = q[:, at], k[:, at], v[:, at], gctx[:, at]
        parts = []
        for which in range(2):
            mine = low if which == 0 else jnp.logical_not(low)
            probs = probs_ref[2 * pair + which]
            probs_f = probs.astype(F32)
            grad_probs = dot_t(jnp.where(mine, c2, zero), v2)
            inner = jnp.sum(probs_f * grad_probs, axis=-1, keepdims=True)
            ds = (probs_f * (grad_probs - inner)).astype(BF)
            parts.append((dot(ds, k2), dot(ds.T, q2), dot(probs.T, c2)))
            wide = jnp.concatenate([dot(flip, ds), jnp.zeros((seq, seq), F32)], 1)
            rolled = pltpu.roll(wide, 0, 1, stride=1, stride_axis=0)
            sums = jnp.sum(rolled, axis=0, keepdims=True)
            diagonals = jnp.where(row8 == 2 * pair + which, sums, diagonals)
        for c in range(3):
            g3_ref[c, :, at] = jnp.where(low, parts[0][c], parts[1][c]).astype(BF)
    g3_ref.send()
    gq, gk, gv = g3_ref[0], g3_ref[1], g3_ref[2]
    ga0, ga1 = ga[:, :cols], ga[:, cols:]
    one = dot(xt_ref[0], gq) + dot(xt_ref[1], gk)
    two = dot(xt_ref[0], gv) + dot(xot_ref[0], ga0) + dot(xot_ref[1], ga1)
    three = (
        dot(xt_ref[2], gq) + dot(xt_ref[3], gk) + dot(xt_ref[4], gv) + dot(xot_ref[2], ga0) + dot(xot_ref[3], ga1)
    )
    gain = jnp.zeros((128, gain_ref.shape[1]), F32)
    for g, (grad, weight) in enumerate(zip((one, two, three), groups(got_ref))):
        send_ref[:, 16 * g : 16 * g + 16, :] = grad.astype(BF).reshape(send_ref.shape[0], 16, cols)
        product = grad * weight.astype(F32)
        product = (product[:, :128] + product[:, 128:256] + product[:, 256:]).astype(BF)
        gain = gain + dot(product.T, s_ref[g])
    gain = jnp.sum(gain, axis=0, keepdims=True) / gain_ref[...]
    table = jnp.dot(diagonals, hits_ref[...], precision=PRECISE, preferred_element_type=F32)
    head_of = lax.broadcasted_iota(jnp.int32, table.shape, 1) // 64
    table = jnp.sum(
        jnp.where(head_of == lax.broadcasted_iota(jnp.int32, table.shape, 0), table, 0.0), axis=0, keepdims=True
    )
    gain_two = two_ref[...]
    row = lax.broadcasted_iota(jnp.int32, (8, cols), 0)
    tiny = jnp.zeros((8, cols), F32)
    for i, value in enumerate(
        (router_ref[...], gain[:, :cols], gain[:, cols:], gain_two[:, :cols], gain_two[:, cols:], table)
    ):
        tiny = jnp.where(row == i, value, tiny)
    send_ref[:, 48:56, :] = jnp.broadcast_to(tiny.astype(BF)[None], (send_ref.shape[0], 8, cols))


def attend_back(t, own, other, wo, qkv, probs, hits, gain, router, two, got, xt, xot, s):
    _, seq, cols = qkv.shape
    shape = jax.ShapeDtypeStruct
    return staged_call(
        attend_back_kernel,
        in_specs=[SCALAR] + [WHOLE] * 13,
        out_specs=[WHOLE] * 2,
        out_shape=[shape((got.shape[0], 56, cols), BF), shape((3, seq, cols), BF)],
        **vmem(58, 4_000_000_000, 16_000_000),
    )(t, own, other, wo, qkv, probs, hits, gain, router, two, xt, xot, got, s)


def iota(rows, columns, axis):
    return lax.broadcasted_iota(jnp.int32, (rows, columns), axis)


def split(value):
    high = value.astype(BF)
    return high, (value - high.astype(F32)).astype(BF)


def onehot(found):
    return jnp.where(found, 1.0, 0.0).astype(BF)


def ranks_along(ids, experts):
    rows = ids.shape[1]
    hits = iota(experts, rows, 0) == ids
    before = onehot(iota(rows, rows, 0) < iota(rows, rows, 1))
    return jnp.sum(dot(onehot(hits), before) * hits.astype(F32), axis=0, keepdims=True).astype(jnp.int32)


def ranks_down(ids, experts):
    rows = ids.shape[0]
    hits = iota(rows, experts, 1) == ids
    before = onehot(iota(rows, rows, 1) < iota(rows, rows, 0))
    return jnp.sum(dot(before, onehot(hits)) * hits.astype(F32), axis=1, keepdims=True).astype(jnp.int32)


def start_kernel(w_ref, wo_ref, qsel_ref, osel_ref, send_ref):
    peers, _, cols = send_ref.shape
    weights = sum(dot(qsel_ref[c], w_ref[:, c, :]) for c in range(3))
    for half in range(2):
        weights = weights + dot(osel_ref[half], wo_ref[:, half * cols : half * cols + cols])
    send_ref[...] = jnp.broadcast_to(weights.astype(BF)[None], send_ref.shape)


def start_send(w_rows, w_o, peers, shard, wo_rows):
    cols = w_rows.shape[2]
    qsel, osel = np.zeros((3, 48, shard), np.float32), np.zeros((2, 48, wo_rows), np.float32)
    for c in range(4):
        for i in range(shard):
            place = 8 * c + i if i < 8 else 32 + 4 * c + i - 8
            if c < 3:
                qsel[c, place, i] = 1
            else:
                osel[i % 2, place, i // 2] = 1
    return staged_call(
        start_kernel,
        in_specs=[WHOLE] * 4,
        out_specs=WHOLE,
        out_shape=jax.ShapeDtypeStruct((peers, 48, cols), BF),
        **vmem(58, 200_000_000, 3_500_000),
    )(w_rows, w_o, jnp.asarray(qsel, BF), jnp.asarray(osel, BF))


def prepare_kernel(
    first_ref, down_ref, along_ref, so_down_ref, offset_ref, seg_down_ref, seg_along_ref, x_ref, xt_ref, so_ref, s_ref, bias_ref
):
    first = first_ref[...]
    width, lanes = first.shape[1], x_ref.shape[2]
    for c in range(5):
        x_ref[c] = dot(first, onehot(iota(width, lanes, 1) == down_ref[:, c : c + 1])).astype(BF)
        sel = onehot(iota(lanes, width, 0) == along_ref[c : c + 1, :])
        xt_ref[c] = dot_t(sel, first).astype(BF)
        if c == 0:
            s_ref[0] = sel
            s_ref[1] = sel
        elif c == 1:
            s_ref[0] = s_ref[0] + sel
        elif c == 2:
            s_ref[2] = sel
        else:
            s_ref[2] = s_ref[2] + sel
    x_ref.send()
    xt_ref.send()
    s_ref.send()
    for c in range(4):
        so_ref[c] = onehot(iota(so_ref.shape[1], lanes, 1) == so_down_ref[:, c : c + 1])
    so_ref.send()
    heads, seq, _ = bias_ref.shape
    same = seg_down_ref[...] == seg_along_ref[...]
    for h in range(heads):
        wide = jnp.broadcast_to(offset_ref[h : h + 1, :], (seq, 2 * seq))
        wide = pltpu.roll(wide, seq + 1, 1, stride=1, stride_axis=0)
        bias_ref[h] = jnp.where(same, wide[:, :seq], MASKED)


def places(n_dp, shard, cols, wo_rows):
    d = np.arange(n_dp * shard)
    i, p = d % shard, d // shard
    down = np.full((n_dp * shard, 8), -1, np.int32)
    for c, (start, big) in enumerate([(0, False), (8, False), (-8, True), (-4, True), (0, True)]):
        down[:, c] = np.where((i >= 8) == big, p * 16 + i + start, -1)
    d = np.arange(cols)
    i, p = d % wo_rows, d // wo_rows
    so_down = np.full((cols, 8), -1, np.int32)
    for c in range(4):
        half, late = c % 2, c // 2 == 1
        place = 12 + 2 * (i - 4) + half if late else 8 + 2 * i + half
        so_down[:, c] = np.where((i >= 4) == late, p * 16 + place, -1)
    return down, so_down


def prepare(first_all, offset_bias, segments, down, so_down, n_dp):
    seq, width = first_all.shape
    cols, lanes, heads = so_down.shape[0], n_dp * 16, 6
    shape = jax.ShapeDtypeStruct
    return staged_call(
        prepare_kernel,
        in_specs=[WHOLE] * 7,
        out_specs=[WHOLE] * 5,
        out_shape=[
            shape((5, seq, lanes), BF),
            shape((5, lanes, seq), BF),
            shape((4, cols, lanes), BF),
            shape((3, lanes, width), BF),
            shape((heads, seq, seq), F32),
        ],
        **vmem(58, 4_000_000_000, 16_000_000),
    )(
        first_all,
        jnp.asarray(down),
        jnp.asarray(np.ascontiguousarray(down.T)),
        jnp.asarray(so_down),
        offset_bias,
        segments.reshape(seq, 1),
        segments,
    )


def dispatch_kernel(ids_ref, og_ref, tokens_ref, keep_ref, got_ref, gain_ref, send_ref, mid_ref, second_ref):
    mid = tokens_ref[...].astype(F32) + (keep_ref[...] + got_ref[...].astype(F32))
    scale = lax.rsqrt(jnp.mean(mid * mid, axis=-1, keepdims=True) + EPSILON)
    second = mid * scale * gain_ref[...]
    mid_ref[...] = mid
    second_ref[...] = second
    mid_ref.send()
    second_ref.send()
    ids = ids_ref[...]
    rows, cols = ids.shape[1], send_ref.shape[1]
    base = ids * 8 + ranks_along(ids, rows // 2) * 2
    row = iota(send_ref.shape[0], rows, 0)
    total = jnp.zeros(send_ref.shape, F32)
    for start, values in ((0, second.astype(BF)), (4, og_ref[...])):
        for half in range(2):
            at = slice(half * cols, half * cols + cols)
            total = total + dot(onehot(row == base + (start + half)), values[:, at])
    send_ref[...] = total.astype(BF)


def dispatch(ids_row, out_grad, tokens, keep, got, gain):
    rows, width = tokens.shape
    shape = jax.ShapeDtypeStruct
    return staged_call(
        dispatch_kernel,
        in_specs=[WHOLE] * 6,
        out_specs=[WHOLE] * 3,
        out_shape=[shape((rows * 4, width // 2), BF), shape((rows, width), F32), shape((rows, width), F32)],
        **vmem(58, 200_000_000, 2_000_000),
    )(ids_row, out_grad, tokens, keep, got, gain)


def between_kernel(
    ids_ref, ctx_ref, so_along_ref, second_ref, router_ref, xot_ref, selt_ref, gate_ref
):
    ctx = ctx_ref[...]
    lanes = xot_ref.shape[1]
    for c in range(4):
        sel = onehot(iota(lanes, ctx.shape[1], 0) == so_along_ref[c : c + 1, :])
        xot_ref[c] = dot_t(sel, ctx).astype(BF)
    xot_ref.send()
    ids = ids_ref[...]
    rows = ids.shape[0]
    experts = router_ref.shape[1]
    base = ids * 32 + ranks_down(ids, experts) * 3
    lane = iota(rows, selt_ref.shape[1], 1)
    for part in range(6):
        shift = part if part < 3 else part + 3
        selt_ref[rows * part : rows * part + rows, :] = onehot((lane == base + shift) | (lane == base + (16 + shift)))
    selt_ref.send()
    s_high, s_low = split(second_ref[...])
    r_high, r_low = split(router_ref[...])
    logits = dot(s_high, r_high) + (dot(s_low, r_high) + dot(s_high, r_low))
    shifted = jnp.exp(logits - jnp.max(logits, axis=-1, keepdims=True))
    hit = iota(rows, experts, 1) == ids
    gate_ref[...] = jnp.sum(jnp.where(hit, shifted, 0.0), axis=-1, keepdims=True) / jnp.sum(
        shifted, axis=-1, keepdims=True
    )


def between(ids, ctx, so_along, second, router, n_dp):
    rows = ids.shape[0]
    seq, cols = ctx.shape
    shape = jax.ShapeDtypeStruct
    return staged_call(
        between_kernel,
        in_specs=[WHOLE] * 5,
        out_specs=[WHOLE] * 3,
        out_shape=[
            shape((4, n_dp * 16, seq), BF),
            shape((6 * rows, rows * 16), BF),
            shape((rows, 1), F32),
        ],
        **vmem(58, 2_000_000_000, 8_000_000),
    )(ids, ctx, so_along, second, router)


def expert_kernel(
    me_ref, t_ref, own_ref, other_ref, router_ref, w1_ref, w2_ref, send_ref, arrived_ref, hidden_ref, pre_ref, ge_ref, *stages
):
    own, other = own_ref[...], other_ref[...]
    first = t_ref[0] == 0
    got = jnp.concatenate([jnp.where(first, own, other), jnp.where(first, other, own)], 0)
    count, cols = ge_ref.shape[0], got.shape[1]
    half = count // 2
    r = iota(count, 1, 0)
    pair = r & (half - 1)
    base = (pair & 1) * own.shape[0] + (pair >> 1) * 8 + (r >= half).astype(jnp.int32) * 2
    lane = iota(count, got.shape[0], 1)
    g = []
    for side in range(2):
        arrived_ref[:, cols * side : cols * side + cols] = dot(onehot(lane == base + side), got).astype(BF)
        g.append(dot(onehot(lane == base + (4 + side)), got))
    g = jnp.concatenate(g, 1)
    arrived = arrived_ref[...]
    r_high, r_low = split(router_ref[...])
    logits = dot(arrived, r_high) + dot(arrived, r_low)
    shifted = jnp.exp(logits - jnp.max(logits, axis=-1, keepdims=True))
    probs = shifted / jnp.sum(shifted, axis=-1, keepdims=True)
    mine = (iota(count, probs.shape[1], 1) == me_ref[0]).astype(F32)
    gate = jnp.sum(probs * mine, axis=-1, keepdims=True)
    ge = (gate * g).astype(BF)
    ge_ref[...] = ge
    width, hidden_cols = w1_ref.shape
    step = 256
    out = jnp.zeros((count, width), F32)
    back = jnp.zeros((count, width), F32)
    for f in range(0, hidden_cols, step):
        at = slice(f, f + step)
        w1, w2 = w1_ref[:, at], w2_ref[at, :]
        u = dot(arrived, w1)
        cdf = 0.5 + 0.5 * lax.erf(u * 0.7071067811865476)
        hidden = (u * cdf).astype(BF)
        slope = cdf + u * (jnp.exp(-0.5 * u * u) * 0.3989422804014327)
        grad = (dot_t(ge, w2) * slope).astype(BF)
        hidden_ref[:, at] = hidden
        pre_ref[:, at] = grad
        out = out + dot(hidden, w2)
        back = back + dot_t(grad, w1)
    hidden_ref.send()
    pre_ref.send()
    ge_ref.send()
    arrived_ref.send()
    grad_gate = jnp.sum(g * out, axis=-1, keepdims=True)
    grad_logits = grad_gate * gate * (mine - probs)
    l_high, l_low = split(grad_logits)
    back = back + (dot_t(l_high, r_high) + (dot_t(l_low, r_high) + dot_t(l_high, r_low)))
    t_high, t_low = split(grad_logits.T)
    router_part = dot(t_high, arrived) + dot(t_low, arrived)
    for side, stage in enumerate(stages):
        stage[...] = jnp.zeros(stage.shape, F32)
        for j in range(3):
            at = slice(256 * j + 128 * side, 256 * j + 128 * side + 128)
            for s in range(2):
                rows = slice(s * half, s * half + half)
                stage[pl.ds(s * 3 + j, half, stride=16), :] = out[rows, at]
                stage[pl.ds(6 + s * 3 + j, half, stride=16), :] = back[rows, at]
        for t in range(2):
            for r in range(2 - side):
                at = cols * t + 256 * r + 128 * side
                stage[pl.ds(12 + r + 16 * t, half // 2, stride=32), :] = router_part[:, at : at + 128]
        send_ref[:, 128 * side : 128 * side + 128] = stage[...].astype(BF)


def expert(me, t, own, other, router, w1, w2):
    count, width = own.shape[0] // 2, own.shape[1] * 2
    hidden = w1.shape[1]
    shape = jax.ShapeDtypeStruct
    return staged_call(
        expert_kernel,
        in_specs=[SCALAR] * 2 + [WHOLE] * 5,
        out_specs=[WHOLE] * 5,
        out_shape=[
            shape((count * 8, 256), BF),
            shape((count, width), BF),
            shape((count, hidden), BF),
            shape((count, hidden), BF),
            shape((count, width), BF),
        ],
        scratch_shapes=[pltpu.VMEM((count * 8, 128), F32)] * 2,
        **vmem(58, 3_000_000_000, 9_000_000),
    )(me, t, own, other, router, w1, w2)


def home_kernel(
    got_ref, selt_ref, mid_ref, gate_ref, gain_ref, og_ref, act_ref, gmid_ref, gattn_ref, router_ref, two_ref
):
    got = got_ref[...]
    rows = mid_ref.shape[0]
    sums = dot(selt_ref[...], got)
    out = jnp.concatenate([sums[rows * j : rows * j + rows] for j in range(3)], 1)
    grad_second = jnp.concatenate([sums[rows * j : rows * j + rows] for j in range(3, 6)], 1)
    lane = iota(16, got.shape[0], 1) & 15
    piece = dot(onehot(lane == iota(16, got.shape[0], 0) + 12), got)
    router_ref[...] = jnp.concatenate([piece[0:1], piece[1:2, :128]], 1)
    mid, gain = mid_ref[...], gain_ref[...]
    router_ref.send()
    act_ref[...] = (mid + gate_ref[...] * out).astype(BF)
    act_ref.send()
    scale = lax.rsqrt(jnp.mean(mid * mid, axis=-1, keepdims=True) + EPSILON)
    u = grad_second * gain
    two_ref[...] = jnp.sum(grad_second * mid * scale, axis=0, keepdims=True)
    spread = jnp.mean(u * mid, axis=-1, keepdims=True)
    gmid = og_ref[...].astype(F32) + (scale * u - scale * scale * scale * mid * spread)
    gmid_ref[...] = gmid
    gattn_ref[...] = gmid.astype(BF)


def home(got, selt, mid, gate, gain, out_grad):
    rows, width = mid.shape
    shape = jax.ShapeDtypeStruct
    return staged_call(
        home_kernel,
        in_specs=[WHOLE] * 6,
        out_specs=[WHOLE] * 5,
        out_shape=[
            shape((rows, width), BF),
            shape((rows, width), F32),
            shape((rows, width), BF),
            shape((1, width // 2), F32),
            shape((1, width), F32),
        ],
        **vmem(58, 500_000_000, 6_000_000),
    )(got, selt, mid, gate, gain, out_grad)


def per_device(
    tokens, gain_attn, rel_table, w_qkv, w_o, gain_moe, router, w_in, w_out, segments, offset_buckets, expert_ids, out_grad
):
    rows, width = tokens.shape
    shard, _, cols = w_qkv.shape
    wo_rows = w_o.shape[0]
    buckets, heads_all = rel_table.shape
    heads = cols // (width // heads_all)
    seq = segments.shape[1]
    n_dp = lax.axis_size("dp")
    n_t = lax.axis_size("tensor")
    t = lax.axis_index("tensor")
    me = lax.axis_index("dp")
    ids_row = expert_ids.reshape(1, rows)

    send_one = start_send(w_qkv, w_o, n_dp, shard, wo_rows)
    got_one = lax.all_to_all(send_one, "dp", 0, 0)

    xf = tokens.astype(F32)
    scale_one = lax.rsqrt(jnp.mean(xf * xf, axis=-1, keepdims=True) + EPSILON)
    first_rows = (xf * scale_one * gain_attn).astype(BF)
    first_all = lax.all_gather(first_rows, "tensor", axis=0, tiled=True)
    table_local = lax.dynamic_slice_in_dim(rel_table, t * heads, heads, 1)
    bucket_hits = (offset_buckets[:, None] == jnp.arange(buckets, dtype=jnp.int32)[None, :]).astype(F32)
    bucket_hits = jnp.pad(bucket_hits, ((0, 1), (0, 0)))
    offset_bias = jnp.einsum("bh,rb->hr", jnp.pad(table_local, ((0, 0), (0, 8 - heads))), bucket_hits, precision=PRECISE)
    hits_wide = jnp.tile(jnp.pad(bucket_hits, ((0, 0), (0, 64 - buckets))), (1, heads))
    down, so_down = places(n_dp, shard, cols, wo_rows)
    x, xt, so, back, bias = prepare(first_all, offset_bias, segments, down, so_down, n_dp)

    keep, give, context, qkv, probs, wo_full = attend(t.reshape(1), got_one, x, so, bias)
    gain_row = gain_moe[None]
    send_two, mid, second = dispatch(ids_row, out_grad, tokens, keep, swap(give), gain_row)

    got_two = lax.all_to_all(send_two.reshape(n_dp, 8, cols), "dp", 0, 0)
    so_along = jnp.asarray(np.ascontiguousarray(so_down.T))
    xot, selt, gate_home = between(expert_ids, context, so_along, second, router, n_dp)
    own, other = [y.reshape(n_dp * 8, cols) for y in (got_two, swap(got_two))]

    t1 = t.reshape(1)
    send_three, arrived, hidden, grad_pre, grad_expert = expert(me.reshape(1), t1, own, other, router, w_in[0], w_out[0])

    got_three = lax.all_to_all(send_three.reshape(n_dp * n_t, 16, 256), ALL, 0, 0).reshape(n_dp * n_t * 16, 256)
    grad_w_out = dot(hidden, grad_expert, ((0,), (0,)))
    grad_w_in = dot(arrived, grad_pre, ((0,), (0,)))
    activations, grad_mid, grad_own, router_piece, gain_two = home(got_three, selt, mid, gate_home, gain_row, out_grad)

    send_four, grad3 = attend_back(
        t1, grad_own, swap(grad_own), wo_full, qkv, probs, hits_wide, gain_attn[None], router_piece, gain_two, got_one, xt, xot, back
    )

    got_four = lax.all_to_all(send_four, "dp", 0, 0)
    one, two, three = [got_one[:, 16 * g : 16 * g + 16].reshape(n_dp * 16, cols) for g in range(3)]
    sel_t = [(jnp.arange(n_dp * 16, dtype=jnp.int32)[:, None] == jnp.asarray(down[:, c])[None, :]).astype(BF) for c in range(5)]
    spread_q, spread_k, spread_v = dot_t(grad3[0], one), dot_t(grad3[1], one), dot_t(grad3[2], two)
    last = [dot_t(grad3[c], three).astype(BF) for c in range(3)]
    grad_first = dot(spread_q.astype(BF), sel_t[0]) + dot(spread_k.astype(BF), sel_t[1]) + dot(spread_v.astype(BF), sel_t[0])
    grad_first = grad_first + sum(dot(last[c], sel_t[2 + c]) for c in range(3))
    keep_first = lax.dynamic_slice_in_dim(grad_first, t * rows, rows, 0)
    give_first = lax.dynamic_slice_in_dim(grad_first, (1 - t) * rows, rows, 0).astype(BF)
    grad_first_own = keep_first + swap(give_first).astype(F32)
    u1 = grad_first_own * gain_attn
    spread_one = jnp.mean(u1 * xf, axis=-1, keepdims=True)
    input_grad = (grad_mid + (scale_one * u1 - scale_one * scale_one * scale_one * xf * spread_one)).astype(BF)

    tiny_got = got_four[:, 48:54].astype(F32)
    router_half = tiny_got[:, 0]
    sums = jnp.sum(tiny_got[:, 1:], axis=0)
    packed = jnp.concatenate([router_half, sums], 0)
    other = swap(packed)
    low, high = jnp.where(t == 0, packed, other), jnp.where(t == 0, other, packed)
    grad_router = jnp.concatenate([low[:n_dp], high[:n_dp]], 1).T
    total = (packed[n_dp:] + other[n_dp:]).reshape(-1)
    gain_one_sum, gain_two_sum = total[:width], total[width : 2 * width]
    tables = [y[-1].reshape(heads, 64)[:, :buckets] for y in (low, high)]
    table_sum = jnp.concatenate(tables, 0).T
    weights = jnp.sum(got_four[:, :48].astype(F32), axis=0)
    full = [jnp.concatenate([weights[8 * c : 8 * c + 8], weights[32 + 4 * c : 36 + 4 * c]], 0) for c in range(4)]
    grad_qkv_shard = jnp.stack(full[:3], 1)
    grad_o_shard = full[3].reshape(wo_rows, width)
    return (
        activations,
        input_grad,
        gain_one_sum,
        table_sum,
        grad_qkv_shard,
        grad_o_shard,
        gain_two_sum,
        grad_router,
        grad_w_in[None],
        grad_w_out[None],
    )


def solution(mesh):
    in_specs = (
        P(("dp", "tensor"), None),
        P(),
        P(),
        P("dp", None, "tensor"),
        P(("tensor", "dp"), None),
        P(),
        P(),
        P("dp", None, "tensor"),
        P("dp", "tensor", None),
        P("dp", None),
        P(),
        P(("dp", "tensor"), None),
        P(("dp", "tensor"), None),
    )
    out_specs = (
        P(("dp", "tensor"), None),
        P(("dp", "tensor"), None),
        P(),
        P(),
        P("dp", None, "tensor"),
        P(("tensor", "dp"), None),
        P(),
        P(),
        P("dp", None, "tensor"),
        P("dp", "tensor", None),
    )
    return jax.shard_map(per_device, mesh=mesh, in_specs=in_specs, out_specs=out_specs, check_vma=False)
```

```python
import jax
import jax.numpy as jnp
import numpy as np
from jax import lax
from jax.experimental import pallas as pl
from jax.experimental.pallas import tpu as pltpu
from jax.sharding import PartitionSpec as P

PRECISE = lax.Precision.HIGHEST
EPSILON = 1e-06
MASKED = -1000000000.0
BF = jnp.bfloat16
F32 = jnp.float32
ALL = ("dp", "tensor")


def swap(rows):
    return lax.ppermute(rows, "tensor", [(0, 1), (1, 0)])


def dot(left, right, dims=((1,), (0,)), precision=None):
    return lax.dot_general(left, right, (dims, ((), ())), precision=precision, preferred_element_type=F32)


def dot_t(left, right):
    return dot(left, right, ((1,), (1,)))


def vmem(limit_mb, flops, moved):
    return dict(
        compiler_params=pltpu.CompilerParams(vmem_limit_bytes=limit_mb * 1024 * 1024),
        cost_estimate=pl.CostEstimate(flops=flops, bytes_accessed=moved, transcendentals=0),
    )


WHOLE = "whole"
HERE = "here"
SCALAR = pl.BlockSpec(memory_space=pltpu.SMEM)


class Arriving:
    def __init__(self, buffer, move):
        self.buffer, self.move, self.shape = buffer, move, buffer.shape

    def __getitem__(self, index):
        if self.move is not None:
            self.move.wait()
            self.move = None
        return self.buffer[index]


class Leaving:
    def __init__(self, buffer, out, sem):
        self.buffer, self.out, self.sem = buffer, out, sem
        self.shape, self.move, self.sent = buffer.shape, None, False

    def __getitem__(self, index):
        return self.buffer[index]

    def __setitem__(self, index, value):
        self.buffer[index] = value

    def send(self):
        if not self.sent:
            self.move = pltpu.make_async_copy(self.buffer, self.out, self.sem)
            self.move.start()
            self.sent = True


def staged_call(body, in_specs, out_specs, out_shape, scratch_shapes=(), **params):
    several = isinstance(out_shape, list)
    results, kinds = (out_shape, out_specs) if several else ([out_shape], [out_specs])
    moved = [i for i, kind in enumerate(in_specs) if kind is WHOLE]
    left = [i for i, kind in enumerate(kinds) if kind is WHOLE]

    def kernel(*refs):
        refs = list(refs)
        ins, outs = refs[: len(in_specs)], refs[len(in_specs) : len(in_specs) + len(results)]
        rest = refs[len(in_specs) + len(results) :]
        in_buffers, rest = rest[: len(moved)], rest[len(moved) :]
        out_buffers, rest = rest[: len(left)], rest[len(left) :]
        in_sems, out_sems, extra = rest[0], rest[1], rest[2:]
        for n, (i, buffer) in enumerate(zip(moved, in_buffers)):
            move = pltpu.make_async_copy(ins[i], buffer, in_sems.at[n])
            move.start()
            ins[i] = Arriving(buffer, move)
        for n, (i, buffer) in enumerate(zip(left, out_buffers)):
            outs[i] = Leaving(buffer, outs[i], out_sems.at[n])
        body(*ins, *outs, *extra)
        for i in moved:
            if ins[i].move is not None:
                ins[i].move.wait()
        for i in left:
            outs[i].send()
        for i in left:
            if outs[i].move is not None:
                outs[i].move.wait()

    def call(*args):
        space = {WHOLE: pltpu.HBM, HERE: pltpu.VMEM}
        place = lambda kind: pl.BlockSpec(memory_space=space[kind]) if kind in (WHOLE, HERE) else kind
        placed = [space[kind](r.shape, r.dtype) for kind, r in zip(kinds, results, strict=True)]
        args = [
            pltpu.with_memory_space_constraint(a, space[kind]) if kind in (WHOLE, HERE) else a
            for kind, a in zip(in_specs, args, strict=True)
        ]
        return pl.pallas_call(
            kernel,
            in_specs=[place(kind) for kind in in_specs],
            out_specs=[place(kind) for kind in kinds] if several else place(kinds[0]),
            out_shape=placed if several else placed[0],
            scratch_shapes=[pltpu.VMEM(args[i].shape, args[i].dtype) for i in moved]
            + [pltpu.VMEM(results[i].shape, results[i].dtype) for i in left]
            + [pltpu.SemaphoreType.DMA((max(1, len(moved)),)), pltpu.SemaphoreType.DMA((max(1, len(left)),))]
            + list(scratch_shapes),
            **params,
        )(*args)

    return call


def send(*refs):
    for ref in refs:
        if isinstance(ref, Leaving):
            ref.send()


def groups(ref):
    return [ref[:, 16 * g : 16 * g + 16, :].reshape(ref.shape[0] * 16, ref.shape[2]) for g in range(3)]


def attend_kernel(t_ref, got_ref, x_ref, so_ref, bias_ref, keep_ref, give_ref, ctx_ref, qkv_ref, probs_ref, wo_ref):
    one, two, three = groups(got_ref)
    q = (dot(x_ref[0], one) + dot(x_ref[2], three)).astype(BF)
    k = (dot(x_ref[1], one) + dot(x_ref[3], three)).astype(BF)
    v = (dot(x_ref[0], two) + dot(x_ref[4], three)).astype(BF)
    qkv_ref[0], qkv_ref[1], qkv_ref[2] = q, k, v
    send(qkv_ref)
    cols = q.shape[1]
    for half in range(2):
        wo_ref[:, half * cols : half * cols + cols] = (
            dot(so_ref[half], two) + dot(so_ref[2 + half], three)
        ).astype(BF)
    send(wo_ref)
    lane = lax.broadcasted_iota(jnp.int32, (q.shape[0], 128), 1)
    zero = jnp.zeros((q.shape[0], 128), BF)
    for pair in range(cols // 128):
        at = slice(128 * pair, 128 * pair + 128)
        q2, k2, v2 = q[:, at], k[:, at], v[:, at]
        outs = []
        for which in range(2):
            mine = (lane < 64) if which == 0 else (lane >= 64)
            scores = dot_t(jnp.where(mine, q2, zero), k2) + bias_ref[2 * pair + which]
            top = jnp.max(scores, axis=-1, keepdims=True)
            shifted = jnp.exp(scores - top)
            probs = (shifted * (1.0 / jnp.sum(shifted, axis=-1, keepdims=True))).astype(BF)
            probs_ref[2 * pair + which] = probs
            outs.append(dot(probs, v2))
        ctx_ref[:, at] = jnp.where(lane < 64, outs[0], outs[1]).astype(BF)
    send(probs_ref)
    send(ctx_ref)
    part = dot(ctx_ref[...], wo_ref[...])
    rows = part.shape[0] // 2
    low, high = part[:rows], part[rows:]
    first = t_ref[0] == 0
    keep_ref[...] = jnp.where(first, low, high)
    give_ref[...] = jnp.where(first, high, low).astype(BF)


def attend(t, got, x, so, bias):
    cols, seq = got.shape[2], x.shape[1]
    heads = bias.shape[0]
    shape = jax.ShapeDtypeStruct
    return staged_call(
        attend_kernel,
        in_specs=[SCALAR, HERE] + [WHOLE] * 3,
        out_specs=[HERE] * 2 + [WHOLE] * 4,
        out_shape=[
            shape((seq // 2, 2 * cols), F32),
            shape((seq // 2, 2 * cols), BF),
            shape((seq, cols), BF),
            shape((3, seq, cols), BF),
            shape((heads, seq, seq), BF),
            shape((cols, 2 * cols), BF),
        ],
        **vmem(34, 4_000_000_000, 14_000_000),
    )(t, got, x, so, bias)


def attend_back_kernel(
    t_ref, own_ref, other_ref, wo_ref, qkv_ref, probs_ref, hits_ref, gain_ref, router_ref, two_ref, xt_ref, xot_ref, got_ref, s_ref,
    send_ref, g3_ref, sems,
):
    own, other = own_ref[...], other_ref[...]
    first = t_ref[0] == 0
    ga = jnp.concatenate([jnp.where(first, own, other), jnp.where(first, other, own)], 0)
    q, k, v = qkv_ref[0], qkv_ref[1], qkv_ref[2]
    seq, cols = q.shape
    gctx = dot_t(ga, wo_ref[...]).astype(BF)
    lane = lax.broadcasted_iota(jnp.int32, (seq, 128), 1)
    low = lane < 64
    zero = jnp.zeros((seq, 128), BF)
    row8 = lax.broadcasted_iota(jnp.int32, (8, 2 * seq), 0)
    along = [lax.broadcasted_iota(jnp.int32, (seq, seq), axis) for axis in range(2)]
    flip = (along[0] + along[1] == seq - 1).astype(F32).astype(BF)
    diagonals = jnp.zeros((8, 2 * seq), F32)
    for pair in range(cols // 128):
        at = slice(128 * pair, 128 * pair + 128)
        q2, k2, v2, c2 = q[:, at], k[:, at], v[:, at], gctx[:, at]
        parts = []
        for which in range(2):
            mine = low if which == 0 else jnp.logical_not(low)
            probs = probs_ref[2 * pair + which]
            probs_f = probs.astype(F32)
            grad_probs = dot_t(jnp.where(mine, c2, zero), v2)
            inner = jnp.sum(probs_f * grad_probs, axis=-1, keepdims=True)
            ds = (probs_f * (grad_probs - inner)).astype(BF)
            parts.append((dot(ds, k2), dot(ds.T, q2), dot(probs.T, c2)))
            wide = jnp.concatenate([dot(flip, ds), jnp.zeros((seq, seq), F32)], 1)
            rolled = pltpu.roll(wide, 0, 1, stride=1, stride_axis=0)
            sums = jnp.sum(rolled, axis=0, keepdims=True)
            diagonals = jnp.where(row8 == 2 * pair + which, sums, diagonals)
        for c in range(3):
            g3_ref[c, :, at] = jnp.where(low, parts[0][c], parts[1][c]).astype(BF)
    send(g3_ref)
    outgoing = []

    def leave(rows, number):
        outgoing.append(
            pltpu.make_async_copy(send_ref.buffer.at[:, rows, :], send_ref.out.at[:, rows, :], sems.at[number])
        )
        outgoing[-1].start()

    gq, gk, gv = g3_ref[0], g3_ref[1], g3_ref[2]
    ga0, ga1 = ga[:, :cols], ga[:, cols:]
    one = dot(xt_ref[0], gq) + dot(xt_ref[1], gk)
    two = dot(xt_ref[0], gv) + dot(xot_ref[0], ga0) + dot(xot_ref[1], ga1)
    three = (
        dot(xt_ref[2], gq) + dot(xt_ref[3], gk) + dot(xt_ref[4], gv) + dot(xot_ref[2], ga0) + dot(xot_ref[3], ga1)
    )
    gain = jnp.zeros((128, gain_ref.shape[0]), F32)
    for g, (grad, weight) in enumerate(zip((one, two, three), groups(got_ref))):
        send_ref[:, 16 * g : 16 * g + 16, :] = grad.astype(BF).reshape(send_ref.shape[0], 16, cols)
        leave(slice(16 * g, 16 * g + 16), g)
        product = grad * weight.astype(F32)
        product = (product[:, :128] + product[:, 128:256] + product[:, 256:]).astype(BF)
        gain = gain + dot(product.T, s_ref[g])
    gain = jnp.sum(gain, axis=0, keepdims=True) / gain_ref[...].reshape(1, gain.shape[1])
    hits = ((iota(cols, 2 * seq, 0) & 63) == hits_ref[...]).astype(F32)
    table = dot(diagonals, hits, ((1,), (1,)), PRECISE)
    head_of = lax.broadcasted_iota(jnp.int32, table.shape, 1) // 64
    table = jnp.sum(
        jnp.where(head_of == lax.broadcasted_iota(jnp.int32, table.shape, 0), table, 0.0), axis=0, keepdims=True
    )
    gain_two = two_ref[...]
    row = lax.broadcasted_iota(jnp.int32, (8, cols), 0)
    tiny = jnp.zeros((8, cols), F32)
    for i, value in enumerate(
        (router_ref[...], gain[:, :cols], gain[:, cols:], gain_two[:, :cols], gain_two[:, cols:], table)
    ):
        tiny = jnp.where(row == i, value, tiny)
    send_ref[:, 48:56, :] = jnp.broadcast_to(tiny.astype(BF)[None], (send_ref.shape[0], 8, cols))
    leave(slice(48, 56), 3)
    send_ref.sent = True
    for move in outgoing:
        move.wait()


def attend_back(t, own, other, wo, qkv, probs, hits, gain, router, two, got, xt, xot, s):
    _, seq, cols = qkv.shape
    shape = jax.ShapeDtypeStruct
    return staged_call(
        attend_back_kernel,
        in_specs=[SCALAR, HERE, HERE] + [WHOLE] * 5 + [HERE] * 2 + [WHOLE] * 4,
        out_specs=[WHOLE] * 2,
        out_shape=[shape((got.shape[0], 56, cols), BF), shape((3, seq, cols), BF)],
        scratch_shapes=[pltpu.SemaphoreType.DMA((4,))],
        **vmem(34, 4_000_000_000, 16_000_000),
    )(t, own, other, wo, qkv, probs, hits, gain, router, two, xt, xot, got, s)


def iota(rows, columns, axis):
    return lax.broadcasted_iota(jnp.int32, (rows, columns), axis)


def split(value):
    high = value.astype(BF)
    return high, (value - high.astype(F32)).astype(BF)


def onehot(found):
    return jnp.where(found, 1.0, 0.0).astype(BF)


def ranks_along(ids, experts):
    rows = ids.shape[1]
    hits = iota(experts, rows, 0) == ids
    before = onehot(iota(rows, rows, 0) < iota(rows, rows, 1))
    return jnp.sum(dot(onehot(hits), before) * hits.astype(F32), axis=0, keepdims=True).astype(jnp.int32)


def ranks_down(ids, experts):
    rows = ids.shape[0]
    hits = iota(rows, experts, 1) == ids
    before = onehot(iota(rows, rows, 1) < iota(rows, rows, 0))
    return jnp.sum(dot(before, onehot(hits)) * hits.astype(F32), axis=1, keepdims=True).astype(jnp.int32)


def start_kernel(w_ref, wo_ref, qsel_ref, osel_ref, send_ref):
    peers, _, cols = send_ref.shape
    weights = sum(dot(qsel_ref[c], w_ref[:, c, :]) for c in range(3))
    for half in range(2):
        weights = weights + dot(osel_ref[half], wo_ref[:, half * cols : half * cols + cols])
    send_ref[...] = jnp.broadcast_to(weights.astype(BF)[None], send_ref.shape)


def start_send(w_rows, w_o, peers, shard, wo_rows):
    cols = w_rows.shape[2]
    qsel, osel = np.zeros((3, 48, shard), np.float32), np.zeros((2, 48, wo_rows), np.float32)
    for c in range(4):
        for i in range(shard):
            place = 8 * c + i if i < 8 else 32 + 4 * c + i - 8
            if c < 3:
                qsel[c, place, i] = 1
            else:
                osel[i % 2, place, i // 2] = 1
    return staged_call(
        start_kernel,
        in_specs=[WHOLE] * 4,
        out_specs=WHOLE,
        out_shape=jax.ShapeDtypeStruct((peers, 48, cols), BF),
        **vmem(34, 200_000_000, 3_500_000),
    )(w_rows, w_o, jnp.asarray(qsel, BF), jnp.asarray(osel, BF))


def prepare_kernel(
    first_ref, down_ref, along_ref, so_down_ref, offset_ref, seg_down_ref, seg_along_ref, x_ref, xt_ref, so_ref, s_ref, bias_ref
):
    first = first_ref[...]
    width, lanes = first.shape[1], x_ref.shape[2]
    for c in range(5):
        x_ref[c] = dot(first, onehot(iota(width, lanes, 1) == down_ref[:, c : c + 1])).astype(BF)
        sel = onehot(iota(lanes, width, 0) == along_ref[c : c + 1, :])
        xt_ref[c] = dot_t(sel, first).astype(BF)
        if c == 0:
            s_ref[0] = sel
            s_ref[1] = sel
        elif c == 1:
            s_ref[0] = s_ref[0] + sel
        elif c == 2:
            s_ref[2] = sel
        else:
            s_ref[2] = s_ref[2] + sel
    send(x_ref)
    send(xt_ref)
    send(s_ref)
    for c in range(4):
        so_ref[c] = onehot(iota(so_ref.shape[1], lanes, 1) == so_down_ref[:, c : c + 1])
    send(so_ref)
    heads, seq, _ = bias_ref.shape
    same = seg_down_ref[...] == seg_along_ref[...]
    for h in range(heads):
        wide = jnp.broadcast_to(offset_ref[h : h + 1, :], (seq, 2 * seq))
        wide = pltpu.roll(wide, seq + 1, 1, stride=1, stride_axis=0)
        bias_ref[h] = jnp.where(same, wide[:, :seq], MASKED)


def places(n_dp, shard, cols, wo_rows):
    d = np.arange(n_dp * shard)
    i, p = d % shard, d // shard
    down = np.full((n_dp * shard, 8), -1, np.int32)
    for c, (start, big) in enumerate([(0, False), (8, False), (-8, True), (-4, True), (0, True)]):
        down[:, c] = np.where((i >= 8) == big, p * 16 + i + start, -1)
    d = np.arange(cols)
    i, p = d % wo_rows, d // wo_rows
    so_down = np.full((cols, 8), -1, np.int32)
    for c in range(4):
        half, late = c % 2, c // 2 == 1
        place = 12 + 2 * (i - 4) + half if late else 8 + 2 * i + half
        so_down[:, c] = np.where((i >= 4) == late, p * 16 + place, -1)
    return down, so_down


def prepare(first_all, offset_bias, segments, down, so_down, n_dp):
    seq, width = first_all.shape
    cols, lanes, heads = so_down.shape[0], n_dp * 16, 6
    shape = jax.ShapeDtypeStruct
    return staged_call(
        prepare_kernel,
        in_specs=[WHOLE] * 7,
        out_specs=[WHOLE] * 5,
        out_shape=[
            shape((5, seq, lanes), BF),
            shape((5, lanes, seq), BF),
            shape((4, cols, lanes), BF),
            shape((3, lanes, width), BF),
            shape((heads, seq, seq), F32),
        ],
        **vmem(34, 4_000_000_000, 16_000_000),
    )(
        first_all,
        jnp.asarray(down),
        jnp.asarray(np.ascontiguousarray(down.T)),
        jnp.asarray(so_down),
        offset_bias,
        segments.reshape(seq, 1),
        segments,
    )


def dispatch_kernel(ids_ref, og_ref, tokens_ref, keep_ref, got_ref, gain_ref, send_ref, mid_ref, second_ref):
    mid = tokens_ref[...].astype(F32) + (keep_ref[...] + got_ref[...].astype(F32))
    scale = lax.rsqrt(jnp.mean(mid * mid, axis=-1, keepdims=True) + EPSILON)
    second = mid * scale * gain_ref[...].reshape(1, mid.shape[1])
    mid_ref[...] = mid
    second_ref[...] = second
    send(mid_ref)
    send(second_ref)
    ids = ids_ref[...]
    rows, cols = ids.shape[1], send_ref.shape[1]
    base = ids * 8 + ranks_along(ids, rows // 2) * 2
    row = iota(send_ref.shape[0], rows, 0)
    total = jnp.zeros(send_ref.shape, F32)
    for start, values in ((0, second.astype(BF)), (4, og_ref[...])):
        for half in range(2):
            at = slice(half * cols, half * cols + cols)
            total = total + dot(onehot(row == base + (start + half)), values[:, at])
    send_ref[...] = total.astype(BF)


def dispatch(ids_row, out_grad, tokens, keep, got, gain):
    rows, width = tokens.shape
    shape = jax.ShapeDtypeStruct
    return staged_call(
        dispatch_kernel,
        in_specs=[WHOLE] * 3 + [HERE, HERE, WHOLE],
        out_specs=[WHOLE] * 3,
        out_shape=[shape((rows * 4, width // 2), BF), shape((rows, width), F32), shape((rows, width), F32)],
        **vmem(16, 200_000_000, 2_000_000),
    )(ids_row, out_grad, tokens, keep, got, gain)


def between_kernel(
    ids_ref, ctx_ref, so_along_ref, second_ref, router_ref, xot_ref, selt_ref, gate_ref
):
    ctx = ctx_ref[...]
    lanes = xot_ref.shape[1]
    for c in range(4):
        sel = onehot(iota(lanes, ctx.shape[1], 0) == so_along_ref[c : c + 1, :])
        xot_ref[c] = dot_t(sel, ctx).astype(BF)
    send(xot_ref)
    ids = ids_ref[...]
    rows = ids.shape[0]
    experts = router_ref.shape[0]
    base = ids * 32 + ranks_down(ids, experts) * 3
    lane = iota(rows, selt_ref.shape[1], 1)
    for part in range(6):
        shift = part if part < 3 else part + 3
        selt_ref[rows * part : rows * part + rows, :] = onehot((lane == base + shift) | (lane == base + (16 + shift)))
    send(selt_ref)
    s_high, s_low = split(second_ref[...])
    r_high, r_low = split(router_ref[...])
    logits = dot_t(s_high, r_high) + (dot_t(s_low, r_high) + dot_t(s_high, r_low))
    shifted = jnp.exp(logits - jnp.max(logits, axis=-1, keepdims=True))
    hit = iota(rows, experts, 1) == ids
    gate_ref[...] = jnp.sum(jnp.where(hit, shifted, 0.0), axis=-1, keepdims=True) / jnp.sum(
        shifted, axis=-1, keepdims=True
    )


def between(ids, ctx, so_along, second, router, n_dp):
    rows = ids.shape[0]
    seq, cols = ctx.shape
    shape = jax.ShapeDtypeStruct
    return staged_call(
        between_kernel,
        in_specs=[WHOLE] * 5,
        out_specs=[WHOLE] * 3,
        out_shape=[
            shape((4, n_dp * 16, seq), BF),
            shape((6 * rows, rows * 16), BF),
            shape((rows, 1), F32),
        ],
        **vmem(20, 2_000_000_000, 8_000_000),
    )(ids, ctx, so_along, second, router)


def expert_kernel(
    me_ref, t_ref, own_ref, other_ref, router_ref, w1_ref, w2_ref, send_ref, arrived_ref, hidden_ref, pre_ref, ge_ref, *stages
):
    own, other = own_ref[...], other_ref[...]
    first = t_ref[0] == 0
    got = jnp.concatenate([jnp.where(first, own, other), jnp.where(first, other, own)], 0)
    count, cols = ge_ref.shape[0], got.shape[1]
    half = count // 2
    r = iota(count, 1, 0)
    pair = r & (half - 1)
    base = (pair & 1) * own.shape[0] + (pair >> 1) * 8 + (r >= half).astype(jnp.int32) * 2
    lane = iota(count, got.shape[0], 1)
    g = []
    for side in range(2):
        arrived_ref[:, cols * side : cols * side + cols] = dot(onehot(lane == base + side), got).astype(BF)
        g.append(dot(onehot(lane == base + (4 + side)), got))
    g = jnp.concatenate(g, 1)
    arrived = arrived_ref[...]
    r_high, r_low = split(router_ref[...])
    logits = dot_t(arrived, r_high) + dot_t(arrived, r_low)
    shifted = jnp.exp(logits - jnp.max(logits, axis=-1, keepdims=True))
    probs = shifted / jnp.sum(shifted, axis=-1, keepdims=True)
    mine = (iota(count, probs.shape[1], 1) == me_ref[0]).astype(F32)
    gate = jnp.sum(probs * mine, axis=-1, keepdims=True)
    ge = (gate * g).astype(BF)
    ge_ref[...] = ge
    width, hidden_cols = w1_ref.shape
    step = 256
    out = jnp.zeros((count, width), F32)
    back = jnp.zeros((count, width), F32)
    for f in range(0, hidden_cols, step):
        at = slice(f, f + step)
        w1, w2 = w1_ref[:, at], w2_ref[at, :]
        u = dot(arrived, w1)
        cdf = 0.5 + 0.5 * lax.erf(u * 0.7071067811865476)
        hidden = (u * cdf).astype(BF)
        slope = cdf + u * (jnp.exp(-0.5 * u * u) * 0.3989422804014327)
        grad = (dot_t(ge, w2) * slope).astype(BF)
        hidden_ref[:, at] = hidden
        pre_ref[:, at] = grad
        out = out + dot(hidden, w2)
        back = back + dot_t(grad, w1)
    send(hidden_ref)
    send(pre_ref)
    send(ge_ref)
    send(arrived_ref)
    grad_gate = jnp.sum(g * out, axis=-1, keepdims=True)
    grad_logits = grad_gate * gate * (mine - probs)
    l_high, l_low = split(grad_logits)
    back = back + (dot(l_high, r_high) + (dot(l_low, r_high) + dot(l_high, r_low)))
    t_high, t_low = split(grad_logits.T)
    router_part = dot(t_high, arrived) + dot(t_low, arrived)
    for side, stage in enumerate(stages):
        stage[...] = jnp.zeros(stage.shape, F32)
        for j in range(3):
            at = slice(256 * j + 128 * side, 256 * j + 128 * side + 128)
            for s in range(2):
                rows = slice(s * half, s * half + half)
                stage[pl.ds(s * 3 + j, half, stride=16), :] = out[rows, at]
                stage[pl.ds(6 + s * 3 + j, half, stride=16), :] = back[rows, at]
        for t in range(2):
            for r in range(2 - side):
                at = cols * t + 256 * r + 128 * side
                stage[pl.ds(12 + r + 16 * t, half // 2, stride=32), :] = router_part[:, at : at + 128]
        send_ref[:, 128 * side : 128 * side + 128] = stage[...].astype(BF)


def expert(me, t, own, other, router, w1, w2):
    count, width = own.shape[0] // 2, own.shape[1] * 2
    hidden = w1.shape[1]
    shape = jax.ShapeDtypeStruct
    return staged_call(
        expert_kernel,
        in_specs=[SCALAR] * 2 + [HERE] * 2 + [WHOLE] * 3,
        out_specs=[WHOLE] * 5,
        out_shape=[
            shape((count * 8, 256), BF),
            shape((count, width), BF),
            shape((count, hidden), BF),
            shape((count, hidden), BF),
            shape((count, width), BF),
        ],
        scratch_shapes=[pltpu.VMEM((count * 8, 128), F32)] * 2,
        **vmem(34, 3_000_000_000, 9_000_000),
    )(me, t, own, other, router, w1, w2)


def home_kernel(
    got_ref, selt_ref, mid_ref, gate_ref, gain_ref, og_ref, act_ref, gmid_ref, gattn_ref, router_ref, two_ref
):
    got = got_ref[...]
    rows = mid_ref.shape[0]
    sums = dot(selt_ref[...], got)
    out = jnp.concatenate([sums[rows * j : rows * j + rows] for j in range(3)], 1)
    grad_second = jnp.concatenate([sums[rows * j : rows * j + rows] for j in range(3, 6)], 1)
    lane = iota(16, got.shape[0], 1) & 15
    piece = dot(onehot(lane == iota(16, got.shape[0], 0) + 12), got)
    router_ref[...] = jnp.concatenate([piece[0:1], piece[1:2, :128]], 1)
    mid = mid_ref[...]
    gain = gain_ref[...].reshape(1, mid.shape[1])
    send(router_ref)
    act_ref[...] = (mid + gate_ref[...] * out).astype(BF)
    send(act_ref)
    scale = lax.rsqrt(jnp.mean(mid * mid, axis=-1, keepdims=True) + EPSILON)
    u = grad_second * gain
    two_ref[...] = jnp.sum(grad_second * mid * scale, axis=0, keepdims=True)
    spread = jnp.mean(u * mid, axis=-1, keepdims=True)
    gmid = og_ref[...].astype(F32) + (scale * u - scale * scale * scale * mid * spread)
    gmid_ref[...] = gmid
    gattn_ref[...] = gmid.astype(BF)


def home(got, selt, mid, gate, gain, out_grad):
    rows, width = mid.shape
    shape = jax.ShapeDtypeStruct
    return staged_call(
        home_kernel,
        in_specs=[HERE] + [WHOLE] * 5,
        out_specs=[WHOLE] * 2 + [HERE] * 3,
        out_shape=[
            shape((rows, width), BF),
            shape((rows, width), F32),
            shape((rows, width), BF),
            shape((1, width // 2), F32),
            shape((1, width), F32),
        ],
        **vmem(16, 500_000_000, 6_000_000),
    )(got, selt, mid, gate, gain, out_grad)


def first_back_kernel(t_ref, g3_ref, got_ref, along_ref, keep_ref, give_ref):
    one, two, three = groups(got_ref)
    g = [g3_ref[c] for c in range(3)]
    lanes, width = one.shape[0], along_ref.shape[1]
    pieces = [dot_t(g[0], one), dot_t(g[1], one), dot_t(g[0], three), dot_t(g[1], three), dot_t(g[2], three)]
    pieces = [p.astype(BF) for p in pieces]
    total = jnp.zeros((g[0].shape[0], width), F32)
    for c in range(5):
        sel = onehot(iota(lanes, width, 0) == along_ref[c : c + 1, :])
        total = total + dot(pieces[c], sel)
        if c == 0:
            total = total + dot(dot_t(g[2], two).astype(BF), sel)
    rows = total.shape[0] // 2
    low, high = total[:rows], total[rows:]
    first = t_ref[0] == 0
    keep_ref[...] = jnp.where(first, low, high)
    give_ref[...] = jnp.where(first, high, low).astype(BF)


def first_back(t, g3, got, along):
    seq, width = g3.shape[1], along.shape[1]
    shape = jax.ShapeDtypeStruct
    return staged_call(
        first_back_kernel,
        in_specs=[SCALAR] + [WHOLE] * 3,
        out_specs=[WHOLE] * 2,
        out_shape=[shape((seq // 2, width), F32), shape((seq // 2, width), BF)],
        **vmem(34, 4_000_000_000, 5_000_000),
    )(t, g3, got, along)


def per_device(
    tokens, gain_attn, rel_table, w_qkv, w_o, gain_moe, router, w_in, w_out, segments, offset_buckets, expert_ids, out_grad
):
    rows, width = tokens.shape
    shard, _, cols = w_qkv.shape
    wo_rows = w_o.shape[0]
    buckets, heads_all = rel_table.shape
    heads = cols // (width // heads_all)
    seq = segments.shape[1]
    n_dp = lax.axis_size("dp")
    n_t = lax.axis_size("tensor")
    t = lax.axis_index("tensor")
    me = lax.axis_index("dp")
    ids_row = expert_ids.reshape(1, rows)

    send_one = start_send(w_qkv, w_o, n_dp, shard, wo_rows)
    got_one = lax.all_to_all(send_one, "dp", 0, 0)

    xf = tokens.astype(F32)
    scale_one = lax.rsqrt(jnp.mean(xf * xf, axis=-1, keepdims=True) + EPSILON)
    first_rows = (xf * scale_one * gain_attn).astype(BF)
    first_all = lax.all_gather(first_rows, "tensor", axis=0, tiled=True)
    table_local = lax.dynamic_slice_in_dim(rel_table, t * heads, heads, 1)
    bucket_row = jnp.pad(offset_buckets, (0, 1), constant_values=-1)[None]
    bucket_hits = (bucket_row[0][:, None] == jnp.arange(buckets, dtype=jnp.int32)[None, :]).astype(F32)
    offset_bias = jnp.einsum("bh,rb->hr", jnp.pad(table_local, ((0, 0), (0, 8 - heads))), bucket_hits, precision=PRECISE)
    down, so_down = places(n_dp, shard, cols, wo_rows)
    along = jnp.asarray(np.ascontiguousarray(down.T))
    x, xt, so, back, bias = prepare(first_all, offset_bias, segments, down, so_down, n_dp)

    keep, give, context, qkv, probs, wo_full = attend(t.reshape(1), got_one, x, so, bias)
    gain_row = gain_moe
    send_two, mid, second = dispatch(ids_row, out_grad, tokens, keep, swap(give), gain_row)

    got_two = lax.all_to_all(send_two.reshape(n_dp, 8, cols), "dp", 0, 0)
    so_along = jnp.asarray(np.ascontiguousarray(so_down.T))
    xot, selt, gate_home = between(expert_ids, context, so_along, second, router.T, n_dp)
    own, other = [y.reshape(n_dp * 8, cols) for y in (got_two, swap(got_two))]

    t1 = t.reshape(1)
    send_three, arrived, hidden, grad_pre, grad_expert = expert(me.reshape(1), t1, own, other, router.T, w_in[0], w_out[0])

    got_three = lax.all_to_all(send_three.reshape(n_dp * n_t, 16, 256), ALL, 0, 0).reshape(n_dp * n_t * 16, 256)
    grad_w_out = dot(hidden, grad_expert, ((0,), (0,)))
    grad_w_in = dot(arrived, grad_pre, ((0,), (0,)))
    activations, grad_mid, grad_own, router_piece, gain_two = home(got_three, selt, mid, gate_home, gain_row, out_grad)

    send_four, grad3 = attend_back(
        t1, grad_own, swap(grad_own), wo_full, qkv, probs, bucket_row, gain_attn, router_piece, gain_two, got_one, xt, xot, back
    )

    got_four = lax.all_to_all(send_four, "dp", 0, 0)
    keep_first, give_first = first_back(t1, grad3, got_one, along)
    grad_first_own = keep_first + swap(give_first).astype(F32)
    u1 = grad_first_own * gain_attn
    spread_one = jnp.mean(u1 * xf, axis=-1, keepdims=True)
    input_grad = (grad_mid + (scale_one * u1 - scale_one * scale_one * scale_one * xf * spread_one)).astype(BF)

    tiny_got = got_four[:, 48:54].astype(F32)
    router_half = tiny_got[:, 0]
    sums = jnp.sum(tiny_got[:, 1:], axis=0)
    packed = jnp.concatenate([router_half, sums], 0)
    other = swap(packed)
    low, high = jnp.where(t == 0, packed, other), jnp.where(t == 0, other, packed)
    grad_router = jnp.concatenate([low[:n_dp], high[:n_dp]], 1).T
    total = (packed[n_dp:] + other[n_dp:]).reshape(-1)
    gain_one_sum, gain_two_sum = total[:width], total[width : 2 * width]
    tables = [y[-1].reshape(heads, 64)[:, :buckets] for y in (low, high)]
    table_sum = jnp.concatenate(tables, 0).T
    weights = jnp.sum(got_four[:, :48].astype(F32), axis=0)
    full = [jnp.concatenate([weights[8 * c : 8 * c + 8], weights[32 + 4 * c : 36 + 4 * c]], 0) for c in range(4)]
    grad_qkv_shard = jnp.stack(full[:3], 1)
    grad_o_shard = full[3].reshape(wo_rows, width)
    return (
        activations,
        input_grad,
        gain_one_sum,
        table_sum,
        grad_qkv_shard,
        grad_o_shard,
        gain_two_sum,
        grad_router,
        grad_w_in[None],
        grad_w_out[None],
    )


def solution(mesh):
    in_specs = (
        P(("dp", "tensor"), None),
        P(),
        P(),
        P("dp", None, "tensor"),
        P(("tensor", "dp"), None),
        P(),
        P(),
        P("dp", None, "tensor"),
        P("dp", "tensor", None),
        P("dp", None),
        P(),
        P(("dp", "tensor"), None),
        P(("dp", "tensor"), None),
    )
    out_specs = (
        P(("dp", "tensor"), None),
        P(("dp", "tensor"), None),
        P(),
        P(),
        P("dp", None, "tensor"),
        P(("tensor", "dp"), None),
        P(),
        P(),
        P("dp", None, "tensor"),
        P("dp", "tensor", None),
    )
    return jax.shard_map(per_device, mesh=mesh, in_specs=in_specs, out_specs=out_specs, check_vma=False)
```

```python
import jax
import jax.numpy as jnp
import numpy as np
from jax import lax
from jax.experimental import pallas as pl
from jax.experimental.pallas import tpu as pltpu
from jax.sharding import PartitionSpec as P

PRECISE = lax.Precision.HIGHEST
EPSILON = 1e-06
MASKED = -1000000000.0
BF = jnp.bfloat16
F32 = jnp.float32
ALL = ("dp", "tensor")


def swap(rows):
    return lax.ppermute(rows, "tensor", [(0, 1), (1, 0)])


def dot(left, right, dims=((1,), (0,)), precision=None):
    return lax.dot_general(left, right, (dims, ((), ())), precision=precision, preferred_element_type=F32)


def dot_t(left, right):
    return dot(left, right, ((1,), (1,)))


def vmem(limit_mb, flops, moved):
    return dict(
        compiler_params=pltpu.CompilerParams(vmem_limit_bytes=limit_mb * 1024 * 1024),
        cost_estimate=pl.CostEstimate(flops=flops, bytes_accessed=moved, transcendentals=0),
    )


WHOLE = "whole"
HERE = "here"
SCALAR = pl.BlockSpec(memory_space=pltpu.SMEM)


class Arriving:
    def __init__(self, source, buffer, sem):
        self.buffer, self.shape = buffer, buffer.shape
        self.move = pltpu.make_async_copy(source, buffer, sem)
        self.move.start()

    def wait(self):
        if self.move is not None:
            self.move.wait()
            self.move = None

    def __getitem__(self, index):
        self.wait()
        return self.buffer[index]


class Leaving:
    def __init__(self, buffer, out, sem):
        self.buffer, self.out, self.sem = buffer, out, sem
        self.shape, self.move, self.sent = buffer.shape, None, False

    def __getitem__(self, index):
        return self.buffer[index]

    def __setitem__(self, index, value):
        self.buffer[index] = value

    def send(self):
        if not self.sent:
            self.move = pltpu.make_async_copy(self.buffer, self.out, self.sem)
            self.move.start()
            self.sent = True


def staged_call(body, in_specs, out_specs, out_shape, scratch_shapes=(), **params):
    several = isinstance(out_shape, list)
    results, kinds = (out_shape, out_specs) if several else ([out_shape], [out_specs])
    moved = [i for i, kind in enumerate(in_specs) if kind is WHOLE]
    left = [i for i, kind in enumerate(kinds) if kind is WHOLE]

    def kernel(*refs):
        refs = list(refs)
        ins, outs = refs[: len(in_specs)], refs[len(in_specs) : len(in_specs) + len(results)]
        rest = refs[len(in_specs) + len(results) :]
        in_buffers, rest = rest[: len(moved)], rest[len(moved) :]
        out_buffers, rest = rest[: len(left)], rest[len(left) :]
        in_sems, out_sems, extra = rest[0], rest[1], rest[2:]
        for n, (i, buffer) in enumerate(zip(moved, in_buffers)):
            ins[i] = Arriving(ins[i], buffer, in_sems.at[n])
        for n, (i, buffer) in enumerate(zip(left, out_buffers)):
            outs[i] = Leaving(buffer, outs[i], out_sems.at[n])
        body(*ins, *outs, *extra)
        for i in moved:
            ins[i].wait()
        for i in left:
            outs[i].send()
        for i in left:
            if outs[i].move is not None:
                outs[i].move.wait()

    def call(*args):
        space = {WHOLE: pltpu.HBM, HERE: pltpu.VMEM}
        place = lambda kind: pl.BlockSpec(memory_space=space[kind]) if kind in (WHOLE, HERE) else kind
        placed = [space[kind](r.shape, r.dtype) for kind, r in zip(kinds, results, strict=True)]
        args = [
            pltpu.with_memory_space_constraint(a, space[kind]) if kind in (WHOLE, HERE) else a
            for kind, a in zip(in_specs, args, strict=True)
        ]
        return pl.pallas_call(
            kernel,
            in_specs=[place(kind) for kind in in_specs],
            out_specs=[place(kind) for kind in kinds] if several else place(kinds[0]),
            out_shape=placed if several else placed[0],
            scratch_shapes=[pltpu.VMEM(args[i].shape, args[i].dtype) for i in moved]
            + [pltpu.VMEM(results[i].shape, results[i].dtype) for i in left]
            + [pltpu.SemaphoreType.DMA((max(1, len(moved)),)), pltpu.SemaphoreType.DMA((max(1, len(left)),))]
            + list(scratch_shapes),
            **params,
        )(*args)

    return call


def send(*refs):
    for ref in refs:
        if isinstance(ref, Leaving):
            ref.send()


def groups(ref):
    return [ref[:, 16 * g : 16 * g + 16, :].reshape(ref.shape[0] * 16, ref.shape[2]) for g in range(3)]


def attend_kernel(t_ref, got_ref, x_ref, so_ref, bias_ref, keep_ref, give_ref, ctx_ref, qkv_ref, probs_ref, wo_ref):
    one, two, three = groups(got_ref)
    q = (dot(x_ref[0], one) + dot(x_ref[2], three)).astype(BF)
    k = (dot(x_ref[1], one) + dot(x_ref[3], three)).astype(BF)
    v = (dot(x_ref[0], two) + dot(x_ref[4], three)).astype(BF)
    qkv_ref[0], qkv_ref[1], qkv_ref[2] = q, k, v
    send(qkv_ref)
    cols = q.shape[1]
    for half in range(2):
        wo_ref[:, half * cols : half * cols + cols] = (
            dot(so_ref[half], two) + dot(so_ref[2 + half], three)
        ).astype(BF)
    send(wo_ref)
    lane = lax.broadcasted_iota(jnp.int32, (q.shape[0], 128), 1)
    zero = jnp.zeros((q.shape[0], 128), BF)
    for pair in range(cols // 128):
        at = slice(128 * pair, 128 * pair + 128)
        q2, k2, v2 = q[:, at], k[:, at], v[:, at]
        outs = []
        for which in range(2):
            mine = (lane < 64) if which == 0 else (lane >= 64)
            scores = dot_t(jnp.where(mine, q2, zero), k2) + bias_ref[2 * pair + which]
            top = jnp.max(scores, axis=-1, keepdims=True)
            shifted = jnp.exp(scores - top)
            probs = (shifted * (1.0 / jnp.sum(shifted, axis=-1, keepdims=True))).astype(BF)
            probs_ref[2 * pair + which] = probs
            outs.append(dot(probs, v2))
        ctx_ref[:, at] = jnp.where(lane < 64, outs[0], outs[1]).astype(BF)
    send(probs_ref)
    send(ctx_ref)
    part = dot(ctx_ref[...], wo_ref[...])
    rows = part.shape[0] // 2
    low, high = part[:rows], part[rows:]
    first = t_ref[0] == 0
    keep_ref[...] = jnp.where(first, low, high)
    give_ref[...] = jnp.where(first, high, low).astype(BF)


def attend(t, got, x, so, bias):
    cols, seq = got.shape[2], x.shape[1]
    heads = bias.shape[0]
    shape = jax.ShapeDtypeStruct
    return staged_call(
        attend_kernel,
        in_specs=[SCALAR, HERE] + [WHOLE] * 3,
        out_specs=[HERE] * 2 + [WHOLE] * 4,
        out_shape=[
            shape((seq // 2, 2 * cols), F32),
            shape((seq // 2, 2 * cols), BF),
            shape((seq, cols), BF),
            shape((3, seq, cols), BF),
            shape((heads, seq, seq), BF),
            shape((cols, 2 * cols), BF),
        ],
        **vmem(34, 4_000_000_000, 14_000_000),
    )(t, got, x, so, bias)


def attend_back_kernel(
    t_ref, own_ref, other_ref, wo_ref, qkv_ref, probs_ref, hits_ref, gain_ref, router_ref, two_ref, xt_ref, xot_ref, got_ref, s_ref,
    send_ref, g3_ref, sems,
):
    own, other = own_ref[...], other_ref[...]
    first = t_ref[0] == 0
    ga = jnp.concatenate([jnp.where(first, own, other), jnp.where(first, other, own)], 0)
    q, k, v = qkv_ref[0], qkv_ref[1], qkv_ref[2]
    seq, cols = q.shape
    gctx = dot_t(ga, wo_ref[...]).astype(BF)
    lane = lax.broadcasted_iota(jnp.int32, (seq, 128), 1)
    low = lane < 64
    zero = jnp.zeros((seq, 128), BF)
    row8 = lax.broadcasted_iota(jnp.int32, (8, 2 * seq), 0)
    along = [lax.broadcasted_iota(jnp.int32, (seq, seq), axis) for axis in range(2)]
    flip = (along[0] + along[1] == seq - 1).astype(F32).astype(BF)
    diagonals = jnp.zeros((8, 2 * seq), F32)
    for pair in range(cols // 128):
        at = slice(128 * pair, 128 * pair + 128)
        q2, k2, v2, c2 = q[:, at], k[:, at], v[:, at], gctx[:, at]
        parts = []
        for which in range(2):
            mine = low if which == 0 else jnp.logical_not(low)
            probs = probs_ref[2 * pair + which]
            probs_f = probs.astype(F32)
            grad_probs = dot_t(jnp.where(mine, c2, zero), v2)
            inner = jnp.sum(probs_f * grad_probs, axis=-1, keepdims=True)
            ds = (probs_f * (grad_probs - inner)).astype(BF)
            parts.append((dot(ds, k2), dot(ds.T, q2), dot(probs.T, c2)))
            wide = jnp.concatenate([dot(flip, ds), jnp.zeros((seq, seq), F32)], 1)
            rolled = pltpu.roll(wide, 0, 1, stride=1, stride_axis=0)
            sums = jnp.sum(rolled, axis=0, keepdims=True)
            diagonals = jnp.where(row8 == 2 * pair + which, sums, diagonals)
        for c in range(3):
            g3_ref[c, :, at] = jnp.where(low, parts[0][c], parts[1][c]).astype(BF)
    send(g3_ref)
    outgoing = []

    def leave(rows, number):
        outgoing.append(
            pltpu.make_async_copy(send_ref.buffer.at[:, rows, :], send_ref.out.at[:, rows, :], sems.at[number])
        )
        outgoing[-1].start()

    gq, gk, gv = g3_ref[0], g3_ref[1], g3_ref[2]
    ga0, ga1 = ga[:, :cols], ga[:, cols:]
    one = dot(xt_ref[0], gq) + dot(xt_ref[1], gk)
    two = dot(xt_ref[0], gv) + dot(xot_ref[0], ga0) + dot(xot_ref[1], ga1)
    three = (
        dot(xt_ref[2], gq) + dot(xt_ref[3], gk) + dot(xt_ref[4], gv) + dot(xot_ref[2], ga0) + dot(xot_ref[3], ga1)
    )
    gain = jnp.zeros((128, gain_ref.shape[0]), F32)
    for g, (grad, weight) in enumerate(zip((one, two, three), groups(got_ref))):
        send_ref[:, 16 * g : 16 * g + 16, :] = grad.astype(BF).reshape(send_ref.shape[0], 16, cols)
        leave(slice(16 * g, 16 * g + 16), g)
        product = grad * weight.astype(F32)
        product = (product[:, :128] + product[:, 128:256] + product[:, 256:]).astype(BF)
        gain = gain + dot(product.T, s_ref[g])
    gain = jnp.sum(gain, axis=0, keepdims=True) / gain_ref[...].reshape(1, gain.shape[1])
    hits = ((iota(cols, 2 * seq, 0) & 63) == hits_ref[...]).astype(F32)
    table = dot(diagonals, hits, ((1,), (1,)), PRECISE)
    head_of = lax.broadcasted_iota(jnp.int32, table.shape, 1) // 64
    table = jnp.sum(
        jnp.where(head_of == lax.broadcasted_iota(jnp.int32, table.shape, 0), table, 0.0), axis=0, keepdims=True
    )
    gain_two = two_ref[...]
    row = lax.broadcasted_iota(jnp.int32, (8, cols), 0)
    tiny = jnp.zeros((8, cols), F32)
    for i, value in enumerate(
        (router_ref[...], gain[:, :cols], gain[:, cols:], gain_two[:, :cols], gain_two[:, cols:], table)
    ):
        tiny = jnp.where(row == i, value, tiny)
    send_ref[:, 48:56, :] = jnp.broadcast_to(tiny.astype(BF)[None], (send_ref.shape[0], 8, cols))
    leave(slice(48, 56), 3)
    send_ref.sent = True
    for move in outgoing:
        move.wait()


def attend_back(t, own, other, wo, qkv, probs, hits, gain, router, two, got, xt, xot, s):
    _, seq, cols = qkv.shape
    shape = jax.ShapeDtypeStruct
    return staged_call(
        attend_back_kernel,
        in_specs=[SCALAR, HERE, HERE] + [WHOLE] * 5 + [HERE] * 2 + [WHOLE] * 4,
        out_specs=[WHOLE] * 2,
        out_shape=[shape((got.shape[0], 56, cols), BF), shape((3, seq, cols), BF)],
        scratch_shapes=[pltpu.SemaphoreType.DMA((4,))],
        **vmem(34, 4_000_000_000, 16_000_000),
    )(t, own, other, wo, qkv, probs, hits, gain, router, two, xt, xot, got, s)


def iota(rows, columns, axis):
    return lax.broadcasted_iota(jnp.int32, (rows, columns), axis)


def split(value):
    high = value.astype(BF)
    return high, (value - high.astype(F32)).astype(BF)


def onehot(found):
    return jnp.where(found, 1.0, 0.0).astype(BF)


def ranks_along(ids, experts):
    rows = ids.shape[1]
    hits = iota(experts, rows, 0) == ids
    before = onehot(iota(rows, rows, 0) < iota(rows, rows, 1))
    return jnp.sum(dot(onehot(hits), before) * hits.astype(F32), axis=0, keepdims=True).astype(jnp.int32)


def ranks_down(ids, experts):
    rows = ids.shape[0]
    hits = iota(rows, experts, 1) == ids
    before = onehot(iota(rows, rows, 1) < iota(rows, rows, 0))
    return jnp.sum(dot(before, onehot(hits)) * hits.astype(F32), axis=1, keepdims=True).astype(jnp.int32)


def start_kernel(w_ref, wo_ref, qsel_ref, osel_ref, send_ref):
    peers, _, cols = send_ref.shape
    weights = sum(dot(qsel_ref[c], w_ref[:, c, :]) for c in range(3))
    for half in range(2):
        weights = weights + dot(osel_ref[half], wo_ref[:, half * cols : half * cols + cols])
    send_ref[...] = jnp.broadcast_to(weights.astype(BF)[None], send_ref.shape)


def start_send(w_rows, w_o, peers, shard, wo_rows):
    cols = w_rows.shape[2]
    qsel, osel = np.zeros((3, 48, shard), np.float32), np.zeros((2, 48, wo_rows), np.float32)
    for c in range(4):
        for i in range(shard):
            place = 8 * c + i if i < 8 else 32 + 4 * c + i - 8
            if c < 3:
                qsel[c, place, i] = 1
            else:
                osel[i % 2, place, i // 2] = 1
    return staged_call(
        start_kernel,
        in_specs=[WHOLE] * 4,
        out_specs=WHOLE,
        out_shape=jax.ShapeDtypeStruct((peers, 48, cols), BF),
        **vmem(34, 200_000_000, 3_500_000),
    )(w_rows, w_o, jnp.asarray(qsel, BF), jnp.asarray(osel, BF))


def prepare_kernel(
    first_ref, down_ref, along_ref, so_down_ref, offset_ref, seg_down_ref, seg_along_ref, x_ref, xt_ref, so_ref, s_ref, bias_ref
):
    first = first_ref[...]
    width, lanes = first.shape[1], x_ref.shape[2]
    for c in range(5):
        x_ref[c] = dot(first, onehot(iota(width, lanes, 1) == down_ref[:, c : c + 1])).astype(BF)
        sel = onehot(iota(lanes, width, 0) == along_ref[c : c + 1, :])
        xt_ref[c] = dot_t(sel, first).astype(BF)
        if c == 0:
            s_ref[0] = sel
            s_ref[1] = sel
        elif c == 1:
            s_ref[0] = s_ref[0] + sel
        elif c == 2:
            s_ref[2] = sel
        else:
            s_ref[2] = s_ref[2] + sel
    send(x_ref)
    send(xt_ref)
    send(s_ref)
    for c in range(4):
        so_ref[c] = onehot(iota(so_ref.shape[1], lanes, 1) == so_down_ref[:, c : c + 1])
    send(so_ref)
    heads, seq, _ = bias_ref.shape
    same = seg_down_ref[...] == seg_along_ref[...]
    for h in range(heads):
        wide = jnp.broadcast_to(offset_ref[h : h + 1, :], (seq, 2 * seq))
        wide = pltpu.roll(wide, seq + 1, 1, stride=1, stride_axis=0)
        bias_ref[h] = jnp.where(same, wide[:, :seq], MASKED)


def places(n_dp, shard, cols, wo_rows):
    d = np.arange(n_dp * shard)
    i, p = d % shard, d // shard
    down = np.full((n_dp * shard, 8), -1, np.int32)
    for c, (start, big) in enumerate([(0, False), (8, False), (-8, True), (-4, True), (0, True)]):
        down[:, c] = np.where((i >= 8) == big, p * 16 + i + start, -1)
    d = np.arange(cols)
    i, p = d % wo_rows, d // wo_rows
    so_down = np.full((cols, 8), -1, np.int32)
    for c in range(4):
        half, late = c % 2, c // 2 == 1
        place = 12 + 2 * (i - 4) + half if late else 8 + 2 * i + half
        so_down[:, c] = np.where((i >= 4) == late, p * 16 + place, -1)
    return down, so_down


def prepare(first_all, offset_bias, segments, down, so_down, n_dp):
    seq, width = first_all.shape
    cols, lanes, heads = so_down.shape[0], n_dp * 16, 6
    shape = jax.ShapeDtypeStruct
    return staged_call(
        prepare_kernel,
        in_specs=[WHOLE] * 7,
        out_specs=[WHOLE] * 5,
        out_shape=[
            shape((5, seq, lanes), BF),
            shape((5, lanes, seq), BF),
            shape((4, cols, lanes), BF),
            shape((3, lanes, width), BF),
            shape((heads, seq, seq), F32),
        ],
        **vmem(34, 4_000_000_000, 16_000_000),
    )(
        first_all,
        jnp.asarray(down),
        jnp.asarray(np.ascontiguousarray(down.T)),
        jnp.asarray(so_down),
        offset_bias,
        segments.reshape(seq, 1),
        segments,
    )


def dispatch_kernel(ids_ref, og_ref, tokens_ref, keep_ref, got_ref, gain_ref, send_ref, mid_ref, second_ref):
    mid = tokens_ref[...].astype(F32) + (keep_ref[...] + got_ref[...].astype(F32))
    scale = lax.rsqrt(jnp.mean(mid * mid, axis=-1, keepdims=True) + EPSILON)
    second = mid * scale * gain_ref[...].reshape(1, mid.shape[1])
    mid_ref[...] = mid
    second_ref[...] = second
    send(mid_ref)
    send(second_ref)
    ids = ids_ref[...]
    rows, cols = ids.shape[1], send_ref.shape[1]
    base = ids * 8 + ranks_along(ids, rows // 2) * 2
    row = iota(send_ref.shape[0], rows, 0)
    total = jnp.zeros(send_ref.shape, F32)
    for start, values in ((0, second.astype(BF)), (4, og_ref[...])):
        for half in range(2):
            at = slice(half * cols, half * cols + cols)
            total = total + dot(onehot(row == base + (start + half)), values[:, at])
    send_ref[...] = total.astype(BF)


def dispatch(ids_row, out_grad, tokens, keep, got, gain):
    rows, width = tokens.shape
    shape = jax.ShapeDtypeStruct
    return staged_call(
        dispatch_kernel,
        in_specs=[WHOLE] * 3 + [HERE, HERE, WHOLE],
        out_specs=[WHOLE] * 3,
        out_shape=[shape((rows * 4, width // 2), BF), shape((rows, width), F32), shape((rows, width), F32)],
        **vmem(16, 200_000_000, 2_000_000),
    )(ids_row, out_grad, tokens, keep, got, gain)


def between_kernel(
    ids_ref, ctx_ref, so_along_ref, second_ref, router_ref, xot_ref, selt_ref, gate_ref
):
    ctx = ctx_ref[...]
    lanes = xot_ref.shape[1]
    for c in range(4):
        sel = onehot(iota(lanes, ctx.shape[1], 0) == so_along_ref[c : c + 1, :])
        xot_ref[c] = dot_t(sel, ctx).astype(BF)
    send(xot_ref)
    ids = ids_ref[...]
    rows = ids.shape[0]
    experts = router_ref.shape[0]
    base = ids * 16 + ranks_down(ids, experts) * 3
    lane = iota(rows, selt_ref.shape[1], 1)
    for j in range(3):
        selt_ref[rows * j : rows * j + rows, :] = onehot((lane == base + j) | (lane == base + (8 + j)))
    send(selt_ref)
    s_high, s_low = split(second_ref[...])
    r_high, r_low = split(router_ref[...])
    logits = dot_t(s_high, r_high) + (dot_t(s_low, r_high) + dot_t(s_high, r_low))
    shifted = jnp.exp(logits - jnp.max(logits, axis=-1, keepdims=True))
    hit = iota(rows, experts, 1) == ids
    gate_ref[...] = jnp.sum(jnp.where(hit, shifted, 0.0), axis=-1, keepdims=True) / jnp.sum(
        shifted, axis=-1, keepdims=True
    )


def between(ids, ctx, so_along, second, router, n_dp):
    rows = ids.shape[0]
    seq, cols = ctx.shape
    shape = jax.ShapeDtypeStruct
    return staged_call(
        between_kernel,
        in_specs=[WHOLE] * 5,
        out_specs=[WHOLE] * 3,
        out_shape=[
            shape((4, n_dp * 16, seq), BF),
            shape((3 * rows, rows * 8), BF),
            shape((rows, 1), F32),
        ],
        **vmem(20, 2_000_000_000, 8_000_000),
    )(ids, ctx, so_along, second, router)


def expert_kernel(
    me_ref, t_ref, own_ref, other_ref, router_ref, w1_ref, w2_ref, send_ref, arrived_ref, hidden_ref, pre_ref, ge_ref, *stages
):
    own, other = own_ref[...], other_ref[...]
    first = t_ref[0] == 0
    got = jnp.concatenate([jnp.where(first, own, other), jnp.where(first, other, own)], 0)
    count, cols = ge_ref.shape[0], got.shape[1]
    half = count // 2
    r = iota(count, 1, 0)
    pair = r & (half - 1)
    base = (pair & 1) * own.shape[0] + (pair >> 1) * 8 + (r >= half).astype(jnp.int32) * 2
    lane = iota(count, got.shape[0], 1)
    g = []
    for side in range(2):
        arrived_ref[:, cols * side : cols * side + cols] = dot(onehot(lane == base + side), got).astype(BF)
        g.append(dot(onehot(lane == base + (4 + side)), got))
    g = jnp.concatenate(g, 1)
    arrived = arrived_ref[...]
    r_high, r_low = split(router_ref[...])
    logits = dot_t(arrived, r_high) + dot_t(arrived, r_low)
    shifted = jnp.exp(logits - jnp.max(logits, axis=-1, keepdims=True))
    probs = shifted / jnp.sum(shifted, axis=-1, keepdims=True)
    mine = (iota(count, probs.shape[1], 1) == me_ref[0]).astype(F32)
    gate = jnp.sum(probs * mine, axis=-1, keepdims=True)
    ge = (gate * g).astype(BF)
    ge_ref[...] = ge
    width, hidden_cols = w1_ref.shape
    step = 256
    out = jnp.zeros((count, width), F32)
    back = jnp.zeros((count, width), F32)
    for f in range(0, hidden_cols, step):
        at = slice(f, f + step)
        w1, w2 = w1_ref[:, at], w2_ref[at, :]
        u = dot(arrived, w1)
        cdf = 0.5 + 0.5 * lax.erf(u * 0.7071067811865476)
        hidden = (u * cdf).astype(BF)
        slope = cdf + u * (jnp.exp(-0.5 * u * u) * 0.3989422804014327)
        grad = (dot_t(ge, w2) * slope).astype(BF)
        hidden_ref[:, at] = hidden
        pre_ref[:, at] = grad
        out = out + dot(hidden, w2)
        back = back + dot_t(grad, w1)
    send(hidden_ref)
    send(pre_ref)
    send(ge_ref)
    send(arrived_ref)
    grad_gate = jnp.sum(g * out, axis=-1, keepdims=True)
    grad_logits = grad_gate * gate * (mine - probs)
    l_high, l_low = split(grad_logits)
    back = back + (dot(l_high, r_high) + (dot(l_low, r_high) + dot(l_high, r_low)))
    t_high, t_low = split(grad_logits.T)
    router_part = dot(t_high, arrived) + dot(t_low, arrived)
    for side, stage in enumerate(stages):
        stage[...] = jnp.zeros(stage.shape, F32)
        values = out if side < 2 else back
        for j in range(3):
            at = slice(256 * j + 128 * (side % 2), 256 * j + 128 * (side % 2) + 128)
            for s in range(2):
                stage[pl.ds(s * 3 + j, half, stride=8), :] = values[s * half : s * half + half, at]
        if side < 3:
            for t in range(2):
                at = cols * t + 128 * side
                stage[pl.ds(6 + 8 * t, half // 2, stride=16), :] = router_part[:, at : at + 128]
        send_ref[:, 128 * side : 128 * side + 128] = stage[...].astype(BF)


def expert(me, t, own, other, router, w1, w2):
    count, width = own.shape[0] // 2, own.shape[1] * 2
    hidden = w1.shape[1]
    shape = jax.ShapeDtypeStruct
    return staged_call(
        expert_kernel,
        in_specs=[SCALAR] * 2 + [HERE] * 2 + [WHOLE] * 3,
        out_specs=[WHOLE] * 5,
        out_shape=[
            shape((count * 4, 512), BF),
            shape((count, width), BF),
            shape((count, hidden), BF),
            shape((count, hidden), BF),
            shape((count, width), BF),
        ],
        scratch_shapes=[pltpu.VMEM((count * 4, 128), F32)] * 4,
        **vmem(34, 3_000_000_000, 9_000_000),
    )(me, t, own, other, router, w1, w2)


def home_kernel(
    got_ref, selt_ref, mid_ref, gate_ref, gain_ref, og_ref, act_ref, gmid_ref, gattn_ref, router_ref, two_ref
):
    got = got_ref[...]
    rows = mid_ref.shape[0]
    sums = dot(selt_ref[...], got)
    out = jnp.concatenate([sums[rows * j : rows * j + rows, :256] for j in range(3)], 1)
    grad_second = jnp.concatenate([sums[rows * j : rows * j + rows, 256:] for j in range(3)], 1)
    lane = iota(16, got.shape[0], 1) & 7
    piece = dot(onehot(lane == iota(16, got.shape[0], 0) + 6), got)
    router_ref[...] = piece[0:1, : router_ref.shape[1]]
    mid = mid_ref[...]
    gain = gain_ref[...].reshape(1, mid.shape[1])
    send(router_ref)
    act_ref[...] = (mid + gate_ref[...] * out).astype(BF)
    send(act_ref)
    scale = lax.rsqrt(jnp.mean(mid * mid, axis=-1, keepdims=True) + EPSILON)
    u = grad_second * gain
    two_ref[...] = jnp.sum(grad_second * mid * scale, axis=0, keepdims=True)
    spread = jnp.mean(u * mid, axis=-1, keepdims=True)
    gmid = og_ref[...].astype(F32) + (scale * u - scale * scale * scale * mid * spread)
    gmid_ref[...] = gmid
    gattn_ref[...] = gmid.astype(BF)


def home(got, selt, mid, gate, gain, out_grad):
    rows, width = mid.shape
    shape = jax.ShapeDtypeStruct
    return staged_call(
        home_kernel,
        in_specs=[HERE] + [WHOLE] * 5,
        out_specs=[WHOLE] * 2 + [HERE] * 3,
        out_shape=[
            shape((rows, width), BF),
            shape((rows, width), F32),
            shape((rows, width), BF),
            shape((1, width // 2), F32),
            shape((1, width), F32),
        ],
        **vmem(16, 500_000_000, 6_000_000),
    )(got, selt, mid, gate, gain, out_grad)


def small_sums_kernel(got_ref, packed_ref):
    tiny = got_ref[:, 48:56, :].astype(F32)
    peers = tiny.shape[0]
    packed_ref[:peers, :] = tiny[:, 0, :]
    packed_ref[peers:, :] = jnp.sum(tiny, axis=0)


def weight_sums_kernel(got_ref, qkv_ref, wo_ref):
    total = jnp.sum(got_ref[:, :48, :].astype(F32), axis=0)
    cols = total.shape[1]
    for c in range(3):
        qkv_ref[0:8, c, :] = total[8 * c : 8 * c + 8]
        qkv_ref[8:12, c, :] = total[32 + 4 * c : 36 + 4 * c]
    for j in range(12):
        row = 24 + j if j < 8 else 36 + j
        wo_ref[j // 2 : j // 2 + 1, (j % 2) * cols : (j % 2) * cols + cols] = total[row : row + 1]


def small_outputs_kernel(t_ref, own_ref, other_ref, router_ref, one_ref, two_ref, table_ref):
    own, other = own_ref[...], other_ref[...]
    first = t_ref[0] == 0
    low, high = jnp.where(first, own, other), jnp.where(first, other, own)
    peers, cols = router_ref.shape[0], own.shape[1]
    router_ref[:, :cols] = low[:peers]
    router_ref[:, cols:] = high[:peers]
    total = own[peers:] + other[peers:]
    for ref, row in ((one_ref, 1), (two_ref, 3)):
        ref[:cols] = total[row]
        ref[cols:] = total[row + 1]
    heads, buckets = table_ref.shape[0] // 2, table_ref.shape[1]
    for h in range(2 * heads):
        row = (low if h < heads else high)[peers + 5 : peers + 6]
        at = 64 * (h % heads)
        table_ref[h : h + 1, :] = row[:, at : at + buckets]


def small_sums(got):
    return staged_call(
        small_sums_kernel,
        in_specs=[HERE],
        out_specs=HERE,
        out_shape=jax.ShapeDtypeStruct((got.shape[0] + 8, got.shape[2]), F32),
        **vmem(8, 100_000, 400_000),
    )(got)


def weight_sums(got, shard, wo_rows):
    shape = jax.ShapeDtypeStruct
    return staged_call(
        weight_sums_kernel,
        in_specs=[HERE],
        out_specs=[WHOLE] * 2,
        out_shape=[shape((shard, 3, got.shape[2]), F32), shape((wo_rows, 2 * got.shape[2]), F32)],
        **vmem(8, 1_000_000, 3_000_000),
    )(got)


def small_outputs(t, own, other, peers, heads, buckets):
    width = 2 * own.shape[1]
    shape = jax.ShapeDtypeStruct
    return staged_call(
        small_outputs_kernel,
        in_specs=[SCALAR, HERE, HERE],
        out_specs=[WHOLE] * 4,
        out_shape=[shape((peers, width), F32), shape((width,), F32), shape((width,), F32), shape((2 * heads, buckets), F32)],
        **vmem(8, 100_000, 700_000),
    )(t, own, other)


def first_back_kernel(t_ref, g3_ref, got_ref, along_ref, keep_ref, give_ref):
    one, two, three = groups(got_ref)
    g = [g3_ref[c] for c in range(3)]
    lanes, width = one.shape[0], along_ref.shape[1]
    pieces = [dot_t(g[0], one), dot_t(g[1], one), dot_t(g[0], three), dot_t(g[1], three), dot_t(g[2], three)]
    pieces = [p.astype(BF) for p in pieces]
    total = jnp.zeros((g[0].shape[0], width), F32)
    for c in range(5):
        sel = onehot(iota(lanes, width, 0) == along_ref[c : c + 1, :])
        total = total + dot(pieces[c], sel)
        if c == 0:
            total = total + dot(dot_t(g[2], two).astype(BF), sel)
    rows = total.shape[0] // 2
    low, high = total[:rows], total[rows:]
    first = t_ref[0] == 0
    keep_ref[...] = jnp.where(first, low, high)
    give_ref[...] = jnp.where(first, high, low).astype(BF)


def first_back(t, g3, got, along):
    seq, width = g3.shape[1], along.shape[1]
    shape = jax.ShapeDtypeStruct
    return staged_call(
        first_back_kernel,
        in_specs=[SCALAR] + [WHOLE] * 3,
        out_specs=[WHOLE] * 2,
        out_shape=[shape((seq // 2, width), F32), shape((seq // 2, width), BF)],
        **vmem(34, 4_000_000_000, 5_000_000),
    )(t, g3, got, along)


def per_device(
    tokens, gain_attn, rel_table, w_qkv, w_o, gain_moe, router, w_in, w_out, segments, offset_buckets, expert_ids, out_grad
):
    rows, width = tokens.shape
    shard, _, cols = w_qkv.shape
    wo_rows = w_o.shape[0]
    buckets, heads_all = rel_table.shape
    heads = cols // (width // heads_all)
    seq = segments.shape[1]
    n_dp = lax.axis_size("dp")
    n_t = lax.axis_size("tensor")
    t = lax.axis_index("tensor")
    me = lax.axis_index("dp")
    ids_row = expert_ids.reshape(1, rows)

    send_one = start_send(w_qkv, w_o, n_dp, shard, wo_rows)
    got_one = lax.all_to_all(send_one, "dp", 0, 0)

    xf = tokens.astype(F32)
    scale_one = lax.rsqrt(jnp.mean(xf * xf, axis=-1, keepdims=True) + EPSILON)
    first_rows = (xf * scale_one * gain_attn).astype(BF)
    first_all = lax.all_gather(first_rows, "tensor", axis=0, tiled=True)
    table_local = lax.dynamic_slice_in_dim(rel_table, t * heads, heads, 1)
    bucket_row = jnp.pad(offset_buckets, (0, 1), constant_values=-1)[None]
    bucket_hits = (bucket_row[0][:, None] == jnp.arange(buckets, dtype=jnp.int32)[None, :]).astype(F32)
    offset_bias = jnp.einsum("bh,rb->hr", jnp.pad(table_local, ((0, 0), (0, 8 - heads))), bucket_hits, precision=PRECISE)
    down, so_down = places(n_dp, shard, cols, wo_rows)
    along = jnp.asarray(np.ascontiguousarray(down.T))
    x, xt, so, back, bias = prepare(first_all, offset_bias, segments, down, so_down, n_dp)

    keep, give, context, qkv, probs, wo_full = attend(t.reshape(1), got_one, x, so, bias)
    gain_row = gain_moe
    send_two, mid, second = dispatch(ids_row, out_grad, tokens, keep, swap(give), gain_row)

    got_two = lax.all_to_all(send_two.reshape(n_dp, 8, cols), "dp", 0, 0)
    so_along = jnp.asarray(np.ascontiguousarray(so_down.T))
    xot, selt, gate_home = between(expert_ids, context, so_along, second, router.T, n_dp)
    own, other = [y.reshape(n_dp * 8, cols) for y in (got_two, swap(got_two))]

    t1 = t.reshape(1)
    send_three, arrived, hidden, grad_pre, grad_expert = expert(me.reshape(1), t1, own, other, router.T, w_in[0], w_out[0])

    got_three = lax.all_to_all(send_three.reshape(n_dp * n_t, 8, 512), ALL, 0, 0).reshape(n_dp * n_t * 8, 512)
    grad_w_out = dot(hidden, grad_expert, ((0,), (0,)))
    grad_w_in = dot(arrived, grad_pre, ((0,), (0,)))
    activations, grad_mid, grad_own, router_piece, gain_two = home(got_three, selt, mid, gate_home, gain_row, out_grad)

    send_four, grad3 = attend_back(
        t1, grad_own, swap(grad_own), wo_full, qkv, probs, bucket_row, gain_attn, router_piece, gain_two, got_one, xt, xot, back
    )

    got_four = lax.all_to_all(send_four, "dp", 0, 0)
    keep_first, give_first = first_back(t1, grad3, got_one, along)
    grad_first_own = keep_first + swap(give_first).astype(F32)
    u1 = grad_first_own * gain_attn
    spread_one = jnp.mean(u1 * xf, axis=-1, keepdims=True)
    input_grad = (grad_mid + (scale_one * u1 - scale_one * scale_one * scale_one * xf * spread_one)).astype(BF)

    got_four, input_grad, grad_w_in, grad_w_out = lax.optimization_barrier(
        (got_four, input_grad, grad_w_in, grad_w_out)
    )
    packed = small_sums(got_four)
    other = swap(packed)
    grad_qkv_shard, grad_o_shard = weight_sums(got_four, shard, wo_rows)
    grad_router, gain_one_sum, gain_two_sum, table_sum = small_outputs(t1, packed, other, n_dp, heads, buckets)
    grad_router, table_sum = grad_router.T, table_sum.T
    return (
        activations,
        input_grad,
        gain_one_sum,
        table_sum,
        grad_qkv_shard,
        grad_o_shard,
        gain_two_sum,
        grad_router,
        grad_w_in[None],
        grad_w_out[None],
    )


def solution(mesh):
    in_specs = (
        P(("dp", "tensor"), None),
        P(),
        P(),
        P("dp", None, "tensor"),
        P(("tensor", "dp"), None),
        P(),
        P(),
        P("dp", None, "tensor"),
        P("dp", "tensor", None),
        P("dp", None),
        P(),
        P(("dp", "tensor"), None),
        P(("dp", "tensor"), None),
    )
    out_specs = (
        P(("dp", "tensor"), None),
        P(("dp", "tensor"), None),
        P(),
        P(),
        P("dp", None, "tensor"),
        P(("tensor", "dp"), None),
        P(),
        P(),
        P("dp", None, "tensor"),
        P("dp", "tensor", None),
    )
    return jax.shard_map(per_device, mesh=mesh, in_specs=in_specs, out_specs=out_specs, check_vma=False)
```

```python
import jax
import jax.numpy as jnp
import numpy as np
from jax import lax
from jax.experimental import pallas as pl
from jax.experimental.pallas import tpu as pltpu
from jax.sharding import PartitionSpec as P

PRECISE = lax.Precision.HIGHEST
EPSILON = 1e-06
MASKED = -1000000000.0
BF = jnp.bfloat16
F32 = jnp.float32
ALL = ("dp", "tensor")


def swap(rows):
    return lax.ppermute(rows, "tensor", [(0, 1), (1, 0)])


def dot(left, right, dims=((1,), (0,)), precision=None):
    return lax.dot_general(left, right, (dims, ((), ())), precision=precision, preferred_element_type=F32)


def dot_t(left, right):
    return dot(left, right, ((1,), (1,)))


def vmem(limit_mb, flops, moved):
    return dict(
        compiler_params=pltpu.CompilerParams(vmem_limit_bytes=limit_mb * 1024 * 1024),
        cost_estimate=pl.CostEstimate(flops=flops, bytes_accessed=moved, transcendentals=0),
    )


WHOLE = "whole"
HERE = "here"
SCALAR = pl.BlockSpec(memory_space=pltpu.SMEM)


class Arriving:
    def __init__(self, source, buffer, sem):
        self.buffer, self.shape = buffer, buffer.shape
        self.move = pltpu.make_async_copy(source, buffer, sem)
        self.move.start()

    def wait(self):
        if self.move is not None:
            self.move.wait()
            self.move = None

    def __getitem__(self, index):
        self.wait()
        return self.buffer[index]


class Leaving:
    def __init__(self, buffer, out, sem):
        self.buffer, self.out, self.sem = buffer, out, sem
        self.shape, self.move, self.sent = buffer.shape, None, False

    def __getitem__(self, index):
        return self.buffer[index]

    def __setitem__(self, index, value):
        self.buffer[index] = value

    def send(self):
        if not self.sent:
            self.move = pltpu.make_async_copy(self.buffer, self.out, self.sem)
            self.move.start()
            self.sent = True


def staged_call(body, in_specs, out_specs, out_shape, scratch_shapes=(), **params):
    several = isinstance(out_shape, list)
    results, kinds = (out_shape, out_specs) if several else ([out_shape], [out_specs])
    moved = [i for i, kind in enumerate(in_specs) if kind is WHOLE]
    left = [i for i, kind in enumerate(kinds) if kind is WHOLE]

    def kernel(*refs):
        refs = list(refs)
        ins, outs = refs[: len(in_specs)], refs[len(in_specs) : len(in_specs) + len(results)]
        rest = refs[len(in_specs) + len(results) :]
        in_buffers, rest = rest[: len(moved)], rest[len(moved) :]
        out_buffers, rest = rest[: len(left)], rest[len(left) :]
        in_sems, out_sems, extra = rest[0], rest[1], rest[2:]
        for n, (i, buffer) in enumerate(zip(moved, in_buffers)):
            ins[i] = Arriving(ins[i], buffer, in_sems.at[n])
        for n, (i, buffer) in enumerate(zip(left, out_buffers)):
            outs[i] = Leaving(buffer, outs[i], out_sems.at[n])
        body(*ins, *outs, *extra)
        for i in moved:
            ins[i].wait()
        for i in left:
            outs[i].send()
        for i in left:
            if outs[i].move is not None:
                outs[i].move.wait()

    def call(*args):
        space = {WHOLE: pltpu.HBM, HERE: pltpu.VMEM}
        place = lambda kind: pl.BlockSpec(memory_space=space[kind]) if kind in (WHOLE, HERE) else kind
        placed = [space[kind](r.shape, r.dtype) for kind, r in zip(kinds, results, strict=True)]
        args = [
            pltpu.with_memory_space_constraint(a, space[kind]) if kind in (WHOLE, HERE) else a
            for kind, a in zip(in_specs, args, strict=True)
        ]
        return pl.pallas_call(
            kernel,
            in_specs=[place(kind) for kind in in_specs],
            out_specs=[place(kind) for kind in kinds] if several else place(kinds[0]),
            out_shape=placed if several else placed[0],
            scratch_shapes=[pltpu.VMEM(args[i].shape, args[i].dtype) for i in moved]
            + [pltpu.VMEM(results[i].shape, results[i].dtype) for i in left]
            + [pltpu.SemaphoreType.DMA((max(1, len(moved)),)), pltpu.SemaphoreType.DMA((max(1, len(left)),))]
            + list(scratch_shapes),
            **params,
        )(*args)

    return call


def send(*refs):
    for ref in refs:
        if isinstance(ref, Leaving):
            ref.send()


def groups(ref):
    return [ref[:, 16 * g : 16 * g + 16, :].reshape(ref.shape[0] * 16, ref.shape[2]) for g in range(3)]


def attend_kernel(t_ref, got_ref, x_ref, so_ref, bias_ref, keep_ref, give_ref, ctx_ref, qkv_ref, probs_ref, wo_ref):
    one, two, three = groups(got_ref)
    q = (dot(x_ref[0], one) + dot(x_ref[2], three)).astype(BF)
    k = (dot(x_ref[1], one) + dot(x_ref[3], three)).astype(BF)
    v = (dot(x_ref[0], two) + dot(x_ref[4], three)).astype(BF)
    qkv_ref[0], qkv_ref[1], qkv_ref[2] = q, k, v
    send(qkv_ref)
    cols = q.shape[1]
    for half in range(2):
        wo_ref[:, half * cols : half * cols + cols] = (
            dot(so_ref[half], two) + dot(so_ref[2 + half], three)
        ).astype(BF)
    send(wo_ref)
    lane = lax.broadcasted_iota(jnp.int32, (q.shape[0], 128), 1)
    zero = jnp.zeros((q.shape[0], 128), BF)
    for pair in range(cols // 128):
        at = slice(128 * pair, 128 * pair + 128)
        q2, k2, v2 = q[:, at], k[:, at], v[:, at]
        outs = []
        for which in range(2):
            mine = (lane < 64) if which == 0 else (lane >= 64)
            scores = dot_t(jnp.where(mine, q2, zero), k2) + bias_ref[2 * pair + which]
            top = jnp.max(scores, axis=-1, keepdims=True)
            shifted = jnp.exp(scores - top)
            probs = (shifted * (1.0 / jnp.sum(shifted, axis=-1, keepdims=True))).astype(BF)
            probs_ref[2 * pair + which] = probs
            outs.append(dot(probs, v2))
        ctx_ref[:, at] = jnp.where(lane < 64, outs[0], outs[1]).astype(BF)
    send(probs_ref)
    send(ctx_ref)
    part = dot(ctx_ref[...], wo_ref[...])
    rows = part.shape[0] // 2
    low, high = part[:rows], part[rows:]
    first = t_ref[0] == 0
    keep_ref[...] = jnp.where(first, low, high)
    give_ref[...] = jnp.where(first, high, low).astype(BF)


def attend(t, got, x, so, bias):
    cols, seq = got.shape[2], x.shape[1]
    heads = bias.shape[0]
    shape = jax.ShapeDtypeStruct
    return staged_call(
        attend_kernel,
        in_specs=[SCALAR, HERE] + [WHOLE] * 3,
        out_specs=[HERE] * 2 + [WHOLE] * 4,
        out_shape=[
            shape((seq // 2, 2 * cols), F32),
            shape((seq // 2, 2 * cols), BF),
            shape((seq, cols), BF),
            shape((3, seq, cols), BF),
            shape((heads, seq, seq), BF),
            shape((cols, 2 * cols), BF),
        ],
        **vmem(34, 4_000_000_000, 14_000_000),
    )(t, got, x, so, bias)


def attend_back_kernel(
    t_ref, own_ref, other_ref, wo_ref, qkv_ref, probs_ref, hits_ref, gain_ref, router_ref, two_ref, xt_ref, xot_ref, got_ref, s_ref,
    send_ref, g3_ref,
):
    own, other = own_ref[...], other_ref[...]
    first = t_ref[0] == 0
    ga = jnp.concatenate([jnp.where(first, own, other), jnp.where(first, other, own)], 0)
    q, k, v = qkv_ref[0], qkv_ref[1], qkv_ref[2]
    seq, cols = q.shape
    gctx = dot_t(ga, wo_ref[...]).astype(BF)
    lane = lax.broadcasted_iota(jnp.int32, (seq, 128), 1)
    low = lane < 64
    zero = jnp.zeros((seq, 128), BF)
    row8 = lax.broadcasted_iota(jnp.int32, (8, 2 * seq), 0)
    along = [lax.broadcasted_iota(jnp.int32, (seq, seq), axis) for axis in range(2)]
    flip = (along[0] + along[1] == seq - 1).astype(F32).astype(BF)
    diagonals = jnp.zeros((8, 2 * seq), F32)
    for pair in range(cols // 128):
        at = slice(128 * pair, 128 * pair + 128)
        q2, k2, v2, c2 = q[:, at], k[:, at], v[:, at], gctx[:, at]
        parts = []
        for which in range(2):
            mine = low if which == 0 else jnp.logical_not(low)
            probs = probs_ref[2 * pair + which]
            probs_f = probs.astype(F32)
            grad_probs = dot_t(jnp.where(mine, c2, zero), v2)
            inner = jnp.sum(probs_f * grad_probs, axis=-1, keepdims=True)
            ds = (probs_f * (grad_probs - inner)).astype(BF)
            parts.append((dot(ds, k2), dot(ds.T, q2), dot(probs.T, c2)))
            wide = jnp.concatenate([dot(flip, ds), jnp.zeros((seq, seq), F32)], 1)
            rolled = pltpu.roll(wide, 0, 1, stride=1, stride_axis=0)
            sums = jnp.sum(rolled, axis=0, keepdims=True)
            diagonals = jnp.where(row8 == 2 * pair + which, sums, diagonals)
        for c in range(3):
            g3_ref[c, :, at] = jnp.where(low, parts[0][c], parts[1][c]).astype(BF)
    send(g3_ref)
    gq, gk, gv = g3_ref[0], g3_ref[1], g3_ref[2]
    ga0, ga1 = ga[:, :cols], ga[:, cols:]
    one = dot(xt_ref[0], gq) + dot(xt_ref[1], gk)
    two = dot(xt_ref[0], gv) + dot(xot_ref[0], ga0) + dot(xot_ref[1], ga1)
    three = (
        dot(xt_ref[2], gq) + dot(xt_ref[3], gk) + dot(xt_ref[4], gv) + dot(xot_ref[2], ga0) + dot(xot_ref[3], ga1)
    )
    gain = jnp.zeros((128, gain_ref.shape[0]), F32)
    for g, (grad, weight) in enumerate(zip((one, two, three), groups(got_ref))):
        send_ref[:, 16 * g : 16 * g + 16, :] = grad.astype(BF).reshape(send_ref.shape[0], 16, cols)
        product = grad * weight.astype(F32)
        product = (product[:, :128] + product[:, 128:256] + product[:, 256:]).astype(BF)
        gain = gain + dot(product.T, s_ref[g])
    gain = jnp.sum(gain, axis=0, keepdims=True) / gain_ref[...].reshape(1, gain.shape[1])
    hits = ((iota(cols, 2 * seq, 0) & 63) == hits_ref[...]).astype(F32)
    table = dot(diagonals, hits, ((1,), (1,)), PRECISE)
    head_of = lax.broadcasted_iota(jnp.int32, table.shape, 1) // 64
    table = jnp.sum(
        jnp.where(head_of == lax.broadcasted_iota(jnp.int32, table.shape, 0), table, 0.0), axis=0, keepdims=True
    )
    gain_two = two_ref[...]
    row = lax.broadcasted_iota(jnp.int32, (8, cols), 0)
    tiny = jnp.zeros((8, cols), F32)
    for i, value in enumerate(
        (router_ref[...], gain[:, :cols], gain[:, cols:], gain_two[:, :cols], gain_two[:, cols:], table)
    ):
        tiny = jnp.where(row == i, value, tiny)
    send_ref[:, 48:56, :] = jnp.broadcast_to(tiny.astype(BF)[None], (send_ref.shape[0], 8, cols))


def attend_back(t, own, other, wo, qkv, probs, hits, gain, router, two, got, xt, xot, s):
    _, seq, cols = qkv.shape
    shape = jax.ShapeDtypeStruct
    return staged_call(
        attend_back_kernel,
        in_specs=[SCALAR, HERE, HERE] + [WHOLE] * 5 + [HERE] * 2 + [WHOLE] * 4,
        out_specs=[WHOLE] * 2,
        out_shape=[shape((got.shape[0], 56, cols), BF), shape((3, seq, cols), BF)],
        **vmem(34, 4_000_000_000, 16_000_000),
    )(t, own, other, wo, qkv, probs, hits, gain, router, two, xt, xot, got, s)


def iota(rows, columns, axis):
    return lax.broadcasted_iota(jnp.int32, (rows, columns), axis)


def split(value):
    high = value.astype(BF)
    return high, (value - high.astype(F32)).astype(BF)


def onehot(found):
    return jnp.where(found, 1.0, 0.0).astype(BF)


def ranks_along(ids, experts):
    rows = ids.shape[1]
    hits = iota(experts, rows, 0) == ids
    before = onehot(iota(rows, rows, 0) < iota(rows, rows, 1))
    return jnp.sum(dot(onehot(hits), before) * hits.astype(F32), axis=0, keepdims=True).astype(jnp.int32)


def ranks_down(ids, experts):
    rows = ids.shape[0]
    hits = iota(rows, experts, 1) == ids
    before = onehot(iota(rows, rows, 1) < iota(rows, rows, 0))
    return jnp.sum(dot(before, onehot(hits)) * hits.astype(F32), axis=1, keepdims=True).astype(jnp.int32)


def start_kernel(w_ref, wo_ref, qsel_ref, osel_ref, send_ref):
    peers, _, cols = send_ref.shape
    weights = sum(dot(qsel_ref[c], w_ref[:, c, :]) for c in range(3))
    for half in range(2):
        weights = weights + dot(osel_ref[half], wo_ref[:, half * cols : half * cols + cols])
    send_ref[...] = jnp.broadcast_to(weights.astype(BF)[None], send_ref.shape)


def start_send(w_rows, w_o, peers, shard, wo_rows):
    cols = w_rows.shape[2]
    qsel, osel = np.zeros((3, 48, shard), np.float32), np.zeros((2, 48, wo_rows), np.float32)
    for c in range(4):
        for i in range(shard):
            place = 8 * c + i if i < 8 else 32 + 4 * c + i - 8
            if c < 3:
                qsel[c, place, i] = 1
            else:
                osel[i % 2, place, i // 2] = 1
    return staged_call(
        start_kernel,
        in_specs=[WHOLE] * 4,
        out_specs=WHOLE,
        out_shape=jax.ShapeDtypeStruct((peers, 48, cols), BF),
        **vmem(34, 200_000_000, 3_500_000),
    )(w_rows, w_o, jnp.asarray(qsel, BF), jnp.asarray(osel, BF))


def prepare_kernel(
    first_ref, down_ref, along_ref, so_down_ref, offset_ref, seg_down_ref, seg_along_ref, x_ref, xt_ref, so_ref, s_ref, bias_ref
):
    first = first_ref[...]
    width, lanes = first.shape[1], x_ref.shape[2]
    for c in range(5):
        x_ref[c] = dot(first, onehot(iota(width, lanes, 1) == down_ref[:, c : c + 1])).astype(BF)
        sel = onehot(iota(lanes, width, 0) == along_ref[c : c + 1, :])
        xt_ref[c] = dot_t(sel, first).astype(BF)
        if c == 0:
            s_ref[0] = sel
            s_ref[1] = sel
        elif c == 1:
            s_ref[0] = s_ref[0] + sel
        elif c == 2:
            s_ref[2] = sel
        else:
            s_ref[2] = s_ref[2] + sel
    send(x_ref)
    send(xt_ref)
    send(s_ref)
    for c in range(4):
        so_ref[c] = onehot(iota(so_ref.shape[1], lanes, 1) == so_down_ref[:, c : c + 1])
    send(so_ref)
    heads, seq, _ = bias_ref.shape
    same = seg_down_ref[...] == seg_along_ref[...]
    for h in range(heads):
        wide = jnp.broadcast_to(offset_ref[h : h + 1, :], (seq, 2 * seq))
        wide = pltpu.roll(wide, seq + 1, 1, stride=1, stride_axis=0)
        bias_ref[h] = jnp.where(same, wide[:, :seq], MASKED)


def places(n_dp, shard, cols, wo_rows):
    d = np.arange(n_dp * shard)
    i, p = d % shard, d // shard
    down = np.full((n_dp * shard, 8), -1, np.int32)
    for c, (start, big) in enumerate([(0, False), (8, False), (-8, True), (-4, True), (0, True)]):
        down[:, c] = np.where((i >= 8) == big, p * 16 + i + start, -1)
    d = np.arange(cols)
    i, p = d % wo_rows, d // wo_rows
    so_down = np.full((cols, 8), -1, np.int32)
    for c in range(4):
        half, late = c % 2, c // 2 == 1
        place = 12 + 2 * (i - 4) + half if late else 8 + 2 * i + half
        so_down[:, c] = np.where((i >= 4) == late, p * 16 + place, -1)
    return down, so_down


def prepare(first_all, offset_bias, segments, down, so_down, n_dp):
    seq, width = first_all.shape
    cols, lanes, heads = so_down.shape[0], n_dp * 16, 6
    shape = jax.ShapeDtypeStruct
    return staged_call(
        prepare_kernel,
        in_specs=[WHOLE] * 7,
        out_specs=[WHOLE] * 5,
        out_shape=[
            shape((5, seq, lanes), BF),
            shape((5, lanes, seq), BF),
            shape((4, cols, lanes), BF),
            shape((3, lanes, width), BF),
            shape((heads, seq, seq), F32),
        ],
        **vmem(34, 4_000_000_000, 16_000_000),
    )(
        first_all,
        jnp.asarray(down),
        jnp.asarray(np.ascontiguousarray(down.T)),
        jnp.asarray(so_down),
        offset_bias,
        segments.reshape(seq, 1),
        segments,
    )


def dispatch_kernel(ids_ref, og_ref, tokens_ref, keep_ref, got_ref, gain_ref, send_ref, mid_ref, second_ref):
    mid = tokens_ref[...].astype(F32) + (keep_ref[...] + got_ref[...].astype(F32))
    scale = lax.rsqrt(jnp.mean(mid * mid, axis=-1, keepdims=True) + EPSILON)
    second = mid * scale * gain_ref[...].reshape(1, mid.shape[1])
    mid_ref[...] = mid
    second_ref[...] = second
    send(mid_ref)
    send(second_ref)
    ids = ids_ref[...]
    rows, cols = ids.shape[1], send_ref.shape[1]
    base = ids * 8 + ranks_along(ids, rows // 2) * 2
    row = iota(send_ref.shape[0], rows, 0)
    total = jnp.zeros(send_ref.shape, F32)
    for start, values in ((0, second.astype(BF)), (4, og_ref[...])):
        for half in range(2):
            at = slice(half * cols, half * cols + cols)
            total = total + dot(onehot(row == base + (start + half)), values[:, at])
    send_ref[...] = total.astype(BF)


def dispatch(ids_row, out_grad, tokens, keep, got, gain):
    rows, width = tokens.shape
    shape = jax.ShapeDtypeStruct
    return staged_call(
        dispatch_kernel,
        in_specs=[WHOLE] * 3 + [HERE, HERE, WHOLE],
        out_specs=[WHOLE] * 3,
        out_shape=[shape((rows * 4, width // 2), BF), shape((rows, width), F32), shape((rows, width), F32)],
        **vmem(16, 200_000_000, 2_000_000),
    )(ids_row, out_grad, tokens, keep, got, gain)


def between_kernel(
    ids_ref, ctx_ref, so_along_ref, second_ref, router_ref, xot_ref, selt_ref, gate_ref
):
    ctx = ctx_ref[...]
    lanes = xot_ref.shape[1]
    for c in range(4):
        sel = onehot(iota(lanes, ctx.shape[1], 0) == so_along_ref[c : c + 1, :])
        xot_ref[c] = dot_t(sel, ctx).astype(BF)
    send(xot_ref)
    ids = ids_ref[...]
    rows = ids.shape[0]
    experts = router_ref.shape[0]
    base = ids * 16 + ranks_down(ids, experts) * 3
    lane = iota(rows, selt_ref.shape[1], 1)
    for j in range(3):
        selt_ref[rows * j : rows * j + rows, :] = onehot((lane == base + j) | (lane == base + (8 + j)))
    send(selt_ref)
    s_high, s_low = split(second_ref[...])
    r_high, r_low = split(router_ref[...])
    logits = dot_t(s_high, r_high) + (dot_t(s_low, r_high) + dot_t(s_high, r_low))
    shifted = jnp.exp(logits - jnp.max(logits, axis=-1, keepdims=True))
    hit = iota(rows, experts, 1) == ids
    gate_ref[...] = jnp.sum(jnp.where(hit, shifted, 0.0), axis=-1, keepdims=True) / jnp.sum(
        shifted, axis=-1, keepdims=True
    )


def between(ids, ctx, so_along, second, router, n_dp):
    rows = ids.shape[0]
    seq, cols = ctx.shape
    shape = jax.ShapeDtypeStruct
    return staged_call(
        between_kernel,
        in_specs=[WHOLE] * 5,
        out_specs=[WHOLE] * 3,
        out_shape=[
            shape((4, n_dp * 16, seq), BF),
            shape((3 * rows, rows * 8), BF),
            shape((rows, 1), F32),
        ],
        **vmem(20, 2_000_000_000, 8_000_000),
    )(ids, ctx, so_along, second, router)


def expert_kernel(
    me_ref, t_ref, own_ref, other_ref, router_ref, w1_ref, w2_ref, send_ref, arrived_ref, hidden_ref, pre_ref, ge_ref, *stages
):
    own, other = own_ref[...], other_ref[...]
    first = t_ref[0] == 0
    got = jnp.concatenate([jnp.where(first, own, other), jnp.where(first, other, own)], 0)
    count, cols = ge_ref.shape[0], got.shape[1]
    half = count // 2
    r = iota(count, 1, 0)
    pair = r & (half - 1)
    base = (pair & 1) * own.shape[0] + (pair >> 1) * 8 + (r >= half).astype(jnp.int32) * 2
    lane = iota(count, got.shape[0], 1)
    g = []
    for side in range(2):
        arrived_ref[:, cols * side : cols * side + cols] = dot(onehot(lane == base + side), got).astype(BF)
        g.append(dot(onehot(lane == base + (4 + side)), got))
    g = jnp.concatenate(g, 1)
    arrived = arrived_ref[...]
    r_high, r_low = split(router_ref[...])
    logits = dot_t(arrived, r_high) + dot_t(arrived, r_low)
    shifted = jnp.exp(logits - jnp.max(logits, axis=-1, keepdims=True))
    probs = shifted / jnp.sum(shifted, axis=-1, keepdims=True)
    mine = (iota(count, probs.shape[1], 1) == me_ref[0]).astype(F32)
    gate = jnp.sum(probs * mine, axis=-1, keepdims=True)
    ge = (gate * g).astype(BF)
    ge_ref[...] = ge
    width, hidden_cols = w1_ref.shape
    step = 256
    out = jnp.zeros((count, width), F32)
    back = jnp.zeros((count, width), F32)
    for f in range(0, hidden_cols, step):
        at = slice(f, f + step)
        w1, w2 = w1_ref[:, at], w2_ref[at, :]
        u = dot(arrived, w1)
        cdf = 0.5 + 0.5 * lax.erf(u * 0.7071067811865476)
        hidden = (u * cdf).astype(BF)
        slope = cdf + u * (jnp.exp(-0.5 * u * u) * 0.3989422804014327)
        grad = (dot_t(ge, w2) * slope).astype(BF)
        hidden_ref[:, at] = hidden
        pre_ref[:, at] = grad
        out = out + dot(hidden, w2)
        back = back + dot_t(grad, w1)
    send(hidden_ref)
    send(pre_ref)
    send(ge_ref)
    send(arrived_ref)
    grad_gate = jnp.sum(g * out, axis=-1, keepdims=True)
    grad_logits = grad_gate * gate * (mine - probs)
    l_high, l_low = split(grad_logits)
    back = back + (dot(l_high, r_high) + (dot(l_low, r_high) + dot(l_high, r_low)))
    t_high, t_low = split(grad_logits.T)
    router_part = dot(t_high, arrived) + dot(t_low, arrived)
    for side, stage in enumerate(stages):
        stage[...] = jnp.zeros(stage.shape, F32)
        values = out if side < 2 else back
        for j in range(3):
            at = slice(256 * j + 128 * (side % 2), 256 * j + 128 * (side % 2) + 128)
            for s in range(2):
                stage[pl.ds(s * 3 + j, half, stride=8), :] = values[s * half : s * half + half, at]
        if side < 3:
            for t in range(2):
                at = cols * t + 128 * side
                stage[pl.ds(6 + 8 * t, half // 2, stride=16), :] = router_part[:, at : at + 128]
        send_ref[:, 128 * side : 128 * side + 128] = stage[...].astype(BF)


def expert(me, t, own, other, router, w1, w2):
    count, width = own.shape[0] // 2, own.shape[1] * 2
    hidden = w1.shape[1]
    shape = jax.ShapeDtypeStruct
    return staged_call(
        expert_kernel,
        in_specs=[SCALAR] * 2 + [HERE] * 2 + [WHOLE] * 3,
        out_specs=[WHOLE] * 5,
        out_shape=[
            shape((count * 4, 512), BF),
            shape((count, width), BF),
            shape((count, hidden), BF),
            shape((count, hidden), BF),
            shape((count, width), BF),
        ],
        scratch_shapes=[pltpu.VMEM((count * 4, 128), F32)] * 4,
        **vmem(34, 3_000_000_000, 9_000_000),
    )(me, t, own, other, router, w1, w2)


def home_kernel(
    got_ref, selt_ref, mid_ref, gate_ref, gain_ref, og_ref, act_ref, gmid_ref, gattn_ref, router_ref, two_ref
):
    got = got_ref[...]
    rows = mid_ref.shape[0]
    sums = dot(selt_ref[...], got)
    out = jnp.concatenate([sums[rows * j : rows * j + rows, :256] for j in range(3)], 1)
    grad_second = jnp.concatenate([sums[rows * j : rows * j + rows, 256:] for j in range(3)], 1)
    lane = iota(16, got.shape[0], 1) & 7
    piece = dot(onehot(lane == iota(16, got.shape[0], 0) + 6), got)
    router_ref[...] = piece[0:1, : router_ref.shape[1]]
    mid = mid_ref[...]
    gain = gain_ref[...].reshape(1, mid.shape[1])
    send(router_ref)
    act_ref[...] = (mid + gate_ref[...] * out).astype(BF)
    send(act_ref)
    scale = lax.rsqrt(jnp.mean(mid * mid, axis=-1, keepdims=True) + EPSILON)
    u = grad_second * gain
    two_ref[...] = jnp.sum(grad_second * mid * scale, axis=0, keepdims=True)
    spread = jnp.mean(u * mid, axis=-1, keepdims=True)
    gmid = og_ref[...].astype(F32) + (scale * u - scale * scale * scale * mid * spread)
    gmid_ref[...] = gmid
    gattn_ref[...] = gmid.astype(BF)


def home(got, selt, mid, gate, gain, out_grad):
    rows, width = mid.shape
    shape = jax.ShapeDtypeStruct
    return staged_call(
        home_kernel,
        in_specs=[HERE] + [WHOLE] * 5,
        out_specs=[WHOLE] * 2 + [HERE] * 3,
        out_shape=[
            shape((rows, width), BF),
            shape((rows, width), F32),
            shape((rows, width), BF),
            shape((1, width // 2), F32),
            shape((1, width), F32),
        ],
        **vmem(16, 500_000_000, 6_000_000),
    )(got, selt, mid, gate, gain, out_grad)


def small_sums_kernel(got_ref, packed_ref):
    tiny = got_ref[:, 48:56, :].astype(F32)
    peers = tiny.shape[0]
    packed_ref[:peers, :] = tiny[:, 0, :]
    packed_ref[peers:, :] = jnp.sum(tiny, axis=0)


def weight_sums_kernel(got_ref, qkv_ref, wo_ref):
    total = jnp.sum(got_ref[:, :48, :].astype(F32), axis=0)
    cols = total.shape[1]
    for c in range(3):
        qkv_ref[0:8, c, :] = total[8 * c : 8 * c + 8]
        qkv_ref[8:12, c, :] = total[32 + 4 * c : 36 + 4 * c]
    for j in range(12):
        row = 24 + j if j < 8 else 36 + j
        wo_ref[j // 2 : j // 2 + 1, (j % 2) * cols : (j % 2) * cols + cols] = total[row : row + 1]


def small_outputs_kernel(t_ref, own_ref, other_ref, router_ref, one_ref, two_ref, table_ref):
    own, other = own_ref[...], other_ref[...]
    first = t_ref[0] == 0
    low, high = jnp.where(first, own, other), jnp.where(first, other, own)
    peers, cols = router_ref.shape[0], own.shape[1]
    router_ref[:, :cols] = low[:peers]
    router_ref[:, cols:] = high[:peers]
    total = own[peers:] + other[peers:]
    for ref, row in ((one_ref, 1), (two_ref, 3)):
        ref[:cols] = total[row]
        ref[cols:] = total[row + 1]
    heads, buckets = table_ref.shape[0] // 2, table_ref.shape[1]
    for h in range(2 * heads):
        row = (low if h < heads else high)[peers + 5 : peers + 6]
        at = 64 * (h % heads)
        table_ref[h : h + 1, :] = row[:, at : at + buckets]


def small_sums(got):
    return staged_call(
        small_sums_kernel,
        in_specs=[HERE],
        out_specs=HERE,
        out_shape=jax.ShapeDtypeStruct((got.shape[0] + 8, got.shape[2]), F32),
        **vmem(8, 100_000, 400_000),
    )(got)


def weight_sums(got, shard, wo_rows):
    shape = jax.ShapeDtypeStruct
    return staged_call(
        weight_sums_kernel,
        in_specs=[HERE],
        out_specs=[WHOLE] * 2,
        out_shape=[shape((shard, 3, got.shape[2]), F32), shape((wo_rows, 2 * got.shape[2]), F32)],
        **vmem(8, 1_000_000, 3_000_000),
    )(got)


def small_outputs(t, own, other, peers, heads, buckets):
    width = 2 * own.shape[1]
    shape = jax.ShapeDtypeStruct
    return staged_call(
        small_outputs_kernel,
        in_specs=[SCALAR, HERE, HERE],
        out_specs=[WHOLE] * 4,
        out_shape=[shape((peers, width), F32), shape((width,), F32), shape((width,), F32), shape((2 * heads, buckets), F32)],
        **vmem(8, 100_000, 700_000),
    )(t, own, other)


def first_back_kernel(t_ref, g3_ref, got_ref, along_ref, keep_ref, give_ref):
    one, two, three = groups(got_ref)
    g = [g3_ref[c] for c in range(3)]
    lanes, width = one.shape[0], along_ref.shape[1]
    pieces = [dot_t(g[0], one), dot_t(g[1], one), dot_t(g[0], three), dot_t(g[1], three), dot_t(g[2], three)]
    pieces = [p.astype(BF) for p in pieces]
    total = jnp.zeros((g[0].shape[0], width), F32)
    for c in range(5):
        sel = onehot(iota(lanes, width, 0) == along_ref[c : c + 1, :])
        total = total + dot(pieces[c], sel)
        if c == 0:
            total = total + dot(dot_t(g[2], two).astype(BF), sel)
    rows = total.shape[0] // 2
    low, high = total[:rows], total[rows:]
    first = t_ref[0] == 0
    keep_ref[...] = jnp.where(first, low, high)
    give_ref[...] = jnp.where(first, high, low).astype(BF)


def first_back(t, g3, got, along):
    seq, width = g3.shape[1], along.shape[1]
    shape = jax.ShapeDtypeStruct
    return staged_call(
        first_back_kernel,
        in_specs=[SCALAR] + [WHOLE] * 3,
        out_specs=[WHOLE] * 2,
        out_shape=[shape((seq // 2, width), F32), shape((seq // 2, width), BF)],
        **vmem(34, 4_000_000_000, 5_000_000),
    )(t, g3, got, along)


def per_device(
    tokens, gain_attn, rel_table, w_qkv, w_o, gain_moe, router, w_in, w_out, segments, offset_buckets, expert_ids, out_grad
):
    rows, width = tokens.shape
    shard, _, cols = w_qkv.shape
    wo_rows = w_o.shape[0]
    buckets, heads_all = rel_table.shape
    heads = cols // (width // heads_all)
    seq = segments.shape[1]
    n_dp = lax.axis_size("dp")
    n_t = lax.axis_size("tensor")
    t = lax.axis_index("tensor")
    me = lax.axis_index("dp")
    ids_row = expert_ids.reshape(1, rows)

    send_one = start_send(w_qkv, w_o, n_dp, shard, wo_rows)
    got_one = lax.all_to_all(send_one, "dp", 0, 0)

    xf = tokens.astype(F32)
    scale_one = lax.rsqrt(jnp.mean(xf * xf, axis=-1, keepdims=True) + EPSILON)
    first_rows = (xf * scale_one * gain_attn).astype(BF)
    first_all = lax.all_gather(first_rows, "tensor", axis=0, tiled=True)
    table_local = lax.dynamic_slice_in_dim(rel_table, t * heads, heads, 1)
    bucket_row = jnp.pad(offset_buckets, (0, 1), constant_values=-1)[None]
    bucket_hits = (bucket_row[0][:, None] == jnp.arange(buckets, dtype=jnp.int32)[None, :]).astype(F32)
    offset_bias = jnp.einsum("bh,rb->hr", jnp.pad(table_local, ((0, 0), (0, 8 - heads))), bucket_hits, precision=PRECISE)
    down, so_down = places(n_dp, shard, cols, wo_rows)
    along = jnp.asarray(np.ascontiguousarray(down.T))
    x, xt, so, back, bias = prepare(first_all, offset_bias, segments, down, so_down, n_dp)

    keep, give, context, qkv, probs, wo_full = attend(t.reshape(1), got_one, x, so, bias)
    gain_row = gain_moe
    send_two, mid, second = dispatch(ids_row, out_grad, tokens, keep, swap(give), gain_row)

    got_two = lax.all_to_all(send_two.reshape(n_dp, 8, cols), "dp", 0, 0)
    so_along = jnp.asarray(np.ascontiguousarray(so_down.T))
    xot, selt, gate_home = between(expert_ids, context, so_along, second, router.T, n_dp)
    own, other = [y.reshape(n_dp * 8, cols) for y in (got_two, swap(got_two))]

    t1 = t.reshape(1)
    send_three, arrived, hidden, grad_pre, grad_expert = expert(me.reshape(1), t1, own, other, router.T, w_in[0], w_out[0])

    got_three = lax.all_to_all(send_three.reshape(n_dp * n_t, 8, 512), ALL, 0, 0).reshape(n_dp * n_t * 8, 512)
    grad_w_out = dot(hidden, grad_expert, ((0,), (0,)))
    grad_w_in = dot(arrived, grad_pre, ((0,), (0,)))
    activations, grad_mid, grad_own, router_piece, gain_two = home(got_three, selt, mid, gate_home, gain_row, out_grad)

    send_four, grad3 = attend_back(
        t1, grad_own, swap(grad_own), wo_full, qkv, probs, bucket_row, gain_attn, router_piece, gain_two, got_one, xt, xot, back
    )

    got_four = lax.all_to_all(send_four, "dp", 0, 0)
    keep_first, give_first = first_back(t1, grad3, got_one, along)
    grad_first_own = keep_first + swap(give_first).astype(F32)
    u1 = grad_first_own * gain_attn
    spread_one = jnp.mean(u1 * xf, axis=-1, keepdims=True)
    input_grad = (grad_mid + (scale_one * u1 - scale_one * scale_one * scale_one * xf * spread_one)).astype(BF)

    got_four, input_grad, grad_w_in, grad_w_out = lax.optimization_barrier(
        (got_four, input_grad, grad_w_in, grad_w_out)
    )
    packed = small_sums(got_four)
    other = swap(packed)
    grad_qkv_shard, grad_o_shard = weight_sums(got_four, shard, wo_rows)
    grad_router, gain_one_sum, gain_two_sum, table_sum = small_outputs(t1, packed, other, n_dp, heads, buckets)
    grad_router, table_sum = grad_router.T, table_sum.T
    return (
        activations,
        input_grad,
        gain_one_sum,
        table_sum,
        grad_qkv_shard,
        grad_o_shard,
        gain_two_sum,
        grad_router,
        grad_w_in[None],
        grad_w_out[None],
    )


def solution(mesh):
    in_specs = (
        P(("dp", "tensor"), None),
        P(),
        P(),
        P("dp", None, "tensor"),
        P(("tensor", "dp"), None),
        P(),
        P(),
        P("dp", None, "tensor"),
        P("dp", "tensor", None),
        P("dp", None),
        P(),
        P(("dp", "tensor"), None),
        P(("dp", "tensor"), None),
    )
    out_specs = (
        P(("dp", "tensor"), None),
        P(("dp", "tensor"), None),
        P(),
        P(),
        P("dp", None, "tensor"),
        P(("tensor", "dp"), None),
        P(),
        P(),
        P("dp", None, "tensor"),
        P("dp", "tensor", None),
    )
    return jax.shard_map(per_device, mesh=mesh, in_specs=in_specs, out_specs=out_specs, check_vma=False)
```

```python
import jax
import jax.numpy as jnp
import numpy as np
from jax import lax
from jax.experimental import pallas as pl
from jax.experimental.pallas import tpu as pltpu
from jax.sharding import PartitionSpec as P

PRECISE = lax.Precision.HIGHEST
EPSILON = 1e-06
MASKED = -1000000000.0
BF = jnp.bfloat16
F32 = jnp.float32
ALL = ("dp", "tensor")


def swap(rows):
    return lax.ppermute(rows, "tensor", [(0, 1), (1, 0)])


def dot(left, right, dims=((1,), (0,)), precision=None):
    return lax.dot_general(left, right, (dims, ((), ())), precision=precision, preferred_element_type=F32)


def dot_t(left, right):
    return dot(left, right, ((1,), (1,)))


def vmem(limit_mb, flops, moved):
    return dict(
        compiler_params=pltpu.CompilerParams(vmem_limit_bytes=limit_mb * 1024 * 1024),
        cost_estimate=pl.CostEstimate(flops=flops, bytes_accessed=moved, transcendentals=0),
    )


WHOLE = "whole"
HERE = "here"
SCALAR = pl.BlockSpec(memory_space=pltpu.SMEM)


class Arriving:
    def __init__(self, source, buffer, sem):
        self.buffer, self.shape = buffer, buffer.shape
        self.move = pltpu.make_async_copy(source, buffer, sem)
        self.move.start()

    def wait(self):
        if self.move is not None:
            self.move.wait()
            self.move = None

    def __getitem__(self, index):
        self.wait()
        return self.buffer[index]


class Leaving:
    def __init__(self, buffer, out, sem):
        self.buffer, self.out, self.sem = buffer, out, sem
        self.shape, self.move, self.sent = buffer.shape, None, False

    def __getitem__(self, index):
        return self.buffer[index]

    def __setitem__(self, index, value):
        self.buffer[index] = value

    def send(self):
        if not self.sent:
            self.move = pltpu.make_async_copy(self.buffer, self.out, self.sem)
            self.move.start()
            self.sent = True


def staged_call(body, in_specs, out_specs, out_shape, scratch_shapes=(), **params):
    several = isinstance(out_shape, list)
    results, kinds = (out_shape, out_specs) if several else ([out_shape], [out_specs])
    moved = [i for i, kind in enumerate(in_specs) if kind is WHOLE]
    left = [i for i, kind in enumerate(kinds) if kind is WHOLE]

    def kernel(*refs):
        refs = list(refs)
        ins, outs = refs[: len(in_specs)], refs[len(in_specs) : len(in_specs) + len(results)]
        rest = refs[len(in_specs) + len(results) :]
        in_buffers, rest = rest[: len(moved)], rest[len(moved) :]
        out_buffers, rest = rest[: len(left)], rest[len(left) :]
        in_sems, out_sems, extra = rest[0], rest[1], rest[2:]
        for n, (i, buffer) in enumerate(zip(moved, in_buffers)):
            ins[i] = Arriving(ins[i], buffer, in_sems.at[n])
        for n, (i, buffer) in enumerate(zip(left, out_buffers)):
            outs[i] = Leaving(buffer, outs[i], out_sems.at[n])
        body(*ins, *outs, *extra)
        for i in moved:
            ins[i].wait()
        for i in left:
            outs[i].send()
        for i in left:
            if outs[i].move is not None:
                outs[i].move.wait()

    def call(*args):
        space = {WHOLE: pltpu.HBM, HERE: pltpu.VMEM}
        place = lambda kind: pl.BlockSpec(memory_space=space[kind]) if kind in (WHOLE, HERE) else kind
        placed = [space[kind](r.shape, r.dtype) for kind, r in zip(kinds, results, strict=True)]
        args = [
            pltpu.with_memory_space_constraint(a, space[kind]) if kind in (WHOLE, HERE) else a
            for kind, a in zip(in_specs, args, strict=True)
        ]
        return pl.pallas_call(
            kernel,
            in_specs=[place(kind) for kind in in_specs],
            out_specs=[place(kind) for kind in kinds] if several else place(kinds[0]),
            out_shape=placed if several else placed[0],
            scratch_shapes=[pltpu.VMEM(args[i].shape, args[i].dtype) for i in moved]
            + [pltpu.VMEM(results[i].shape, results[i].dtype) for i in left]
            + [pltpu.SemaphoreType.DMA((max(1, len(moved)),)), pltpu.SemaphoreType.DMA((max(1, len(left)),))]
            + list(scratch_shapes),
            **params,
        )(*args)

    return call


def send(*refs):
    for ref in refs:
        if isinstance(ref, Leaving):
            ref.send()


def groups(ref):
    return [ref[:, 16 * g : 16 * g + 16, :].reshape(ref.shape[0] * 16, ref.shape[2]) for g in range(3)]


def attend_kernel(t_ref, got_ref, x_ref, so_ref, bias_ref, keep_ref, give_ref, ctx_ref, qkv_ref, probs_ref, wo_ref):
    one, two, three = groups(got_ref)
    q = (dot(x_ref[0], one) + dot(x_ref[2], three)).astype(BF)
    k = (dot(x_ref[1], one) + dot(x_ref[3], three)).astype(BF)
    v = (dot(x_ref[0], two) + dot(x_ref[4], three)).astype(BF)
    qkv_ref[0], qkv_ref[1], qkv_ref[2] = q, k, v
    send(qkv_ref)
    cols = q.shape[1]
    so_ref.wait()
    bias_ref.wait()
    lane = lax.broadcasted_iota(jnp.int32, (q.shape[0], 128), 1)
    zero = jnp.zeros((q.shape[0], 128), BF)
    for pair in range(cols // 128):
        at = slice(128 * pair, 128 * pair + 128)
        q2, k2, v2 = q[:, at], k[:, at], v[:, at]
        outs = []
        if pair < 2:
            wo_ref[:, pair * cols : pair * cols + cols] = (
                dot(so_ref[pair], two) + dot(so_ref[2 + pair], three)
            ).astype(BF)
        for which in range(2):
            mine = (lane < 64) if which == 0 else (lane >= 64)
            scores = dot_t(jnp.where(mine, q2, zero), k2) + bias_ref[2 * pair + which]
            top = jnp.max(scores, axis=-1, keepdims=True)
            shifted = jnp.exp(scores - top)
            probs = (shifted * (1.0 / jnp.sum(shifted, axis=-1, keepdims=True))).astype(BF)
            probs_ref[2 * pair + which] = probs
            outs.append(dot(probs, v2))
        ctx_ref[:, at] = jnp.where(lane < 64, outs[0], outs[1]).astype(BF)
    send(probs_ref, wo_ref)
    send(ctx_ref)
    part = dot(ctx_ref[...], wo_ref[...])
    rows = part.shape[0] // 2
    low, high = part[:rows], part[rows:]
    first = t_ref[0] == 0
    keep_ref[...] = jnp.where(first, low, high)
    give_ref[...] = jnp.where(first, high, low).astype(BF)


def attend(t, got, x, so, bias):
    cols, seq = got.shape[2], x.shape[1]
    heads = bias.shape[0]
    shape = jax.ShapeDtypeStruct
    return staged_call(
        attend_kernel,
        in_specs=[SCALAR, HERE] + [WHOLE] * 3,
        out_specs=[HERE] * 2 + [WHOLE] * 4,
        out_shape=[
            shape((seq // 2, 2 * cols), F32),
            shape((seq // 2, 2 * cols), BF),
            shape((seq, cols), BF),
            shape((3, seq, cols), BF),
            shape((heads, seq, seq), BF),
            shape((cols, 2 * cols), BF),
        ],
        **vmem(34, 4_000_000_000, 14_000_000),
    )(t, got, x, so, bias)


def attend_back_kernel(
    t_ref, own_ref, other_ref, wo_ref, qkv_ref, probs_ref, hits_ref, gain_ref, router_ref, two_ref, xt_ref, xot_ref, got_ref, s_ref,
    send_ref, g3_ref,
):
    own, other = own_ref[...], other_ref[...]
    first = t_ref[0] == 0
    ga = jnp.concatenate([jnp.where(first, own, other), jnp.where(first, other, own)], 0)
    q, k, v = qkv_ref[0], qkv_ref[1], qkv_ref[2]
    seq, cols = q.shape
    gctx = dot_t(ga, wo_ref[...]).astype(BF)
    lane = lax.broadcasted_iota(jnp.int32, (seq, 128), 1)
    low = lane < 64
    zero = jnp.zeros((seq, 128), BF)
    row8 = lax.broadcasted_iota(jnp.int32, (8, 2 * seq), 0)
    along = [lax.broadcasted_iota(jnp.int32, (seq, seq), axis) for axis in range(2)]
    flip = (along[0] + along[1] == seq - 1).astype(F32).astype(BF)
    diagonals = jnp.zeros((8, 2 * seq), F32)
    for pair in range(cols // 128):
        at = slice(128 * pair, 128 * pair + 128)
        q2, k2, v2, c2 = q[:, at], k[:, at], v[:, at], gctx[:, at]
        parts = []
        for which in range(2):
            mine = low if which == 0 else jnp.logical_not(low)
            probs = probs_ref[2 * pair + which]
            probs_f = probs.astype(F32)
            grad_probs = dot_t(jnp.where(mine, c2, zero), v2)
            inner = jnp.sum(probs_f * grad_probs, axis=-1, keepdims=True)
            ds = (probs_f * (grad_probs - inner)).astype(BF)
            parts.append((dot(ds, k2), dot(ds.T, q2), dot(probs.T, c2)))
            wide = jnp.concatenate([dot(flip, ds), jnp.zeros((seq, seq), F32)], 1)
            rolled = pltpu.roll(wide, 0, 1, stride=1, stride_axis=0)
            sums = jnp.sum(rolled, axis=0, keepdims=True)
            diagonals = jnp.where(row8 == 2 * pair + which, sums, diagonals)
        for c in range(3):
            g3_ref[c, :, at] = jnp.where(low, parts[0][c], parts[1][c]).astype(BF)
    send(g3_ref)
    gq, gk, gv = g3_ref[0], g3_ref[1], g3_ref[2]
    ga0, ga1 = ga[:, :cols], ga[:, cols:]
    one = dot(xt_ref[0], gq) + dot(xt_ref[1], gk)
    two = dot(xt_ref[0], gv) + dot(xot_ref[0], ga0) + dot(xot_ref[1], ga1)
    three = (
        dot(xt_ref[2], gq) + dot(xt_ref[3], gk) + dot(xt_ref[4], gv) + dot(xot_ref[2], ga0) + dot(xot_ref[3], ga1)
    )
    gain = jnp.zeros((128, gain_ref.shape[0]), F32)
    for g, (grad, weight) in enumerate(zip((one, two, three), groups(got_ref))):
        send_ref[:, 16 * g : 16 * g + 16, :] = grad.astype(BF).reshape(send_ref.shape[0], 16, cols)
        product = grad * weight.astype(F32)
        product = (product[:, :128] + product[:, 128:256] + product[:, 256:]).astype(BF)
        gain = gain + dot(product.T, s_ref[g])
    gain = jnp.sum(gain, axis=0, keepdims=True) / gain_ref[...].reshape(1, gain.shape[1])
    hits = ((iota(cols, 2 * seq, 0) & 63) == hits_ref[...]).astype(F32)
    table = dot(diagonals, hits, ((1,), (1,)), PRECISE)
    head_of = lax.broadcasted_iota(jnp.int32, table.shape, 1) // 64
    table = jnp.sum(
        jnp.where(head_of == lax.broadcasted_iota(jnp.int32, table.shape, 0), table, 0.0), axis=0, keepdims=True
    )
    gain_two = two_ref[...]
    row = lax.broadcasted_iota(jnp.int32, (8, cols), 0)
    tiny = jnp.zeros((8, cols), F32)
    for i, value in enumerate(
        (router_ref[...], gain[:, :cols], gain[:, cols:], gain_two[:, :cols], gain_two[:, cols:], table)
    ):
        tiny = jnp.where(row == i, value, tiny)
    send_ref[:, 48:56, :] = jnp.broadcast_to(tiny.astype(BF)[None], (send_ref.shape[0], 8, cols))


def attend_back(t, own, other, wo, qkv, probs, hits, gain, router, two, got, xt, xot, s):
    _, seq, cols = qkv.shape
    shape = jax.ShapeDtypeStruct
    return staged_call(
        attend_back_kernel,
        in_specs=[SCALAR, HERE, HERE] + [WHOLE] * 5 + [HERE] * 2 + [WHOLE] * 4,
        out_specs=[WHOLE] * 2,
        out_shape=[shape((got.shape[0], 56, cols), BF), shape((3, seq, cols), BF)],
        **vmem(34, 4_000_000_000, 16_000_000),
    )(t, own, other, wo, qkv, probs, hits, gain, router, two, xt, xot, got, s)


def iota(rows, columns, axis):
    return lax.broadcasted_iota(jnp.int32, (rows, columns), axis)


def split(value):
    high = value.astype(BF)
    return high, (value - high.astype(F32)).astype(BF)


def onehot(found):
    return jnp.where(found, 1.0, 0.0).astype(BF)


def ranks_along(ids, experts):
    rows = ids.shape[1]
    hits = iota(experts, rows, 0) == ids
    before = onehot(iota(rows, rows, 0) < iota(rows, rows, 1))
    return jnp.sum(dot(onehot(hits), before) * hits.astype(F32), axis=0, keepdims=True).astype(jnp.int32)


def ranks_down(ids, experts):
    rows = ids.shape[0]
    hits = iota(rows, experts, 1) == ids
    before = onehot(iota(rows, rows, 1) < iota(rows, rows, 0))
    return jnp.sum(dot(before, onehot(hits)) * hits.astype(F32), axis=1, keepdims=True).astype(jnp.int32)


def start_kernel(w_ref, wo_ref, qsel_ref, osel_ref, send_ref):
    peers, _, cols = send_ref.shape
    weights = sum(dot(qsel_ref[c], w_ref[:, c, :]) for c in range(3))
    for half in range(2):
        weights = weights + dot(osel_ref[half], wo_ref[:, half * cols : half * cols + cols])
    send_ref[...] = jnp.broadcast_to(weights.astype(BF)[None], send_ref.shape)


def start_send(w_rows, w_o, peers, shard, wo_rows):
    cols = w_rows.shape[2]
    qsel, osel = np.zeros((3, 48, shard), np.float32), np.zeros((2, 48, wo_rows), np.float32)
    for c in range(4):
        for i in range(shard):
            place = 8 * c + i if i < 8 else 32 + 4 * c + i - 8
            if c < 3:
                qsel[c, place, i] = 1
            else:
                osel[i % 2, place, i // 2] = 1
    return staged_call(
        start_kernel,
        in_specs=[WHOLE] * 4,
        out_specs=WHOLE,
        out_shape=jax.ShapeDtypeStruct((peers, 48, cols), BF),
        **vmem(34, 200_000_000, 3_500_000),
    )(w_rows, w_o, jnp.asarray(qsel, BF), jnp.asarray(osel, BF))


def prepare_kernel(
    first_ref, down_ref, along_ref, so_down_ref, offset_ref, seg_down_ref, seg_along_ref, x_ref, xt_ref, so_ref, s_ref, bias_ref
):
    first = first_ref[...]
    width, lanes = first.shape[1], x_ref.shape[2]
    for c in range(5):
        x_ref[c] = dot(first, onehot(iota(width, lanes, 1) == down_ref[:, c : c + 1])).astype(BF)
        sel = onehot(iota(lanes, width, 0) == along_ref[c : c + 1, :])
        xt_ref[c] = dot_t(sel, first).astype(BF)
        if c == 0:
            s_ref[0] = sel
            s_ref[1] = sel
        elif c == 1:
            s_ref[0] = s_ref[0] + sel
        elif c == 2:
            s_ref[2] = sel
        else:
            s_ref[2] = s_ref[2] + sel
    send(x_ref)
    send(xt_ref)
    send(s_ref)
    for c in range(4):
        so_ref[c] = onehot(iota(so_ref.shape[1], lanes, 1) == so_down_ref[:, c : c + 1])
    send(so_ref)
    heads, seq, _ = bias_ref.shape
    same = seg_down_ref[...] == seg_along_ref[...]
    for h in range(heads):
        wide = jnp.broadcast_to(offset_ref[h : h + 1, :], (seq, 2 * seq))
        wide = pltpu.roll(wide, seq + 1, 1, stride=1, stride_axis=0)
        bias_ref[h] = jnp.where(same, wide[:, :seq], MASKED)


def places(n_dp, shard, cols, wo_rows):
    d = np.arange(n_dp * shard)
    i, p = d % shard, d // shard
    down = np.full((n_dp * shard, 8), -1, np.int32)
    for c, (start, big) in enumerate([(0, False), (8, False), (-8, True), (-4, True), (0, True)]):
        down[:, c] = np.where((i >= 8) == big, p * 16 + i + start, -1)
    d = np.arange(cols)
    i, p = d % wo_rows, d // wo_rows
    so_down = np.full((cols, 8), -1, np.int32)
    for c in range(4):
        half, late = c % 2, c // 2 == 1
        place = 12 + 2 * (i - 4) + half if late else 8 + 2 * i + half
        so_down[:, c] = np.where((i >= 4) == late, p * 16 + place, -1)
    return down, so_down


def prepare(first_all, offset_bias, segments, down, so_down, n_dp):
    seq, width = first_all.shape
    cols, lanes, heads = so_down.shape[0], n_dp * 16, 6
    shape = jax.ShapeDtypeStruct
    return staged_call(
        prepare_kernel,
        in_specs=[WHOLE] * 7,
        out_specs=[WHOLE] * 5,
        out_shape=[
            shape((5, seq, lanes), BF),
            shape((5, lanes, seq), BF),
            shape((4, cols, lanes), BF),
            shape((3, lanes, width), BF),
            shape((heads, seq, seq), F32),
        ],
        **vmem(34, 4_000_000_000, 16_000_000),
    )(
        first_all,
        jnp.asarray(down),
        jnp.asarray(np.ascontiguousarray(down.T)),
        jnp.asarray(so_down),
        offset_bias,
        segments.reshape(seq, 1),
        segments,
    )


def dispatch_kernel(ids_ref, og_ref, tokens_ref, keep_ref, got_ref, gain_ref, send_ref, mid_ref, second_ref):
    mid = tokens_ref[...].astype(F32) + (keep_ref[...] + got_ref[...].astype(F32))
    scale = lax.rsqrt(jnp.mean(mid * mid, axis=-1, keepdims=True) + EPSILON)
    second = mid * scale * gain_ref[...].reshape(1, mid.shape[1])
    mid_ref[...] = mid
    second_ref[...] = second
    send(mid_ref)
    send(second_ref)
    ids = ids_ref[...]
    rows, cols = ids.shape[1], send_ref.shape[1]
    base = ids * 8 + ranks_along(ids, rows // 2) * 2
    row = iota(send_ref.shape[0], rows, 0)
    total = jnp.zeros(send_ref.shape, F32)
    for start, values in ((0, second.astype(BF)), (4, og_ref[...])):
        for half in range(2):
            at = slice(half * cols, half * cols + cols)
            total = total + dot(onehot(row == base + (start + half)), values[:, at])
    send_ref[...] = total.astype(BF)


def dispatch(ids_row, out_grad, tokens, keep, got, gain):
    rows, width = tokens.shape
    shape = jax.ShapeDtypeStruct
    return staged_call(
        dispatch_kernel,
        in_specs=[WHOLE] * 3 + [HERE, HERE, WHOLE],
        out_specs=[WHOLE] * 3,
        out_shape=[shape((rows * 4, width // 2), BF), shape((rows, width), F32), shape((rows, width), F32)],
        **vmem(16, 200_000_000, 2_000_000),
    )(ids_row, out_grad, tokens, keep, got, gain)


def between_kernel(
    ids_ref, ctx_ref, so_along_ref, second_ref, router_ref, xot_ref, selt_ref, gate_ref
):
    ctx = ctx_ref[...]
    lanes = xot_ref.shape[1]
    for c in range(4):
        sel = onehot(iota(lanes, ctx.shape[1], 0) == so_along_ref[c : c + 1, :])
        xot_ref[c] = dot_t(sel, ctx).astype(BF)
    send(xot_ref)
    ids = ids_ref[...]
    rows = ids.shape[0]
    experts = router_ref.shape[0]
    base = ids * 16 + ranks_down(ids, experts) * 3
    lane = iota(rows, selt_ref.shape[1], 1)
    for j in range(3):
        selt_ref[rows * j : rows * j + rows, :] = onehot((lane == base + j) | (lane == base + (8 + j)))
    send(selt_ref)
    s_high, s_low = split(second_ref[...])
    r_high, r_low = split(router_ref[...])
    logits = dot_t(s_high, r_high) + (dot_t(s_low, r_high) + dot_t(s_high, r_low))
    shifted = jnp.exp(logits - jnp.max(logits, axis=-1, keepdims=True))
    hit = iota(rows, experts, 1) == ids
    gate_ref[...] = jnp.sum(jnp.where(hit, shifted, 0.0), axis=-1, keepdims=True) / jnp.sum(
        shifted, axis=-1, keepdims=True
    )


def between(ids, ctx, so_along, second, router, n_dp):
    rows = ids.shape[0]
    seq, cols = ctx.shape
    shape = jax.ShapeDtypeStruct
    return staged_call(
        between_kernel,
        in_specs=[WHOLE] * 5,
        out_specs=[WHOLE] * 3,
        out_shape=[
            shape((4, n_dp * 16, seq), BF),
            shape((3 * rows, rows * 8), BF),
            shape((rows, 1), F32),
        ],
        **vmem(20, 2_000_000_000, 8_000_000),
    )(ids, ctx, so_along, second, router)


def expert_kernel(
    me_ref, t_ref, own_ref, other_ref, router_ref, w1_ref, w2_ref, send_ref, arrived_ref, hidden_ref, pre_ref, ge_ref, *stages
):
    own, other = own_ref[...], other_ref[...]
    first = t_ref[0] == 0
    got = jnp.concatenate([jnp.where(first, own, other), jnp.where(first, other, own)], 0)
    count, cols = ge_ref.shape[0], got.shape[1]
    half = count // 2
    r = iota(count, 1, 0)
    pair = r & (half - 1)
    base = (pair & 1) * own.shape[0] + (pair >> 1) * 8 + (r >= half).astype(jnp.int32) * 2
    lane = iota(count, got.shape[0], 1)
    g = []
    for side in range(2):
        arrived_ref[:, cols * side : cols * side + cols] = dot(onehot(lane == base + side), got).astype(BF)
        g.append(dot(onehot(lane == base + (4 + side)), got))
    g = jnp.concatenate(g, 1)
    arrived = arrived_ref[...]
    r_high, r_low = split(router_ref[...])
    logits = dot_t(arrived, r_high) + dot_t(arrived, r_low)
    shifted = jnp.exp(logits - jnp.max(logits, axis=-1, keepdims=True))
    probs = shifted / jnp.sum(shifted, axis=-1, keepdims=True)
    mine = (iota(count, probs.shape[1], 1) == me_ref[0]).astype(F32)
    gate = jnp.sum(probs * mine, axis=-1, keepdims=True)
    ge = (gate * g).astype(BF)
    ge_ref[...] = ge
    width, hidden_cols = w1_ref.shape
    step = 256
    out = jnp.zeros((count, width), F32)
    back = jnp.zeros((count, width), F32)
    for f in range(0, hidden_cols, step):
        at = slice(f, f + step)
        w1, w2 = w1_ref[:, at], w2_ref[at, :]
        u = dot(arrived, w1)
        cdf = 0.5 + 0.5 * lax.erf(u * 0.7071067811865476)
        hidden = (u * cdf).astype(BF)
        slope = cdf + u * (jnp.exp(-0.5 * u * u) * 0.3989422804014327)
        grad = (dot_t(ge, w2) * slope).astype(BF)
        hidden_ref[:, at] = hidden
        pre_ref[:, at] = grad
        out = out + dot(hidden, w2)
        back = back + dot_t(grad, w1)
    send(hidden_ref)
    send(pre_ref)
    send(ge_ref)
    send(arrived_ref)
    grad_gate = jnp.sum(g * out, axis=-1, keepdims=True)
    grad_logits = grad_gate * gate * (mine - probs)
    l_high, l_low = split(grad_logits)
    back = back + (dot(l_high, r_high) + (dot(l_low, r_high) + dot(l_high, r_low)))
    t_high, t_low = split(grad_logits.T)
    router_part = dot(t_high, arrived) + dot(t_low, arrived)
    for side, stage in enumerate(stages):
        stage[...] = jnp.zeros(stage.shape, F32)
        values = out if side < 2 else back
        for j in range(3):
            at = slice(256 * j + 128 * (side % 2), 256 * j + 128 * (side % 2) + 128)
            for s in range(2):
                stage[pl.ds(s * 3 + j, half, stride=8), :] = values[s * half : s * half + half, at]
        if side < 3:
            for t in range(2):
                at = cols * t + 128 * side
                stage[pl.ds(6 + 8 * t, half // 2, stride=16), :] = router_part[:, at : at + 128]
        send_ref[:, 128 * side : 128 * side + 128] = stage[...].astype(BF)


def expert(me, t, own, other, router, w1, w2):
    count, width = own.shape[0] // 2, own.shape[1] * 2
    hidden = w1.shape[1]
    shape = jax.ShapeDtypeStruct
    return staged_call(
        expert_kernel,
        in_specs=[SCALAR] * 2 + [HERE] * 2 + [WHOLE] * 3,
        out_specs=[WHOLE] * 5,
        out_shape=[
            shape((count * 4, 512), BF),
            shape((count, width), BF),
            shape((count, hidden), BF),
            shape((count, hidden), BF),
            shape((count, width), BF),
        ],
        scratch_shapes=[pltpu.VMEM((count * 4, 128), F32)] * 4,
        **vmem(34, 3_000_000_000, 9_000_000),
    )(me, t, own, other, router, w1, w2)


def home_kernel(
    got_ref, selt_ref, mid_ref, gate_ref, gain_ref, og_ref, act_ref, gmid_ref, gattn_ref, router_ref, two_ref
):
    got = got_ref[...]
    rows = mid_ref.shape[0]
    sums = dot(selt_ref[...], got)
    out = jnp.concatenate([sums[rows * j : rows * j + rows, :256] for j in range(3)], 1)
    grad_second = jnp.concatenate([sums[rows * j : rows * j + rows, 256:] for j in range(3)], 1)
    lane = iota(16, got.shape[0], 1) & 7
    piece = dot(onehot(lane == iota(16, got.shape[0], 0) + 6), got)
    router_ref[...] = piece[0:1, : router_ref.shape[1]]
    mid = mid_ref[...]
    gain = gain_ref[...].reshape(1, mid.shape[1])
    send(router_ref)
    act_ref[...] = (mid + gate_ref[...] * out).astype(BF)
    send(act_ref)
    scale = lax.rsqrt(jnp.mean(mid * mid, axis=-1, keepdims=True) + EPSILON)
    u = grad_second * gain
    two_ref[...] = jnp.sum(grad_second * mid * scale, axis=0, keepdims=True)
    spread = jnp.mean(u * mid, axis=-1, keepdims=True)
    gmid = og_ref[...].astype(F32) + (scale * u - scale * scale * scale * mid * spread)
    gmid_ref[...] = gmid
    gattn_ref[...] = gmid.astype(BF)


def home(got, selt, mid, gate, gain, out_grad):
    rows, width = mid.shape
    shape = jax.ShapeDtypeStruct
    return staged_call(
        home_kernel,
        in_specs=[HERE] + [WHOLE] * 5,
        out_specs=[WHOLE] * 2 + [HERE] * 3,
        out_shape=[
            shape((rows, width), BF),
            shape((rows, width), F32),
            shape((rows, width), BF),
            shape((1, width // 2), F32),
            shape((1, width), F32),
        ],
        **vmem(16, 500_000_000, 6_000_000),
    )(got, selt, mid, gate, gain, out_grad)


def small_sums_kernel(got_ref, packed_ref):
    tiny = got_ref[:, 48:56, :].astype(F32)
    peers = tiny.shape[0]
    packed_ref[:peers, :] = tiny[:, 0, :]
    packed_ref[peers:, :] = jnp.sum(tiny, axis=0)


def weight_sums_kernel(got_ref, qkv_ref, wo_ref):
    total = jnp.sum(got_ref[:, :48, :].astype(F32), axis=0)
    cols = total.shape[1]
    for c in range(3):
        qkv_ref[0:8, c, :] = total[8 * c : 8 * c + 8]
        qkv_ref[8:12, c, :] = total[32 + 4 * c : 36 + 4 * c]
    for j in range(12):
        row = 24 + j if j < 8 else 36 + j
        wo_ref[j // 2 : j // 2 + 1, (j % 2) * cols : (j % 2) * cols + cols] = total[row : row + 1]


def small_outputs_kernel(t_ref, own_ref, other_ref, router_ref, one_ref, two_ref, table_ref):
    own, other = own_ref[...], other_ref[...]
    first = t_ref[0] == 0
    low, high = jnp.where(first, own, other), jnp.where(first, other, own)
    peers, cols = router_ref.shape[0], own.shape[1]
    router_ref[:, :cols] = low[:peers]
    router_ref[:, cols:] = high[:peers]
    total = own[peers:] + other[peers:]
    for ref, row in ((one_ref, 1), (two_ref, 3)):
        ref[:cols] = total[row]
        ref[cols:] = total[row + 1]
    heads, buckets = table_ref.shape[0] // 2, table_ref.shape[1]
    for h in range(2 * heads):
        row = (low if h < heads else high)[peers + 5 : peers + 6]
        at = 64 * (h % heads)
        table_ref[h : h + 1, :] = row[:, at : at + buckets]


def small_sums(got):
    return staged_call(
        small_sums_kernel,
        in_specs=[HERE],
        out_specs=HERE,
        out_shape=jax.ShapeDtypeStruct((got.shape[0] + 8, got.shape[2]), F32),
        **vmem(8, 100_000, 400_000),
    )(got)


def weight_sums(got, shard, wo_rows):
    shape = jax.ShapeDtypeStruct
    return staged_call(
        weight_sums_kernel,
        in_specs=[HERE],
        out_specs=[WHOLE] * 2,
        out_shape=[shape((shard, 3, got.shape[2]), F32), shape((wo_rows, 2 * got.shape[2]), F32)],
        **vmem(8, 1_000_000, 3_000_000),
    )(got)


def small_outputs(t, own, other, peers, heads, buckets):
    width = 2 * own.shape[1]
    shape = jax.ShapeDtypeStruct
    return staged_call(
        small_outputs_kernel,
        in_specs=[SCALAR, HERE, HERE],
        out_specs=[WHOLE] * 4,
        out_shape=[shape((peers, width), F32), shape((width,), F32), shape((width,), F32), shape((2 * heads, buckets), F32)],
        **vmem(8, 100_000, 700_000),
    )(t, own, other)


def first_back_kernel(t_ref, g3_ref, got_ref, along_ref, keep_ref, give_ref):
    one, two, three = groups(got_ref)
    g = [g3_ref[c] for c in range(3)]
    lanes, width = one.shape[0], along_ref.shape[1]
    pieces = [dot_t(g[0], one), dot_t(g[1], one), dot_t(g[0], three), dot_t(g[1], three), dot_t(g[2], three)]
    pieces = [p.astype(BF) for p in pieces]
    total = jnp.zeros((g[0].shape[0], width), F32)
    for c in range(5):
        sel = onehot(iota(lanes, width, 0) == along_ref[c : c + 1, :])
        total = total + dot(pieces[c], sel)
        if c == 0:
            total = total + dot(dot_t(g[2], two).astype(BF), sel)
    rows = total.shape[0] // 2
    low, high = total[:rows], total[rows:]
    first = t_ref[0] == 0
    keep_ref[...] = jnp.where(first, low, high)
    give_ref[...] = jnp.where(first, high, low).astype(BF)


def first_back(t, g3, got, along):
    seq, width = g3.shape[1], along.shape[1]
    shape = jax.ShapeDtypeStruct
    return staged_call(
        first_back_kernel,
        in_specs=[SCALAR] + [WHOLE] * 3,
        out_specs=[WHOLE] * 2,
        out_shape=[shape((seq // 2, width), F32), shape((seq // 2, width), BF)],
        **vmem(34, 4_000_000_000, 5_000_000),
    )(t, g3, got, along)


def per_device(
    tokens, gain_attn, rel_table, w_qkv, w_o, gain_moe, router, w_in, w_out, segments, offset_buckets, expert_ids, out_grad
):
    rows, width = tokens.shape
    shard, _, cols = w_qkv.shape
    wo_rows = w_o.shape[0]
    buckets, heads_all = rel_table.shape
    heads = cols // (width // heads_all)
    seq = segments.shape[1]
    n_dp = lax.axis_size("dp")
    n_t = lax.axis_size("tensor")
    t = lax.axis_index("tensor")
    me = lax.axis_index("dp")
    ids_row = expert_ids.reshape(1, rows)

    send_one = start_send(w_qkv, w_o, n_dp, shard, wo_rows)
    got_one = lax.all_to_all(send_one, "dp", 0, 0)

    xf = tokens.astype(F32)
    scale_one = lax.rsqrt(jnp.mean(xf * xf, axis=-1, keepdims=True) + EPSILON)
    first_rows = (xf * scale_one * gain_attn).astype(BF)
    first_all = lax.all_gather(first_rows, "tensor", axis=0, tiled=True)
    table_local = lax.dynamic_slice_in_dim(rel_table, t * heads, heads, 1)
    bucket_row = jnp.pad(offset_buckets, (0, 1), constant_values=-1)[None]
    bucket_hits = (bucket_row[0][:, None] == jnp.arange(buckets, dtype=jnp.int32)[None, :]).astype(F32)
    offset_bias = jnp.einsum("bh,rb->hr", jnp.pad(table_local, ((0, 0), (0, 8 - heads))), bucket_hits, precision=PRECISE)
    down, so_down = places(n_dp, shard, cols, wo_rows)
    along = jnp.asarray(np.ascontiguousarray(down.T))
    x, xt, so, back, bias = prepare(first_all, offset_bias, segments, down, so_down, n_dp)

    keep, give, context, qkv, probs, wo_full = attend(t.reshape(1), got_one, x, so, bias)
    gain_row = gain_moe
    send_two, mid, second = dispatch(ids_row, out_grad, tokens, keep, swap(give), gain_row)

    got_two = lax.all_to_all(send_two.reshape(n_dp, 8, cols), "dp", 0, 0)
    so_along = jnp.asarray(np.ascontiguousarray(so_down.T))
    xot, selt, gate_home = between(expert_ids, context, so_along, second, router.T, n_dp)
    own, other = [y.reshape(n_dp * 8, cols) for y in (got_two, swap(got_two))]

    t1 = t.reshape(1)
    send_three, arrived, hidden, grad_pre, grad_expert = expert(me.reshape(1), t1, own, other, router.T, w_in[0], w_out[0])

    got_three = lax.all_to_all(send_three.reshape(n_dp * n_t, 8, 512), ALL, 0, 0).reshape(n_dp * n_t * 8, 512)
    grad_w_out = dot(hidden, grad_expert, ((0,), (0,)))
    grad_w_in = dot(arrived, grad_pre, ((0,), (0,)))
    activations, grad_mid, grad_own, router_piece, gain_two = home(got_three, selt, mid, gate_home, gain_row, out_grad)

    send_four, grad3 = attend_back(
        t1, grad_own, swap(grad_own), wo_full, qkv, probs, bucket_row, gain_attn, router_piece, gain_two, got_one, xt, xot, back
    )

    got_four = lax.all_to_all(send_four, "dp", 0, 0)
    keep_first, give_first = first_back(t1, grad3, got_one, along)
    grad_first_own = keep_first + swap(give_first).astype(F32)
    u1 = grad_first_own * gain_attn
    spread_one = jnp.mean(u1 * xf, axis=-1, keepdims=True)
    input_grad = (grad_mid + (scale_one * u1 - scale_one * scale_one * scale_one * xf * spread_one)).astype(BF)

    got_four, input_grad, grad_w_in, grad_w_out = lax.optimization_barrier(
        (got_four, input_grad, grad_w_in, grad_w_out)
    )
    packed = small_sums(got_four)
    other = swap(packed)
    grad_qkv_shard, grad_o_shard = weight_sums(got_four, shard, wo_rows)
    grad_router, gain_one_sum, gain_two_sum, table_sum = small_outputs(t1, packed, other, n_dp, heads, buckets)
    grad_router, table_sum = grad_router.T, table_sum.T
    return (
        activations,
        input_grad,
        gain_one_sum,
        table_sum,
        grad_qkv_shard,
        grad_o_shard,
        gain_two_sum,
        grad_router,
        grad_w_in[None],
        grad_w_out[None],
    )


def solution(mesh):
    in_specs = (
        P(("dp", "tensor"), None),
        P(),
        P(),
        P("dp", None, "tensor"),
        P(("tensor", "dp"), None),
        P(),
        P(),
        P("dp", None, "tensor"),
        P("dp", "tensor", None),
        P("dp", None),
        P(),
        P(("dp", "tensor"), None),
        P(("dp", "tensor"), None),
    )
    out_specs = (
        P(("dp", "tensor"), None),
        P(("dp", "tensor"), None),
        P(),
        P(),
        P("dp", None, "tensor"),
        P(("tensor", "dp"), None),
        P(),
        P(),
        P("dp", None, "tensor"),
        P("dp", "tensor", None),
    )
    return jax.shard_map(per_device, mesh=mesh, in_specs=in_specs, out_specs=out_specs, check_vma=False)
```
